32 devices in a mesh: seq: 2 (over x), fsdp: 4 (over y, core), rep: 4 (over z).
Axes of the slice: x: 2, y: 2, z: 4, core: 2. Of those that a mesh axis runs over, the one named last changes fastest.
Arguments:
- tokens: bfloat16 [4, 2048, 2304], P('fsdp', ('seq', 'rep')), may hold values from -40 to 40
- doc_lengths: int32 [4, 4], P('fsdp'), may hold values from 1 to 2045, as said below
- cotangent: bfloat16 [4, 2048, 2304], P('fsdp', ('seq', 'rep')), may hold values from -6 to 6
- attn_gain: bfloat16 [2304], P('fsdp'), may hold values from 0.5 to 1.5
- w_query: bfloat16 [2304, 2304], P('fsdp'), may hold values from -0.125 to 0.125
- w_key: bfloat16 [2304, 2304], P('fsdp'), may hold values from -0.125 to 0.125
- w_value: bfloat16 [2304, 2304], P('fsdp'), may hold values from -0.125 to 0.125
- w_out: bfloat16 [2304, 2304], P('fsdp'), may hold values from -1 to 1
- mlp_gain: bfloat16 [2304], P('fsdp'), may hold values from 0.5 to 1.5
- w_gate: bfloat16 [2304, 5760], P('fsdp'), may hold values from -0.125 to 0.125
- w_up: bfloat16 [2304, 5760], P('fsdp'), may hold values from -0.125 to 0.125
- w_down: bfloat16 [5760, 2304], P('fsdp'), may hold values from -0.625 to 0.625
Outputs:
- output: bfloat16 [4, 2048, 2304], P('fsdp', ('seq', 'rep'))
- grad_tokens: bfloat16 [4, 2048, 2304], P('fsdp', ('seq', 'rep'))
- grad_attn_gain: float32 [2304], P('fsdp')
- grad_w_query: float32 [2304, 2304], P('fsdp')
- grad_w_key: float32 [2304, 2304], P('fsdp')
- grad_w_value: float32 [2304, 2304], P('fsdp')
- grad_w_out: float32 [2304, 2304], P('fsdp')
- grad_mlp_gain: float32 [2304], P('fsdp')
- grad_w_gate: float32 [2304, 5760], P('fsdp')
- grad_w_up: float32 [2304, 5760], P('fsdp')
- grad_w_down: float32 [5760, 2304], P('fsdp')
The draws below stay inside these ranges and needn't reach their ends.
Inputs may be any that keep to these rules, and one draw needn't show every extreme that they name: `doc_lengths`: each row holds 4 lengths that add up to 2048; they are the documents of that sequence in order.
All inputs are finite; a program needn't handle non-finite values.
Results may differ from the reference program's by a relative error of at most 0.02.
Values may be sent and summed in bfloat16 or wider, within the bound.
A program may use at most 512 MiB of HBM per device.

```python
import math
import jax
import jax.numpy as jnp
from jax import lax

D = 2304
HEADS = 36
HEAD_DIM = 64
FF = 5760
TOK_DEV = 256
WINDOW = 1024
DOCS = 4
SEQS = 4
LEN = 2048


def draw_tokens(key, part):
    key = jax.random.fold_in(key, 5)
    normal_key, row_key, column_key = jax.random.split(key, 3)
    normal_draw = jax.random.truncated_normal(normal_key, -4.0, 4.0, (SEQS, LEN, D), jnp.float32)
    row_scale = jnp.exp(jax.random.uniform(row_key, (SEQS, LEN, 1), jnp.float32, -1.15, 1.15))
    column_scale = jnp.exp(jax.random.uniform(column_key, (1, 1, D), jnp.float32, -1.15, 1.15))
    return (normal_draw * row_scale * column_scale).astype(jnp.bfloat16)


def draw_doc_lengths(key, part):
    key = jax.random.fold_in(key, 9)
    lead_key, tail_key = jax.random.split(key)
    lead_doc = jax.random.randint(lead_key, (SEQS, 1), 1, TOK_DEV, jnp.int32)
    tail_docs = jax.random.randint(tail_key, (SEQS, DOCS - 2), 1, TOK_DEV // (DOCS - 2), jnp.int32)
    middle = LEN - jnp.sum(lead_doc, 1, keepdims=True) - jnp.sum(tail_docs, 1, keepdims=True)
    return jnp.concatenate([lead_doc, middle, tail_docs], 1).astype(jnp.int32)


def block_scale(own_key, extent, shards, low, high):
    loudness = 1.0
    for dim, parts in shards:
        heights = jax.random.uniform(jax.random.fold_in(jax.random.fold_in(own_key, 6), dim), (parts,), jnp.float32, low / len(shards), high / len(shards))
        loudness = loudness * jnp.repeat(jnp.exp(heights), extent[dim] // parts).reshape((-1,) + (1,) * (len(extent) - 1 - dim))
    return loudness


def scatter_about(rng, shape, scale, limit, pieces=(), kind=jnp.bfloat16):
    drawn = jax.random.normal(rng, shape, jnp.float32) * scale
    if len(pieces) > 0:
        drawn = block_scale(rng, shape, pieces, -0.22, 0.18) * drawn
    return jnp.clip(drawn, min=-limit, max=limit).astype(kind)


def setup_inputs(seed: int = 0) -> dict:
    seeds = jax.random.split(jax.random.key(seed), 13)
    tokens = draw_tokens(jax.random.fold_in(seeds[12], 71), 0)
    doc_lengths = draw_doc_lengths(jax.random.fold_in(seeds[12], 71), 0)
    cotangent = scatter_about(seeds[2], (SEQS, LEN, D), 1.0, 6.0, ((0, 4), (1, 8)))
    attn_gain = jnp.clip(1.0 + 0.1 * jax.random.normal(seeds[3], (D,), jnp.float32), 0.5, 1.5).astype(jnp.bfloat16)
    w_query = scatter_about(seeds[4], (D, D), D ** -0.5, 0.125, ((0, 4),))
    w_key = scatter_about(seeds[5], (D, D), D ** -0.5, 0.125, ((0, 4),))
    w_value = scatter_about(seeds[6], (D, D), D ** -0.5, 0.125, ((0, 4),))
    w_out = scatter_about(seeds[7], (D, D), (D // 64) ** -0.5, 1.0, ((0, 4),))
    mlp_gain = jnp.clip(1.0 + 0.1 * jax.random.normal(seeds[8], (D,), jnp.float32), 0.5, 1.5).astype(jnp.bfloat16)
    w_gate = scatter_about(seeds[9], (D, FF), D ** -0.5, 0.125, ((0, 4),))
    w_up = scatter_about(seeds[10], (D, FF), D ** -0.5, 0.125, ((0, 4),))
    w_down = scatter_about(seeds[11], (FF, D), (FF // 64) ** -0.5, 0.625, ((0, 4),))
    return {"tokens": tokens, "doc_lengths": doc_lengths, "cotangent": cotangent, "attn_gain": attn_gain, "w_query": w_query, "w_key": w_key, "w_value": w_value, "w_out": w_out, "mlp_gain": mlp_gain, "w_gate": w_gate, "w_up": w_up, "w_down": w_down}


@jax.custom_vjp
def low(v):
    return lax.optimization_barrier(v.astype(jnp.bfloat16)).astype(jnp.float32)

@jax.custom_vjp
def low_back(v):
    return v

def low_keep(v):
    return (low(v), None)

def low_pass(kept, grad):
    return (grad,)

def back_keep(v):
    return (v, None)

def back_low(kept, grad):
    return (low(grad),)
low.defvjp(low_keep, low_pass)
low_back.defvjp(back_keep, back_low)
BETA = 1.4 / math.sqrt(40.0)
EPSILON = 1e-05
NEGATIVE = -1e+30
HIGH = lax.Precision.HIGHEST

def product(left_side, right_side):
    return jnp.dot(left_side, right_side, precision=HIGH, preferred_element_type=jnp.float32)

def doc_layout(lengths):
    doc_ends = jnp.cumsum(lengths).astype(jnp.int32)
    position = jnp.arange(LEN, dtype=jnp.int32)
    doc_ids = lax.optimization_barrier(jnp.sum((position[:, None] >= doc_ends[None, :]).astype(jnp.int32), axis=1))
    doc_starts = (doc_ends - lengths).astype(jnp.int32)
    choose = doc_ids[:, None] == jnp.arange(DOCS, dtype=jnp.int32)[None, :]
    doc_first = lax.optimization_barrier(jnp.sum(jnp.where(choose, doc_starts[None, :], 0), axis=1)).astype(jnp.int32)
    return (doc_ids, (position - doc_first).astype(jnp.int32))

def rope_tables(offset):
    half_dim = HEAD_DIM // 2
    frequency = jnp.exp(jnp.arange(half_dim, dtype=jnp.float32) * (-2.0 * math.log(10000.0) / HEAD_DIM))
    angles = offset.astype(jnp.float32)[:, None] * frequency[None, :]
    cosine = jnp.cos(angles)
    sine_table = jnp.sin(angles)
    return (jnp.concatenate([cosine, cosine], 1), jnp.concatenate([sine_table, sine_table], 1))

def rotate(heads_in, cosine, sine_table):
    half_dim = HEAD_DIM // 2
    turned = jnp.concatenate([-heads_in[..., half_dim:], heads_in[..., :half_dim]], -1)
    return heads_in * cosine[:, None, :] + turned * sine_table[:, None, :]

def attend(query_rot, key_rot, value_low, doc_ids):
    block_rows = min(512, LEN)
    key_span = WINDOW + block_rows
    keys_padded = jnp.pad(key_rot, ((WINDOW, 0), (0, 0), (0, 0)))
    values_padded = jnp.pad(value_low, ((WINDOW, 0), (0, 0), (0, 0)))
    docs_padded = jnp.concatenate([jnp.full((WINDOW,), -1, jnp.int32), doc_ids.astype(jnp.int32)])

    def score_block(block_index):
        first_row = (block_index * block_rows).astype(jnp.int32)
        query_block = lax.dynamic_slice_in_dim(query_rot, first_row, block_rows, 0)
        key_block = lax.dynamic_slice_in_dim(keys_padded, first_row, key_span, 0)
        value_block = lax.dynamic_slice_in_dim(values_padded, first_row, key_span, 0)
        query_docs = lax.dynamic_slice_in_dim(doc_ids.astype(jnp.int32), first_row, block_rows, 0)
        key_docs = lax.dynamic_slice_in_dim(docs_padded, first_row, key_span, 0)
        query_place = first_row + jnp.arange(block_rows, dtype=jnp.int32)
        key_place = first_row - WINDOW + jnp.arange(key_span, dtype=jnp.int32)
        visible = (key_docs[None, :] == query_docs[:, None]) & (key_place[None, :] <= query_place[:, None]) & (key_place[None, :] > query_place[:, None] - WINDOW)
        scores = low_back(jnp.einsum('qhd,khd->hqk', query_block, key_block, precision=HIGH) * 0.125)
        scores = jnp.where(visible[None], scores, NEGATIVE)
        row_top = lax.optimization_barrier(jnp.max(scores, -1, keepdims=True))
        exp_scores = jnp.exp(scores - row_top)
        probability = exp_scores / lax.optimization_barrier(jnp.sum(exp_scores, -1, keepdims=True))
        return jnp.einsum('hqk,khd->qhd', low(probability), value_block, precision=HIGH)
    blocks = lax.map(jax.checkpoint(score_block), jnp.arange(LEN // block_rows, dtype=jnp.int32))
    return blocks.reshape(LEN, HEADS * HEAD_DIM)

def block_forward(tokens_in, doc_ids, offset, attn_gain, w_query, w_key, w_value, w_out, mlp_gain, w_gate, w_up, w_down):
    rms_one = lax.rsqrt(lax.optimization_barrier(jnp.mean(tokens_in * tokens_in, -1, keepdims=True)) + EPSILON)
    normed_one = low(tokens_in * rms_one * attn_gain)
    query_raw = low_back(product(normed_one, w_query))
    key_raw = low_back(product(normed_one, w_key))
    value_raw = low_back(product(normed_one, w_value))
    cosine, sine_table = rope_tables(offset)
    head_shape = (LEN, HEADS, HEAD_DIM)
    query_rot = low(rotate(query_raw.reshape(head_shape), cosine, sine_table))
    key_rot = low(rotate(key_raw.reshape(head_shape), cosine, sine_table))
    value_low = low(value_raw.reshape(head_shape))
    context = low(low_back(attend(query_rot, key_rot, value_low, doc_ids)))
    hidden_res = tokens_in + BETA * low_back(product(context, w_out))
    rms_two = lax.rsqrt(lax.optimization_barrier(jnp.mean(hidden_res * hidden_res, -1, keepdims=True)) + EPSILON)
    normed_two = low(hidden_res * rms_two * mlp_gain)
    gate_proj = low_back(product(normed_two, w_gate))
    up_proj = low_back(product(normed_two, w_up))
    activation = low(jax.nn.silu(gate_proj) * up_proj)
    return hidden_res + BETA * low_back(product(activation, w_down))

def reference(tokens, doc_lengths, cotangent, attn_gain, w_query, w_key, w_value, w_out, mlp_gain, w_gate, w_up, w_down):
    params = tuple((weight.astype(jnp.float32) for weight in (attn_gain, w_query, w_key, w_value, w_out, mlp_gain, w_gate, w_up, w_down)))
    initial = tuple((jnp.zeros(weight.shape, jnp.float32) for weight in params))

    def per_sequence(totals, sequence_item):
        tokens_seq, lengths, grad_seq = sequence_item
        doc_ids, offset = doc_layout(lengths)

        def forward(tokens_in, *weight_list):
            return block_forward(tokens_in, doc_ids, offset, *weight_list)
        result, pullback = jax.vjp(forward, tokens_seq.astype(jnp.float32), *params)
        gradients = pullback(grad_seq.astype(jnp.float32))
        totals = tuple((total + grad_one for total, grad_one in zip(totals, gradients[1:])))
        return (totals, (result.astype(jnp.bfloat16), gradients[0].astype(jnp.bfloat16)))
    totals, (output, grad_tokens) = lax.scan(per_sequence, initial, (tokens, doc_lengths, cotangent))
    return (output, grad_tokens, totals[0], totals[1], totals[2], totals[3], totals[4], totals[5], totals[6], totals[7], totals[8])
```

```python
from functools import partial
import math

import jax
import jax.numpy as jnp
from jax import lax
from jax.experimental import pallas as pl
from jax.experimental.pallas import tpu as pltpu
from jax.sharding import Mesh, PartitionSpec as P

HEADS = 36
HEAD_DIM = 64
WINDOW = 1024

BETA = 1.4 / math.sqrt(40.0)
EPSILON = 1e-05
NEGATIVE = -1e30

PLANE = ("x", "y", "c")
LANES = 128
VMEM_LIMIT = 60 * 1024 * 1024
F32 = jnp.float32
BF16 = jnp.bfloat16


def dot(left, right):
    return jnp.dot(left, right, preferred_element_type=F32)


def dot_tn(left, right):
    return lax.dot_general(left, right, (((0,), (0,)), ((), ())), preferred_element_type=F32)


def dot_nt(left, right):
    return lax.dot_general(left, right, (((1,), (1,)), ((), ())), preferred_element_type=F32)


def swap(array, axis):
    return lax.ppermute(array, axis, [(0, 1), (1, 0)])


def layout(lengths, position):
    doc_ends = jnp.cumsum(lengths)
    doc_ids = jnp.sum((position[:, None] >= doc_ends[None, :]).astype(jnp.int32), axis=1)
    doc_starts = doc_ends - lengths
    choose = doc_ids[:, None] == jnp.arange(lengths.shape[0], dtype=jnp.int32)[None, :]
    doc_first = jnp.sum(jnp.where(choose, doc_starts[None, :], 0), axis=1)
    return (doc_ids, position - doc_first)


def rope_tables(offset):
    half_dim = HEAD_DIM // 2
    frequency = jnp.exp(
        jnp.arange(half_dim, dtype=F32) * (-2.0 * math.log(10000.0) / HEAD_DIM)
    )
    angles = offset.astype(F32)[:, None] * frequency[None, :]
    cosine = jnp.cos(angles)
    sine_table = jnp.sin(angles)
    return (
        jnp.concatenate([cosine, cosine] * 2, 1),
        jnp.concatenate([-sine_table, sine_table] * 2, 1),
    )


MESH_ID = pl.DeviceIdType.MESH
ANY = pl.BlockSpec(memory_space=pl.ANY)
IN_VMEM = pl.BlockSpec(memory_space=pltpu.VMEM)


def remote(src, dst, sems, index, device):
    return pltpu.make_async_remote_copy(
        src_ref=src,
        dst_ref=dst,
        send_sem=sems[0].at[index],
        recv_sem=sems[1].at[index],
        device_id=device,
        device_id_type=MESH_ID,
    )


def meet(devices):
    barrier = pltpu.get_barrier_semaphore()
    for device in devices:
        pl.semaphore_signal(barrier, inc=1, device_id=device, device_id_type=MESH_ID)
    pl.semaphore_wait(barrier, len(devices))


def gather_kernel(cores, block, out, send, recv, here):
    x, y, c = (lax.axis_index(a) for a in PLANE)
    slot = c if cores == 2 else 0
    to_x, to_y, to_c = {"x": 1 - x}, {"y": 1 - y}, {"c": 1 - c}
    sems = (send, recv)
    half = block.shape[0] // 2
    top, low = pl.ds(0, half), pl.ds(half, half)
    own, next_x = 2 * x + y, 2 * (1 - x) + y
    next_y, across = 2 * x + 1 - y, 2 * (1 - x) + 1 - y
    meet([to_x, to_y] + ([to_c] if cores == 2 else []))

    def give(index, rows, device):
        copy = remote(block.at[rows], out.at[own, slot, rows], sems, index, device)
        copy.start()
        return copy

    def forward(index, chip, rows, device):
        place = out.at[chip, slot, rows]
        copy = remote(place, place, sems, index, device)
        copy.start()
        return copy

    x_top = give(0, top, to_x)
    y_low = give(1, low, to_y)
    x_low = give(2, low, to_x)
    y_top = give(3, top, to_y)
    stay = pltpu.make_async_copy(block, out.at[own, slot], here)
    stay.start()
    sends = [x_top, y_low, x_low, y_top]
    passed = []
    if cores == 2:
        passed.append(give(4, pl.ds(0, 2 * half), to_c))
    x_top.wait_recv()
    y_across = forward(5, next_x, top, to_y)
    if cores == 2:
        passed.append(forward(6, next_x, top, to_c))
    y_low.wait_recv()
    x_across = forward(7, next_y, low, to_x)
    if cores == 2:
        passed.append(forward(8, next_y, low, to_c))
    x_low.wait_recv()
    if cores == 2:
        passed.append(forward(9, next_x, low, to_c))
    y_top.wait_recv()
    if cores == 2:
        passed.append(forward(10, next_y, top, to_c))
    y_across.wait_recv()
    if cores == 2:
        passed.append(forward(11, across, top, to_c))
    x_across.wait_recv()
    if cores == 2:
        passed.append(forward(12, across, low, to_c))
    for copy in passed:
        copy.wait_recv()
    stay.wait()
    for copy in sends + [y_across, x_across] + passed:
        copy.wait_send()


def gather_rows(block, cores, ident):
    rows, cols = block.shape
    out = pl.pallas_call(
        partial(gather_kernel, cores),
        out_shape=jax.ShapeDtypeStruct((4, cores, rows, cols), block.dtype),
        in_specs=[IN_VMEM],
        out_specs=ANY,
        scratch_shapes=[
            pltpu.SemaphoreType.DMA((13,)),
            pltpu.SemaphoreType.DMA((13,)),
            pltpu.SemaphoreType.DMA,
        ],
        compiler_params=pltpu.CompilerParams(
            collective_id=ident, has_side_effects=True, vmem_limit_bytes=VMEM_LIMIT
        ),
        name="gather_rows",
    )(block)
    return out.reshape(4 * cores * rows, cols)


def add_rows(target, first, rows, terms):
    step = 16

    @pl.loop(0, rows // step)
    def _(i):
        at = pl.ds(first + i * step, step)
        total = None
        for ref, ref_first in terms:
            part = ref[pl.ds(ref_first + i * step, step), :].astype(F32)
            total = part if total is None else total + part
        target[at, :] = total.astype(target.dtype)


def scatter_kernel(cores, part, out, side, ready, got_x, got_y, pass_x, pass_y, send, recv):
    x, y, c = (lax.axis_index(a) for a in PLANE)
    slot = c if cores == 2 else 0
    to_x, to_y, to_c = {"x": 1 - x}, {"y": 1 - y}, {"c": 1 - c}
    sems = (send, recv)
    rows = part.shape[2]
    half = rows // 2
    top, low = pl.ds(0, half), pl.ds(half, half)
    own, next_x = 2 * x + y, 2 * (1 - x) + y
    next_y, across = 2 * x + 1 - y, 2 * (1 - x) + 1 - y
    order = [across, next_x, next_y, own]
    meet([to_x, to_y] + ([to_c] if cores == 2 else []))
    from_side = []
    if cores == 2:
        for k, chip in enumerate(order):
            copy = remote(part.at[chip, 1 - c], side.at[k], sems, k, to_c)
            copy.start()
            from_side.append(copy)

    def terms(k, first):
        out_terms = [(part.at[order[k], slot], first)]
        if cores == 2:
            out_terms.append((side.at[k], first))
        return out_terms

    def arrived(k):
        if cores == 2:
            from_side[k].wait_recv()

    def launch(index, src, dst, device):
        copy = remote(src, dst, sems, index, device)
        copy.start()
        return copy

    arrived(0)
    add_rows(ready.at[0], 0, half, terms(0, 0))
    a_x = launch(4, ready.at[0, top], pass_x, to_x)
    add_rows(ready.at[0], half, half, terms(0, half))
    a_y = launch(5, ready.at[0, low], pass_y, to_y)
    arrived(1)
    add_rows(ready.at[1], 0, half, terms(1, 0))
    x_top = launch(6, ready.at[1, top], got_x.at[top], to_x)
    arrived(2)
    add_rows(ready.at[2], half, half, terms(2, half))
    y_low = launch(7, ready.at[2, low], got_y.at[low], to_y)
    a_y.wait_recv()
    add_rows(ready.at[1], half, half, terms(1, half) + [(pass_y, 0)])
    x_low = launch(8, ready.at[1, low], got_x.at[low], to_x)
    a_x.wait_recv()
    add_rows(ready.at[2], 0, half, terms(2, 0) + [(pass_x, 0)])
    y_top = launch(9, ready.at[2, top], got_y.at[top], to_y)
    arrived(3)
    x_top.wait_recv()
    y_low.wait_recv()
    x_low.wait_recv()
    y_top.wait_recv()
    add_rows(out, 0, rows, terms(3, 0) + [(got_x, 0), (got_y, 0)])
    for copy in from_side + [a_x, a_y, x_top, y_low, x_low, y_top]:
        copy.wait_send()


def scatter_rows(partial_rows, cores, ident):
    rows = partial_rows.shape[0] // (4 * cores)
    cols = partial_rows.shape[1]
    part = partial_rows.astype(BF16).reshape(4, cores, rows, cols)
    return pl.pallas_call(
        partial(scatter_kernel, cores),
        out_shape=jax.ShapeDtypeStruct((rows, cols), F32),
        in_specs=[IN_VMEM],
        out_specs=IN_VMEM,
        scratch_shapes=[
            pltpu.VMEM((4, rows if cores == 2 else 16, cols), BF16),
            pltpu.VMEM((3, rows, cols), BF16),
            pltpu.VMEM((rows, cols), BF16),
            pltpu.VMEM((rows, cols), BF16),
            pltpu.VMEM((rows // 2, cols), BF16),
            pltpu.VMEM((rows // 2, cols), BF16),
            pltpu.SemaphoreType.DMA((10,)),
            pltpu.SemaphoreType.DMA((10,)),
        ],
        compiler_params=pltpu.CompilerParams(
            collective_id=ident, has_side_effects=True, vmem_limit_bytes=VMEM_LIMIT
        ),
        name="scatter_rows",
    )(part)


def lanes(rows):
    return lax.broadcasted_iota(jnp.int32, (rows, LANES), 1)


def rotated(block, cosine, sine_signed):
    lane = lanes(block.shape[0])
    turned = jnp.where(
        lane % HEAD_DIM < HEAD_DIM // 2,
        pltpu.roll(block, LANES - HEAD_DIM // 2, 1),
        pltpu.roll(block, HEAD_DIM // 2, 1),
    )
    return block * cosine + turned * sine_signed


def key_spans(pieces, rows):
    reach = WINDOW // rows
    return [
        (max(0, 2 * j - reach) * rows, (2 * j + 2) * rows) for j in range(pieces // 2)
    ]


def seen(first_ref, place_ref, rows, low, high):
    keys = low + lax.broadcasted_iota(jnp.int32, (1, high - low), 1)
    return (keys >= first_ref[rows, :]) & (keys <= place_ref[rows, :])


def forward_kernel(
    spans, width, q_raw, k_raw, v_ref, cos_q, sin_q, cos_k, sin_k, first, place,
    q_out, k_out, ctx_out, lse_out, v_keep,
):
    valid = width - pl.program_id(0) * LANES
    k_rows = k_raw.shape[0]
    keep = lanes(k_rows) < valid
    k_out[...] = jnp.where(keep, rotated(k_raw[...], cos_k[...], sin_k[...]), 0.0).astype(BF16)
    v_keep[...] = jnp.where(keep, v_ref[...], jnp.zeros((), BF16))
    keep_q = lanes(q_raw.shape[0]) < valid
    q_out[...] = jnp.where(keep_q, rotated(q_raw[...], cos_q[...], sin_q[...]), 0.0).astype(BF16)
    rows_j = q_raw.shape[0] // len(spans)
    left = lanes(rows_j) < HEAD_DIM
    zero = jnp.zeros((), BF16)
    for j, (low, high) in enumerate(spans):
        rows = pl.ds(j * rows_j, rows_j)
        visible = seen(first, place, rows, low, high)
        query = q_out[rows, :]
        halves = []
        for side in range(2):
            mine = jnp.where(left if side == 0 else ~left, query, zero)
            scores = lax.dot_general(
                mine, k_out[low:high, :], (((1,), (1,)), ((), ())), preferred_element_type=F32
            )
            scores = jnp.where(visible, scores * 0.125, NEGATIVE)
            top = jnp.max(scores, -1, keepdims=True)
            grown = jnp.exp(scores - top)
            total = jnp.sum(grown, -1, keepdims=True)
            probs = (grown * (1.0 / total)).astype(BF16)
            ctx = jnp.dot(probs, v_keep[low:high, :], preferred_element_type=F32)
            halves.append((ctx, top + jnp.log(total)))
        ctx_out[rows, :] = jnp.where(left, halves[0][0], halves[1][0]).astype(BF16)
        lse_out[rows, :] = jnp.where(left, halves[0][1], halves[1][1])


def lane_block(rows):
    return pl.BlockSpec((rows, LANES), lambda p: (0, p))


def whole(rows, cols):
    return pl.BlockSpec((rows, cols), lambda p: (0, 0))


def attend_forward(q_raw, k_raw, value, tables, limits, pieces):
    q_rows, width = q_raw.shape
    k_rows = k_raw.shape[0]
    spans = key_spans(pieces, k_rows // pieces)
    steps = -(-width // LANES)
    shape = jax.ShapeDtypeStruct
    return pl.pallas_call(
        partial(forward_kernel, spans, width),
        grid=(steps,),
        out_shape=(
            shape((q_rows, width), BF16),
            shape((k_rows, width), BF16),
            shape((q_rows, width), BF16),
            shape((q_rows, width), F32),
        ),
        in_specs=[
            lane_block(q_rows),
            lane_block(k_rows),
            lane_block(k_rows),
            whole(q_rows, LANES),
            whole(q_rows, LANES),
            whole(k_rows, LANES),
            whole(k_rows, LANES),
            whole(q_rows, 1),
            whole(q_rows, 1),
        ],
        out_specs=(
            lane_block(q_rows),
            lane_block(k_rows),
            lane_block(q_rows),
            lane_block(q_rows),
        ),
        scratch_shapes=[pltpu.VMEM((k_rows, LANES), BF16)],
        compiler_params=pltpu.CompilerParams(vmem_limit_bytes=VMEM_LIMIT),
        name="attend_forward",
    )(q_raw, k_raw, value, *tables, *limits)


def backward_kernel(
    spans, width, q_ref, k_ref, v_ref, g_ref, lse, cos_q, sin_q, cos_k, sin_k, first, place,
    dq_out, dk_out, dv_out, k_keep, v_keep,
):
    valid = width - pl.program_id(0) * LANES
    zero = jnp.zeros((), BF16)
    keep = lanes(k_ref.shape[0]) < valid
    k_keep[...] = jnp.where(keep, k_ref[...], zero)
    v_keep[...] = jnp.where(keep, v_ref[...], zero)
    dk_out[...] = jnp.zeros_like(dk_out)
    dv_out[...] = jnp.zeros_like(dv_out)
    rows_j = q_ref.shape[0] // len(spans)
    lane = lanes(rows_j)
    left = (lane < HEAD_DIM) & (lane < valid)
    right = (lane >= HEAD_DIM) & (lane < valid)
    for j, (low, high) in enumerate(spans):
        rows = pl.ds(j * rows_j, rows_j)
        visible = seen(first, place, rows, low, high)
        query, grad = q_ref[rows, :], g_ref[rows, :]
        stats = lse[rows, :]
        halves = []
        for side in range(2):
            mask = left if side == 0 else right
            mine = jnp.where(mask, query, zero)
            grad_mine = jnp.where(mask, grad, zero)
            nt = (((1,), (1,)), ((), ()))
            tn = (((0,), (0,)), ((), ()))
            scores = lax.dot_general(mine, k_keep[low:high, :], nt, preferred_element_type=F32)
            column = side * HEAD_DIM
            log_total = stats[:, column : column + 1]
            probs = jnp.where(visible, jnp.exp(scores * 0.125 - log_total), 0.0)
            grad_probs = lax.dot_general(
                grad_mine, v_keep[low:high, :], nt, preferred_element_type=F32
            )
            mixed = probs * grad_probs
            delta = jnp.sum(mixed, -1, keepdims=True)
            grad_scores = (mixed - probs * delta).astype(BF16)
            halves.append(
                jnp.dot(grad_scores, k_keep[low:high, :], preferred_element_type=F32) * 0.125
            )
            dk_out[low:high, :] += (
                lax.dot_general(grad_scores, mine, tn, preferred_element_type=F32) * 0.125
            )
            dv_out[low:high, :] += lax.dot_general(
                probs.astype(BF16), grad_mine, tn, preferred_element_type=F32
            )
        grad_query = jnp.where(lane < HEAD_DIM, halves[0], halves[1])
        dq_out[rows, :] = rotated(grad_query, cos_q[rows, :], -sin_q[rows, :]).astype(BF16)
    dk_out[...] = rotated(dk_out[...], cos_k[...], -sin_k[...])


def attend_backward(query, key, value, grad, lse, tables, limits, pieces):
    q_rows, width = query.shape
    k_rows = key.shape[0]
    spans = key_spans(pieces, k_rows // pieces)
    steps = -(-width // LANES)
    shape = jax.ShapeDtypeStruct
    return pl.pallas_call(
        partial(backward_kernel, spans, width),
        grid=(steps,),
        out_shape=(
            shape((q_rows, width), BF16),
            shape((k_rows, width), F32),
            shape((k_rows, width), F32),
        ),
        in_specs=[
            lane_block(q_rows),
            lane_block(k_rows),
            lane_block(k_rows),
            lane_block(q_rows),
            lane_block(q_rows),
            whole(q_rows, LANES),
            whole(q_rows, LANES),
            whole(k_rows, LANES),
            whole(k_rows, LANES),
            whole(q_rows, 1),
            whole(q_rows, 1),
        ],
        out_specs=(lane_block(q_rows), lane_block(k_rows), lane_block(k_rows)),
        scratch_shapes=[pltpu.VMEM((k_rows, LANES), BF16)] * 2,
        compiler_params=pltpu.CompilerParams(vmem_limit_bytes=VMEM_LIMIT),
        name="attend_backward",
    )(query, key, value, grad, lse, *tables, *limits)


def norm_back(grad_normed, unit_rows, rms_rows, gain_rows):
    scaled = grad_normed * gain_rows
    return rms_rows * (scaled - unit_rows * jnp.mean(scaled * unit_rows, -1, keepdims=True))


def on_device(
    tokens,
    doc_lengths,
    cotangent,
    attn_gain,
    w_query,
    w_key,
    w_value,
    w_out,
    mlp_gain,
    w_gate,
    w_up,
    w_down,
):
    outer = lax.axis_size("g")
    pieces_z = lax.axis_size("z")
    x, y, c = (lax.axis_index(a) for a in PLANE)
    own = 2 * y + c

    def joined(shard):
        if outer == 1:
            return shard
        return lax.all_gather(shard, "g", axis=0, tiled=True)

    w_query, w_key, w_value, w_out = map(joined, (w_query, w_key, w_value, w_out))
    w_gate, w_up, w_down = map(joined, (w_gate, w_up, w_down))
    rows_d = w_query.shape[0]
    model = w_query.shape[1]
    tok_rows = tokens.shape[1]
    pieces = 2 * pieces_z
    seq_len = pieces * tok_rows
    cols_h = model // 4
    cols_f = w_gate.shape[1] // 8

    turn_pairs = [
        (i * pieces_z + z, z * pieces_z + i) for i in range(pieces_z) for z in range(pieces_z)
    ]

    def turned(block):
        return lax.ppermute(block, ("y", "c", "z"), turn_pairs)

    gains = lax.all_gather(
        jnp.stack([joined(attn_gain), joined(mlp_gain)]), ("y", "c"), axis=1, tiled=True
    ).astype(F32)
    gain_one, gain_two = gains[0:1], gains[1:2]
    lengths = turned(doc_lengths)[0]
    inputs = turned(tokens[0]).astype(F32)
    upstream = turned(cotangent[0]).astype(F32)

    def head_cols(weight, group):
        return lax.dynamic_slice_in_dim(weight, group * cols_h, cols_h, 1)

    def qkv_cols(group):
        return jnp.concatenate([head_cols(w, group) for w in (w_query, w_key, w_value)], 1)

    qkv_own = qkv_cols(2 * y + x)
    qkv_far = swap(qkv_cols(2 * (1 - y) + x), "y")
    qkv_pair = jnp.where(y == 0, jnp.stack([qkv_own, qkv_far]), jnp.stack([qkv_far, qkv_own]))
    qkv_side = swap(qkv_pair, "c")
    w_qkv = jnp.where(
        c == 0, jnp.stack([qkv_pair, qkv_side], 1), jnp.stack([qkv_side, qkv_pair], 1)
    ).reshape(4 * rows_d, 3 * cols_h)
    out_side = swap(w_out, "c")
    w_out_use = jnp.where(c == x, w_out, out_side)

    def ff_cols(dest):
        first = (2 * dest + x) * cols_f
        return jnp.concatenate(
            [lax.dynamic_slice_in_dim(w, first, cols_f, 1) for w in (w_gate, w_up)], 1
        )

    ff_own = ff_cols(own)
    ff_c = swap(ff_cols(2 * y + 1 - c), "c")
    ff_y = swap(ff_cols(2 * (1 - y) + c), "y")
    ff_yc = lax.ppermute(
        ff_cols(2 * (1 - y) + 1 - c), ("y", "c"), [(i, 3 - i) for i in range(4)]
    )

    def ordered(a, b, flag):
        return jnp.where(flag == 0, jnp.stack([a, b]), jnp.stack([b, a]))

    ff_near = ordered(ff_own, ff_c, c)
    ff_far = ordered(ff_y, ff_yc, c)
    w_ff = ordered(ff_near, ff_far, y).reshape(4 * rows_d, 2 * cols_f)
    down_use = lax.dynamic_slice_in_dim(w_down, x * cols_f, cols_f, 0)

    place = jnp.arange(seq_len, dtype=jnp.int32)
    docs, offset = layout(lengths, place)
    cosine, sine_table = rope_tables(offset)

    def own_rows(array):
        cols = array.shape[1:]
        split = array.reshape((pieces // 2, 2, tok_rows) + cols)
        return lax.dynamic_index_in_dim(split, c, 1, keepdims=False).reshape(
            (seq_len // 2,) + cols
        )

    def other_rows(array):
        cols = array.shape[1:]
        split = array.reshape((pieces // 2, 2, tok_rows) + cols)
        return lax.dynamic_index_in_dim(split, 1 - c, 1, keepdims=False).reshape(
            (seq_len // 2,) + cols
        )

    tables = (own_rows(cosine), own_rows(sine_table), cosine, sine_table)
    first_key = jnp.maximum(place - offset, place - (WINDOW - 1))
    limits = (own_rows(first_key)[:, None], own_rows(place)[:, None])

    grad_mlp = lax.all_gather((BETA * upstream).astype(BF16), PLANE, axis=0, tiled=True)

    rms_one = lax.rsqrt(jnp.mean(inputs * inputs, -1, keepdims=True) + EPSILON)
    unit_one = inputs * rms_one
    normed_one = gather_rows((unit_one * gain_one).astype(BF16), 2, 1)

    query_raw = dot(own_rows(normed_one), w_qkv[:, :cols_h])
    key_raw = dot(normed_one, w_qkv[:, cols_h : 2 * cols_h])
    value = dot(normed_one, w_qkv[:, 2 * cols_h :]).astype(BF16)
    query, key, context, lse = attend_forward(query_raw, key_raw, value, tables, limits, pieces)

    attn_out = scatter_rows(dot(context, w_out_use), 1, 2)
    hidden_res = inputs + BETA * attn_out
    rms_two = lax.rsqrt(jnp.mean(hidden_res * hidden_res, -1, keepdims=True) + EPSILON)
    unit_two = hidden_res * rms_two
    normed_two = gather_rows((unit_two * gain_two).astype(BF16), 2, 3)

    gate_up = dot(normed_two, w_ff)
    gate, up = gate_up[:, :cols_f], gate_up[:, cols_f:]
    sigmoid_gate = jax.nn.sigmoid(gate)
    silu_gate = gate * sigmoid_gate
    activation = (silu_gate * up).astype(BF16)
    mlp_out = lax.psum_scatter(
        dot(activation, down_use).astype(BF16), PLANE, scatter_dimension=0, tiled=True
    ).astype(F32)
    output = turned((hidden_res + BETA * mlp_out).astype(BF16))[None]

    grad_activation = dot_nt(grad_mlp, down_use)
    grad_up = (grad_activation * silu_gate).astype(BF16)
    grad_gate = (
        grad_activation * up * (sigmoid_gate * (1.0 + gate * (1.0 - sigmoid_gate)))
    ).astype(BF16)
    grad_ff = jnp.concatenate([grad_gate, grad_up], 1)
    grad_normed_two = scatter_rows(dot_nt(grad_ff, w_ff), 2, 4)

    def summed_z(grad):
        part = lax.psum_scatter(grad.astype(BF16), "z", scatter_dimension=0, tiled=True)
        return lax.all_gather(part, "z", axis=0, tiled=True)

    grad_down = summed_z(dot_tn(activation, grad_mlp))
    grad_ff_side = swap(grad_ff, "c")
    grad_ff_chip = jnp.concatenate(
        [
            jnp.where(c == 0, grad_ff, grad_ff_side),
            jnp.where(c == 0, grad_ff_side, grad_ff),
        ],
        1,
    )

    def row_block(normed, y_of):
        return lax.dynamic_slice_in_dim(normed, (2 * y_of + c) * rows_d, rows_d, 1)

    def row_grads(normed, grads):
        near = dot_tn(row_block(normed, y), grads).astype(BF16)
        far = dot_tn(row_block(normed, 1 - y), grads).astype(BF16)
        return (near, far)

    grad_ff_w = [summed_z(g) for g in row_grads(normed_two, grad_ff_chip)]

    gain_grad_two = jnp.sum(grad_normed_two * unit_two, 0)
    grad_hidden = upstream + norm_back(grad_normed_two, unit_two, rms_two, gain_two)
    grad_attn = gather_rows((BETA * grad_hidden).astype(BF16), 1, 5)
    grad_context = dot_nt(grad_attn, w_out_use).astype(BF16)

    grad_out_part = dot_tn(context, grad_attn).astype(BF16)
    half = model // 2
    keep = lax.dynamic_slice_in_dim(grad_out_part, c * half, half, 1)
    give = lax.dynamic_slice_in_dim(grad_out_part, (1 - c) * half, half, 1)
    grad_out_half = summed_z(keep.astype(F32) + swap(give, "c").astype(F32))

    grad_query, grad_key, grad_value = attend_backward(
        query, key, value, grad_context, lse, tables, limits, pieces
    )
    grad_kv = jnp.concatenate([grad_key, grad_value], 1)
    grad_kv = own_rows(grad_kv) + swap(other_rows(grad_kv).astype(BF16), "c").astype(F32)
    grad_key = grad_kv[:, :cols_h].astype(BF16)
    grad_value = grad_kv[:, cols_h:].astype(BF16)
    grad_qkv = jnp.concatenate([grad_query, grad_key, grad_value], 1)

    grad_normed_one = scatter_rows(dot_nt(grad_qkv, w_qkv), 1, 6)
    grad_qkv_side = swap(grad_qkv, "c")
    grad_qkv_all = (
        jnp.where(
            c == 0,
            jnp.stack([grad_qkv, grad_qkv_side]),
            jnp.stack([grad_qkv_side, grad_qkv]),
        )
        .reshape(2, pieces // 2, tok_rows, 3 * cols_h)
        .transpose(1, 0, 2, 3)
        .reshape(seq_len, 3 * cols_h)
    )
    grad_qkv_w = [summed_z(g) for g in row_grads(normed_one, grad_qkv_all)]

    gain_grad_one = jnp.sum(grad_normed_one * unit_one, 0)
    grad_inputs = grad_hidden + norm_back(grad_normed_one, unit_one, rms_one, gain_one)
    grad_tokens = turned(grad_inputs.astype(BF16))[None]

    gain_grads = lax.psum(jnp.stack([gain_grad_one, gain_grad_two]), ("x", "y", "c", "g", "z"))
    shard = attn_gain.shape[0]
    first = own * rows_d + lax.axis_index("g") * shard
    gain_grads = lax.dynamic_slice_in_dim(gain_grads, first, shard, 1)

    def finish(grad):
        if outer > 1:
            grad = lax.psum_scatter(grad, "g", scatter_dimension=0, tiled=True)
        return grad.astype(F32)

    def owner_rows(pair):
        near, far = pair[0], swap(pair[1], "y")
        both = ordered(near, far, y)
        return lax.all_gather(both, "x", axis=0, tiled=False)

    ff_all = owner_rows(grad_ff_w)
    ff_all = [
        jnp.concatenate(
            [
                ff_all[i, j, :, (2 * k + kind) * cols_f : (2 * k + kind + 1) * cols_f]
                for j in range(2)
                for k in range(2)
                for i in range(2)
            ],
            1,
        )
        for kind in range(2)
    ]
    qkv_all = owner_rows(grad_qkv_w)
    qkv_all = [
        jnp.concatenate(
            [
                qkv_all[i, j, :, kind * cols_h : (kind + 1) * cols_h]
                for j in range(2)
                for i in range(2)
            ],
            1,
        )
        for kind in range(3)
    ]
    down_all = lax.all_gather(grad_down, "x", axis=0, tiled=True)
    out_near = lax.all_gather(grad_out_half, "c", axis=1, tiled=True)
    out_far = lax.ppermute(out_near, ("x", "c"), [(0, 2), (3, 1)])
    out_all = jnp.where(c == x, out_near, out_far)

    return (
        output,
        grad_tokens,
        gain_grads[0],
        finish(qkv_all[0]),
        finish(qkv_all[1]),
        finish(qkv_all[2]),
        finish(out_all),
        gain_grads[1],
        finish(ff_all[0]),
        finish(ff_all[1]),
        finish(down_all),
    )


def solution(mesh):
    seq, fsdp, rep = (mesh.shape[a] for a in ("seq", "fsdp", "rep"))
    inner = Mesh(
        mesh.devices.reshape(seq, rep // 2, 2, fsdp // rep, rep), ("x", "y", "c", "g", "z")
    )
    owners = ("y", "c", "g")
    token_spec = P(owners, ("x", "z"), None)
    placed = (token_spec, P(owners, None), token_spec, P(owners)) + (P(owners, None),) * 4
    placed = placed + (P(owners),) + (P(owners, None),) * 3
    return jax.shard_map(
        on_device,
        mesh=inner,
        in_specs=placed,
        out_specs=(token_spec, token_spec, P(owners))
        + (P(owners, None),) * 4
        + (P(owners),)
        + (P(owners, None),) * 3,
        check_vma=False,
    )
```

```python
from functools import partial
import math

import jax
import jax.numpy as jnp
from jax import lax
from jax.experimental import pallas as pl
from jax.experimental.pallas import tpu as pltpu
from jax.sharding import Mesh, PartitionSpec as P

HEADS = 36
HEAD_DIM = 64
WINDOW = 1024

BETA = 1.4 / math.sqrt(40.0)
EPSILON = 1e-05
NEGATIVE = -1e30

PLANE = ("x", "y", "c")
LANES = 128
VMEM_LIMIT = 60 * 1024 * 1024
F32 = jnp.float32
BF16 = jnp.bfloat16


def dot(left, right):
    return jnp.dot(left, right, preferred_element_type=F32)


def dot_tn(left, right):
    return lax.dot_general(left, right, (((0,), (0,)), ((), ())), preferred_element_type=F32)


def dot_nt(left, right):
    return lax.dot_general(left, right, (((1,), (1,)), ((), ())), preferred_element_type=F32)


def swap(array, axis):
    return lax.ppermute(array, axis, [(0, 1), (1, 0)])


def layout(lengths, position):
    doc_ends = jnp.cumsum(lengths)
    doc_ids = jnp.sum((position[:, None] >= doc_ends[None, :]).astype(jnp.int32), axis=1)
    doc_starts = doc_ends - lengths
    choose = doc_ids[:, None] == jnp.arange(lengths.shape[0], dtype=jnp.int32)[None, :]
    doc_first = jnp.sum(jnp.where(choose, doc_starts[None, :], 0), axis=1)
    return (doc_ids, position - doc_first)


def rope_tables(offset):
    half_dim = HEAD_DIM // 2
    frequency = jnp.exp(
        jnp.arange(half_dim, dtype=F32) * (-2.0 * math.log(10000.0) / HEAD_DIM)
    )
    angles = offset.astype(F32)[:, None] * frequency[None, :]
    cosine = jnp.cos(angles)
    sine_table = jnp.sin(angles)
    return (
        jnp.concatenate([cosine, cosine] * 2, 1),
        jnp.concatenate([-sine_table, sine_table] * 2, 1),
    )


MESH_ID = pl.DeviceIdType.MESH
ANY = pl.BlockSpec(memory_space=pl.ANY)
IN_VMEM = pl.BlockSpec(memory_space=pltpu.VMEM)


def remote(src, dst, sems, index, device):
    return pltpu.make_async_remote_copy(
        src_ref=src,
        dst_ref=dst,
        send_sem=sems[0].at[index],
        recv_sem=sems[1].at[index],
        device_id=device,
        device_id_type=MESH_ID,
    )


def meet(devices):
    barrier = pltpu.get_barrier_semaphore()
    for device in devices:
        pl.semaphore_signal(barrier, inc=1, device_id=device, device_id_type=MESH_ID)
    pl.semaphore_wait(barrier, len(devices))


def gather_steps(cores, block, out, sems, base, here):
    x, y, c = (lax.axis_index(a) for a in PLANE)
    slot = c if cores == 2 else 0
    to_x, to_y, to_c = {"x": 1 - x}, {"y": 1 - y}, {"c": 1 - c}
    half = block.shape[0] // 2
    top, low = pl.ds(0, half), pl.ds(half, half)
    own, next_x = 2 * x + y, 2 * (1 - x) + y
    next_y, across = 2 * x + 1 - y, 2 * (1 - x) + 1 - y

    def give(index, rows, device):
        copy = remote(block.at[rows], out.at[own, slot, rows], sems, base + index, device)
        copy.start()
        return copy

    def forward(index, chip, rows, device):
        place = out.at[chip, slot, rows]
        copy = remote(place, place, sems, base + index, device)
        copy.start()
        return copy

    x_top = give(0, top, to_x)
    y_low = give(1, low, to_y)
    x_low = give(2, low, to_x)
    y_top = give(3, top, to_y)
    stay = pltpu.make_async_copy(block, out.at[own, slot], here)
    stay.start()
    sends = [x_top, y_low, x_low, y_top]
    passed = []
    if cores == 2:
        passed.append(give(4, pl.ds(0, 2 * half), to_c))
    x_top.wait_recv()
    y_across = forward(5, next_x, top, to_y)
    if cores == 2:
        passed.append(forward(6, next_x, top, to_c))
    y_low.wait_recv()
    x_across = forward(7, next_y, low, to_x)
    if cores == 2:
        passed.append(forward(8, next_y, low, to_c))
    x_low.wait_recv()
    if cores == 2:
        passed.append(forward(9, next_x, low, to_c))
    y_top.wait_recv()
    if cores == 2:
        passed.append(forward(10, next_y, top, to_c))
    y_across.wait_recv()
    if cores == 2:
        passed.append(forward(11, across, top, to_c))
    x_across.wait_recv()
    if cores == 2:
        passed.append(forward(12, across, low, to_c))
    for copy in passed:
        copy.wait_recv()
    stay.wait()
    for copy in sends + [y_across, x_across] + passed:
        copy.wait_send()


def gather_kernel(cores, block, out, send, recv, here):
    x, y, c = (lax.axis_index(a) for a in PLANE)
    meet([{"x": 1 - x}, {"y": 1 - y}] + ([{"c": 1 - c}] if cores == 2 else []))
    gather_steps(cores, block, out, (send, recv), 0, here)


def gather_rows(block, cores, ident):
    rows, cols = block.shape
    out = pl.pallas_call(
        partial(gather_kernel, cores),
        out_shape=jax.ShapeDtypeStruct((4, cores, rows, cols), block.dtype),
        in_specs=[IN_VMEM],
        out_specs=ANY,
        scratch_shapes=[
            pltpu.SemaphoreType.DMA((13,)),
            pltpu.SemaphoreType.DMA((13,)),
            pltpu.SemaphoreType.DMA,
        ],
        compiler_params=pltpu.CompilerParams(
            collective_id=ident, has_side_effects=True, vmem_limit_bytes=VMEM_LIMIT
        ),
        name="gather_rows",
    )(block)
    return out.reshape(4 * cores * rows, cols)


def front_kernel(
    tokens, cotangent, lengths, gains, near, far, w_out,
    rows_all, tok_out, cot_out, len_out, gain_out, qkv_out, side_out,
    tok_in, len_in, gain_in, normed, send, recv, here,
):
    x, y, c = (lax.axis_index(a) for a in PLANE)
    z = lax.axis_index("z")
    to_x, to_y, to_c = {"x": 1 - x}, {"y": 1 - y}, {"c": 1 - c}
    to_yc = {"y": 1 - y, "c": 1 - c}
    own = 2 * y + c
    goal = {"y": z // 2, "c": z % 2, "z": own}
    sems = (send, recv)
    moves = own != z
    barrier = pltpu.get_barrier_semaphore()
    for device in (to_x, to_y, to_c, to_yc):
        pl.semaphore_signal(barrier, inc=1, device_id=device, device_id_type=MESH_ID)

    @pl.when(moves)
    def _():
        pl.semaphore_signal(barrier, inc=1, device_id=goal, device_id_type=MESH_ID)
        pl.semaphore_wait(barrier, 5)

    @pl.when(~moves)
    def _():
        pl.semaphore_wait(barrier, 4)

    gain_copies = [
        remote(gains, gain_in.at[2 * y + c], sems, k, device)
        for k, device in enumerate((to_y, to_c, to_yc))
    ]
    turn_copies = [
        remote(src, dst, sems, 3 + k, goal)
        for k, (src, dst) in enumerate(
            ((lengths, len_in), (tokens, tok_in), (cotangent, cot_out))
        )
    ]
    stay_copies = [
        pltpu.make_async_copy(src, dst, here.at[k])
        for k, (src, dst) in enumerate(
            ((lengths, len_in), (tokens, tok_in), (cotangent, cot_out))
        )
    ]
    for copy in gain_copies:
        copy.start()
    own_gain = pltpu.make_async_copy(gains, gain_in.at[2 * y + c], here.at[3])
    own_gain.start()

    @pl.when(moves)
    def _():
        for copy in turn_copies[:2]:
            copy.start()

    @pl.when(~moves)
    def _():
        for copy in stay_copies:
            copy.start()

    far_copy = remote(far, qkv_out.at[y, c], sems, 6, to_y)
    near_copy = remote(near, qkv_out.at[y, c], sems, 7, to_c)
    side_copy = remote(w_out, side_out, sems, 8, to_c)
    far_copy.start()
    near_copy.start()
    side_copy.start()
    own_near = pltpu.make_async_copy(near, qkv_out.at[y, c], here.at[4])
    own_near.start()

    @pl.when(moves)
    def _():
        for copy in turn_copies[:2]:
            copy.wait_recv()
        turn_copies[2].start()

    @pl.when(~moves)
    def _():
        for copy in stay_copies[:2]:
            copy.wait()

    own_gain.wait()
    for copy in gain_copies:
        copy.wait_recv()
    len_out[...] = len_in[...]
    gain_out[...] = gain_in[0] + gain_in[1] + gain_in[2] + gain_in[3]
    keep_tok = pltpu.make_async_copy(tok_in, tok_out, here.at[5])
    keep_tok.start()
    step = 16

    @pl.loop(0, tok_in.shape[0] // step)
    def _(i):
        at = pl.ds(i * step, step)
        rows = tok_in[at, :].astype(F32)
        scale = lax.rsqrt(jnp.mean(rows * rows, -1, keepdims=True) + EPSILON)
        normed[at, :] = (rows * scale * gain_out[0:1, :]).astype(BF16)

    gather_steps(2, normed, rows_all, sems, 9, here.at[6])
    far_copy.wait_recv()
    from_far = qkv_out.at[1 - y, c]
    pass_copy = remote(from_far, from_far, sems, 22, to_c)
    pass_copy.start()
    keep_tok.wait()
    own_near.wait()
    near_copy.wait_recv()
    side_copy.wait_recv()
    pass_copy.wait_recv()

    @pl.when(moves)
    def _():
        turn_copies[2].wait_recv()
        for copy in turn_copies:
            copy.wait_send()

    @pl.when(~moves)
    def _():
        stay_copies[2].wait()

    for copy in gain_copies + [far_copy, near_copy, side_copy, pass_copy]:
        copy.wait_send()


def front(tokens, cotangent, lengths, gains, near, far, w_out, ident):
    rows, cols = tokens.shape
    shape = jax.ShapeDtypeStruct
    dma = pltpu.SemaphoreType.DMA
    outs = pl.pallas_call(
        front_kernel,
        out_shape=(
            shape((4, 2, rows, cols), BF16),
            shape((rows, cols), BF16),
            shape((rows, cols), BF16),
            shape(lengths.shape, lengths.dtype),
            shape(gains.shape, F32),
            shape((2, 2) + near.shape, BF16),
            shape(w_out.shape, BF16),
        ),
        in_specs=[IN_VMEM] * 6 + [ANY],
        out_specs=(ANY, ANY, ANY, IN_VMEM, IN_VMEM, ANY, ANY),
        scratch_shapes=[
            pltpu.VMEM((rows, cols), BF16),
            pltpu.VMEM(lengths.shape, lengths.dtype),
            pltpu.VMEM((4,) + gains.shape, F32),
            pltpu.VMEM((rows, cols), BF16),
            dma((23,)),
            dma((23,)),
            dma((7,)),
        ],
        compiler_params=pltpu.CompilerParams(
            collective_id=ident, has_side_effects=True, vmem_limit_bytes=VMEM_LIMIT
        ),
        name="front",
    )(tokens, cotangent, lengths, gains, near, far, w_out)
    return (outs[0].reshape(8 * rows, cols),) + tuple(outs[1:])


def add_rows(target, first, rows, terms):
    step = 16

    @pl.loop(0, rows // step)
    def _(i):
        at = pl.ds(first + i * step, step)
        total = None
        for ref, ref_first in terms:
            part = ref[pl.ds(ref_first + i * step, step), :].astype(F32)
            total = part if total is None else total + part
        target[at, :] = total.astype(target.dtype)


def scatter_kernel(cores, part, out, side, ready, got_x, got_y, pass_x, pass_y, send, recv):
    x, y, c = (lax.axis_index(a) for a in PLANE)
    slot = c if cores == 2 else 0
    to_x, to_y, to_c = {"x": 1 - x}, {"y": 1 - y}, {"c": 1 - c}
    sems = (send, recv)
    rows = part.shape[2]
    half = rows // 2
    top, low = pl.ds(0, half), pl.ds(half, half)
    own, next_x = 2 * x + y, 2 * (1 - x) + y
    next_y, across = 2 * x + 1 - y, 2 * (1 - x) + 1 - y
    order = [across, next_x, next_y, own]
    meet([to_x, to_y] + ([to_c] if cores == 2 else []))
    from_side = []
    if cores == 2:
        for k, chip in enumerate(order):
            copy = remote(part.at[chip, 1 - c], side.at[k], sems, k, to_c)
            copy.start()
            from_side.append(copy)

    def terms(k, first):
        out_terms = [(part.at[order[k], slot], first)]
        if cores == 2:
            out_terms.append((side.at[k], first))
        return out_terms

    def arrived(k):
        if cores == 2:
            from_side[k].wait_recv()

    def launch(index, src, dst, device):
        copy = remote(src, dst, sems, index, device)
        copy.start()
        return copy

    arrived(0)
    add_rows(ready.at[0], 0, half, terms(0, 0))
    a_x = launch(4, ready.at[0, top], pass_x, to_x)
    add_rows(ready.at[0], half, half, terms(0, half))
    a_y = launch(5, ready.at[0, low], pass_y, to_y)
    arrived(1)
    add_rows(ready.at[1], 0, half, terms(1, 0))
    x_top = launch(6, ready.at[1, top], got_x.at[top], to_x)
    arrived(2)
    add_rows(ready.at[2], half, half, terms(2, half))
    y_low = launch(7, ready.at[2, low], got_y.at[low], to_y)
    a_y.wait_recv()
    add_rows(ready.at[1], half, half, terms(1, half) + [(pass_y, 0)])
    x_low = launch(8, ready.at[1, low], got_x.at[low], to_x)
    a_x.wait_recv()
    add_rows(ready.at[2], 0, half, terms(2, 0) + [(pass_x, 0)])
    y_top = launch(9, ready.at[2, top], got_y.at[top], to_y)
    arrived(3)
    x_top.wait_recv()
    y_low.wait_recv()
    x_low.wait_recv()
    y_top.wait_recv()
    add_rows(out, 0, rows, terms(3, 0) + [(got_x, 0), (got_y, 0)])
    for copy in from_side + [a_x, a_y, x_top, y_low, x_low, y_top]:
        copy.wait_send()


def scatter_rows(partial_rows, cores, ident):
    rows = partial_rows.shape[0] // (4 * cores)
    cols = partial_rows.shape[1]
    part = partial_rows.astype(BF16).reshape(4, cores, rows, cols)
    return pl.pallas_call(
        partial(scatter_kernel, cores),
        out_shape=jax.ShapeDtypeStruct((rows, cols), F32),
        in_specs=[IN_VMEM],
        out_specs=IN_VMEM,
        scratch_shapes=[
            pltpu.VMEM((4, rows if cores == 2 else 16, cols), BF16),
            pltpu.VMEM((3, rows, cols), BF16),
            pltpu.VMEM((rows, cols), BF16),
            pltpu.VMEM((rows, cols), BF16),
            pltpu.VMEM((rows // 2, cols), BF16),
            pltpu.VMEM((rows // 2, cols), BF16),
            pltpu.SemaphoreType.DMA((10,)),
            pltpu.SemaphoreType.DMA((10,)),
        ],
        compiler_params=pltpu.CompilerParams(
            collective_id=ident, has_side_effects=True, vmem_limit_bytes=VMEM_LIMIT
        ),
        name="scatter_rows",
    )(part)


PARTS = 3
UNIT = 48 // PARTS
OUT_AT, NEAR_AT, DOWN_AT, UNITS = 3 * PARTS, 4 * PARTS, 7 * PARTS, 9 * PARTS
FAR_PLACE = 4 * 12 * PARTS
DOWN_PLACE = FAR_PLACE + 12 * PARTS
MINE_PLACE = DOWN_PLACE + 2 * 8 * PARTS
OUT_PLACE = MINE_PLACE + 4 * PARTS
PLACES = OUT_PLACE + 2 * 4 * PARTS


def reduce_kernel(
    grads, gain, out, gain_out,
    inbox, final, gain_in, rs_send, rs_recv, ag_send, ag_recv, y_send, y_recv, x_send, x_recv,
    o_send, o_recv, g_send, g_recv, here,
):
    x, y, c = (lax.axis_index(a) for a in PLANE)
    z = lax.axis_index("z")
    to_x, to_y, to_c = {"x": 1 - x}, {"y": 1 - y}, {"c": 1 - c}
    to_xc = {"x": 1 - x, "c": 1 - c}
    above, below = {"z": z + 1}, {"z": z - 1}
    others = [{"z": (z + k) % 4} for k in (1, 2, 3)]
    meet([to_x, to_y, to_c, to_xc] + others)

    def add_unit(target, sources):
        for first in range(0, UNIT, 16):
            at = pl.ds(first, 16)
            total = sources[0][at, :].astype(F32)
            for ref in sources[1:]:
                total = total + ref[at, :].astype(F32)
            target[at, :] = total.astype(BF16)

    def near_place(q, u):
        return (2 * x + y) * 12 * PARTS + q * 3 * PARTS + u - NEAR_AT

    def place(q, u):
        far = FAR_PLACE + q * 3 * PARTS + u
        mine = MINE_PLACE + q * PARTS + u - OUT_AT
        down = DOWN_PLACE + x * 8 * PARTS + q * 2 * PARTS + u - DOWN_AT
        return jnp.where(
            u < OUT_AT,
            far,
            jnp.where(u < NEAR_AT, mine, jnp.where(u < DOWN_AT, near_place(q, u), down)),
        )

    def copy(src, dst, send, recv, device):
        return pltpu.make_async_remote_copy(
            src_ref=src, dst_ref=dst, send_sem=send, recv_sem=recv,
            device_id=device, device_id_type=MESH_ID,
        )

    def rs_copy(src, q, u, slot, device):
        return copy(src, inbox.at[slot, u], rs_send.at[q, u], rs_recv.at[slot, u], device)

    def rs_arrived(slot, u):
        rs_copy(inbox.at[slot, u], 0, u, slot, to_x).wait_recv()

    def up(u):
        for q in (3, 2, 1):
            @pl.when(z == 0)
            def _():
                rs_copy(grads.at[q, u], q, u, q, above).start()

            @pl.when((z > 0) & (z < q))
            def _():
                rs_arrived(q, u)
                add_unit(inbox.at[q, u], [inbox.at[q, u], grads.at[q, u]])
                rs_copy(inbox.at[q, u], q, u, q, above).start()

    def down(u):
        for q in (0, 1, 2):
            @pl.when(z == 3)
            def _():
                rs_copy(grads.at[q, u], q, u, 4 if q == 2 else q, below).start()

            for here_z in (1, 2):
                if here_z > q:
                    @pl.when(z == here_z)
                    def _():
                        rs_arrived(q, u)
                        add_unit(inbox.at[q, u], [inbox.at[q, u], grads.at[q, u]])
                        slot = 4 if here_z - 1 == q else q
                        rs_copy(inbox.at[q, u], q, u, slot, below).start()

    def ag_copy(src, q, u, way, device):
        return copy(src, out.at[place(q, u)], ag_send.at[way, q, u], ag_recv.at[q, u], device)

    def stay_copy(u):
        return pltpu.make_async_copy(final.at[u], out.at[place(z, u)], here.at[u])

    def x_copy(src, dst, q, u):
        return copy(src, out.at[dst], x_send.at[q, u], x_recv.at[q, u], to_x)

    def y_copy(src, q, u, owner_y):
        dst = (2 * x + owner_y) * 12 * PARTS + q * 3 * PARTS + u
        return copy(src, out.at[dst], y_send.at[q, u], y_recv.at[q, u], to_y)

    def o_copy(src, q, k, half, way, device):
        dst = OUT_PLACE + half * 4 * PARTS + q * PARTS + k
        return copy(src, out.at[dst], o_send.at[way, q, k], o_recv.at[half, q, k], device)

    def spread(src, q, u):
        @pl.when(u < OUT_AT)
        def _():
            y_copy(src, q, u, y).start()

        @pl.when((u >= OUT_AT) & (u < NEAR_AT) & (c == x))
        def _():
            o_copy(src, q, u - OUT_AT, c, 0, to_x).start()

        @pl.when((u >= OUT_AT) & (u < NEAR_AT) & (c != x))
        def _():
            o_copy(src, q, u - OUT_AT, c, 0, to_xc).start()
            o_copy(src, q, u - OUT_AT, c, 1, to_c).start()

        @pl.when(u >= NEAR_AT)
        def _():
            x_copy(src, place(q, u), q, u).start()

    def finish(u):
        @pl.when(z == 0)
        def _():
            rs_arrived(4, u)
            add_unit(final.at[u], [grads.at[0, u], inbox.at[4, u]])

        for here_z in (1, 2):
            @pl.when(z == here_z)
            def _():
                rs_arrived(here_z, u)
                rs_arrived(4, u)
                add_unit(
                    final.at[u], [grads.at[here_z, u], inbox.at[here_z, u], inbox.at[4, u]]
                )

        @pl.when(z == 3)
        def _():
            rs_arrived(3, u)
            add_unit(final.at[u], [grads.at[3, u], inbox.at[3, u]])

        @pl.when(z < 3)
        def _():
            ag_copy(final.at[u], z, u, 0, above).start()

        @pl.when(z > 0)
        def _():
            ag_copy(final.at[u], z, u, 1, below).start()

        spread(final.at[u], z, u)
        stay_copy(u).start()

    def relay(u, far):
        for q in range(4):
            got = out.at[place(q, u)]

            @pl.when(z == q + far)
            def _():
                ag_copy(got, q, u, 0, to_x).wait_recv()

                @pl.when(z < 3)
                def _():
                    ag_copy(got, q, u, 0, above).start()

                spread(got, q, u)

            @pl.when(z == q - far)
            def _():
                ag_copy(got, q, u, 1, to_x).wait_recv()

                @pl.when(z > 0)
                def _():
                    ag_copy(got, q, u, 1, below).start()

                spread(got, q, u)

    def cross(u, far):
        for q in range(4):
            @pl.when((z == q + far) | (z == q - far))
            def _():
                dst = (2 * x + 1 - y) * 12 * PARTS + q * 3 * PARTS + u
                got = out.at[dst]
                y_copy(got, q, u, 1 - y).wait_recv()
                x_copy(got, dst, q, u).start()

    def gain_copy(k, device):
        return copy(gain_in.at[0], gain_in.at[1 + k], g_send.at[k], g_recv.at[k], device)

    def gain_z(k, device):
        return copy(gain_in.at[0], gain_in.at[4 + z], g_send.at[3 + k], g_recv.at[3 + z], device)

    def gain_step(i):
        for k, device in enumerate((to_c, to_x, to_y)):
            @pl.when(i == k)
            def _():
                if k == 0:
                    gain_in[0] = gain[...]
                gain_copy(k, device).start()
                gain_copy(k, device).wait()
                gain_in[0] += gain_in[1 + k]

        @pl.when(i == 3)
        def _():
            for k, device in enumerate(others):
                gain_z(k, device).start()

        @pl.when(i == 5)
        def _():
            for k in range(4):
                @pl.when(z == k)
                def _():
                    gain_in[4 + k] = gain_in[0]

                @pl.when(z != k)
                def _():
                    copy(
                        gain_in.at[0], gain_in.at[4 + k], g_send.at[3], g_recv.at[3 + k], to_x
                    ).wait_recv()

            for k, device in enumerate(others):
                gain_z(k, device).wait_send()
            gain_out[...] = (gain_in[4] + gain_in[5]) + (gain_in[6] + gain_in[7])

    def when_unit(u, last, work):
        @pl.when((u >= 0) & (u < last))
        def _():
            work(u)

    @pl.loop(0, UNITS + 8)
    def _(i):
        when_unit(i - z, UNITS, up)
        when_unit(i - (3 - z), UNITS, down)
        gain_step(i)
        when_unit(i - 3, UNITS, finish)
        for far in (1, 2, 3):
            when_unit(i - 3 - far, UNITS, lambda u: relay(u, far))
        for far in (0, 1, 2, 3):
            when_unit(i - 4 - far, OUT_AT, lambda u: cross(u, far))

    @pl.loop(0, UNITS)
    def _(u):
        stay_copy(u).wait()
        for q in range(4):
            src = grads.at[q, u]

            @pl.when(z != q)
            def _():
                rs_copy(src, q, u, q, to_x).wait_send()

            @pl.when((z < 3) & (q <= z))
            def _():
                ag_copy(src, q, u, 0, to_x).wait_send()

            @pl.when((z > 0) & (q >= z))
            def _():
                ag_copy(src, q, u, 1, to_x).wait_send()

            @pl.when(u < OUT_AT)
            def _():
                y_copy(src, q, u, y).wait_send()

            @pl.when((u >= OUT_AT) & (u < NEAR_AT))
            def _():
                k = u - OUT_AT
                o_copy(src, q, k, c, 0, to_x).wait_send()
                o_copy(src, q, k, 1 - c, 0, to_x).wait_recv()

                @pl.when(c != x)
                def _():
                    o_copy(src, q, k, c, 1, to_x).wait_send()
                    o_copy(src, q, k, c, 0, to_x).wait_recv()

            @pl.when((u < OUT_AT) | (u >= NEAR_AT))
            def _():
                x_copy(src, 0, q, u).wait()


def reduce_grads(grads, gain, ident):
    cols = grads.shape[3]
    shape = jax.ShapeDtypeStruct
    dma = pltpu.SemaphoreType.DMA
    return pl.pallas_call(
        reduce_kernel,
        out_shape=(shape((PLACES, UNIT, cols), BF16), shape(gain.shape, F32)),
        in_specs=[IN_VMEM] * 2,
        out_specs=(ANY, IN_VMEM),
        scratch_shapes=[
            pltpu.VMEM((5, UNITS, UNIT, cols), BF16),
            pltpu.VMEM((UNITS, UNIT, cols), BF16),
            pltpu.VMEM((8,) + gain.shape, F32),
            dma((4, UNITS)),
            dma((5, UNITS)),
            dma((2, 4, UNITS)),
            dma((4, UNITS)),
            dma((4, OUT_AT)),
            dma((4, OUT_AT)),
            dma((4, UNITS)),
            dma((4, UNITS)),
            dma((2, 4, PARTS)),
            dma((2, 4, PARTS)),
            dma((6,)),
            dma((7,)),
            dma((UNITS,)),
        ],
        compiler_params=pltpu.CompilerParams(
            collective_id=ident, has_side_effects=True, vmem_limit_bytes=VMEM_LIMIT
        ),
        name="reduce_grads",
    )(grads, gain)


def rows_kernel(cols_f, cols_h, flags, *refs):
    sources, outs = refs[:4], refs[4:]
    core = flags[0]
    rows = outs[0].shape[0]
    cols = sources[0].shape[-1]
    full = [[sources[2 * i + j][...].reshape(rows, cols) for j in range(2)] for i in range(2)]
    for kind in range(3):
        first = 4 * cols_f + kind * cols_h
        outs[kind][...] = jnp.concatenate(
            [full[i][j][:, first : first + cols_h] for j in range(2) for i in range(2)], 1
        ).astype(F32)
    for kind in range(2):
        pieces = []
        for j in range(2):
            for k in range(2):
                for i in range(2):
                    own = full[i][j][:, kind * cols_f : (kind + 1) * cols_f]
                    first = (2 + kind) * cols_f
                    side = full[i][j][:, first : first + cols_f]
                    pieces.append(jnp.where(core == k, own, side))
        outs[3 + kind][...] = jnp.concatenate(pieces, 1).astype(F32)


def place_rows(summed, c, rows_d, cols_f, cols_h):
    cols = summed.shape[-1]
    steps = rows_d // 48
    shape = jax.ShapeDtypeStruct

    def source(i, j):
        return pl.BlockSpec((PARTS, UNIT, cols), lambda s: ((2 * i + j) * 12 + s, 0, 0))

    def target(width):
        return pl.BlockSpec((48, width), lambda s: (s, 0))

    widths = (4 * cols_h,) * 3 + (8 * cols_f,) * 2
    return pl.pallas_call(
        partial(rows_kernel, cols_f, cols_h),
        grid=(steps,),
        out_shape=tuple(shape((rows_d, width), F32) for width in widths),
        in_specs=[pl.BlockSpec(memory_space=pltpu.SMEM)]
        + [source(i, j) for i in range(2) for j in range(2)],
        out_specs=tuple(target(width) for width in widths),
        compiler_params=pltpu.CompilerParams(vmem_limit_bytes=VMEM_LIMIT),
        name="place_rows",
    )(jnp.reshape(c, (1,)).astype(jnp.int32), summed, summed, summed, summed)


def lanes(rows):
    return lax.broadcasted_iota(jnp.int32, (rows, LANES), 1)


def rotated(block, cosine, sine_signed):
    lane = lanes(block.shape[0])
    turned = jnp.where(
        lane % HEAD_DIM < HEAD_DIM // 2,
        pltpu.roll(block, LANES - HEAD_DIM // 2, 1),
        pltpu.roll(block, HEAD_DIM // 2, 1),
    )
    return block * cosine + turned * sine_signed


def key_spans(pieces, rows):
    reach = WINDOW // rows
    return [
        (max(0, 2 * j - reach) * rows, (2 * j + 2) * rows) for j in range(pieces // 2)
    ]


def seen(first_ref, place_ref, rows, low, high):
    keys = low + lax.broadcasted_iota(jnp.int32, (1, high - low), 1)
    return (keys >= first_ref[rows, :]) & (keys <= place_ref[rows, :])


def forward_kernel(
    spans, width, q_raw, k_raw, v_ref, cos_q, sin_q, cos_k, sin_k, first, place,
    q_out, k_out, ctx_out, lse_out, v_keep,
):
    valid = width - pl.program_id(0) * LANES
    k_rows = k_raw.shape[0]
    keep = lanes(k_rows) < valid
    k_out[...] = jnp.where(keep, rotated(k_raw[...], cos_k[...], sin_k[...]), 0.0).astype(BF16)
    v_keep[...] = jnp.where(keep, v_ref[...], jnp.zeros((), BF16))
    keep_q = lanes(q_raw.shape[0]) < valid
    q_out[...] = jnp.where(keep_q, rotated(q_raw[...], cos_q[...], sin_q[...]), 0.0).astype(BF16)
    rows_j = q_raw.shape[0] // len(spans)
    left = lanes(rows_j) < HEAD_DIM
    zero = jnp.zeros((), BF16)
    for j, (low, high) in enumerate(spans):
        rows = pl.ds(j * rows_j, rows_j)
        visible = seen(first, place, rows, low, high)
        query = q_out[rows, :]
        halves = []
        for side in range(2):
            mine = jnp.where(left if side == 0 else ~left, query, zero)
            scores = lax.dot_general(
                mine, k_out[low:high, :], (((1,), (1,)), ((), ())), preferred_element_type=F32
            )
            scores = jnp.where(visible, scores * 0.125, NEGATIVE)
            top = jnp.max(scores, -1, keepdims=True)
            grown = jnp.exp(scores - top)
            total = jnp.sum(grown, -1, keepdims=True)
            probs = (grown * (1.0 / total)).astype(BF16)
            ctx = jnp.dot(probs, v_keep[low:high, :], preferred_element_type=F32)
            halves.append((ctx, top + jnp.log(total)))
        ctx_out[rows, :] = jnp.where(left, halves[0][0], halves[1][0]).astype(BF16)
        lse_out[rows, :] = jnp.where(left, halves[0][1], halves[1][1])


def lane_block(rows):
    return pl.BlockSpec((rows, LANES), lambda p: (0, p))


def whole(rows, cols):
    return pl.BlockSpec((rows, cols), lambda p: (0, 0))


def attend_forward(q_raw, k_raw, value, tables, limits, pieces):
    q_rows, width = q_raw.shape
    k_rows = k_raw.shape[0]
    spans = key_spans(pieces, k_rows // pieces)
    steps = -(-width // LANES)
    shape = jax.ShapeDtypeStruct
    return pl.pallas_call(
        partial(forward_kernel, spans, width),
        grid=(steps,),
        out_shape=(
            shape((q_rows, width), BF16),
            shape((k_rows, width), BF16),
            shape((q_rows, width), BF16),
            shape((q_rows, width), F32),
        ),
        in_specs=[
            lane_block(q_rows),
            lane_block(k_rows),
            lane_block(k_rows),
            whole(q_rows, LANES),
            whole(q_rows, LANES),
            whole(k_rows, LANES),
            whole(k_rows, LANES),
            whole(q_rows, 1),
            whole(q_rows, 1),
        ],
        out_specs=(
            lane_block(q_rows),
            lane_block(k_rows),
            lane_block(q_rows),
            lane_block(q_rows),
        ),
        scratch_shapes=[pltpu.VMEM((k_rows, LANES), BF16)],
        compiler_params=pltpu.CompilerParams(vmem_limit_bytes=VMEM_LIMIT),
        name="attend_forward",
    )(q_raw, k_raw, value, *tables, *limits)


def backward_kernel(
    spans, width, q_ref, k_ref, v_ref, g_ref, lse, cos_q, sin_q, cos_k, sin_k, first, place,
    dq_out, dk_out, dv_out, k_keep, v_keep,
):
    valid = width - pl.program_id(0) * LANES
    zero = jnp.zeros((), BF16)
    keep = lanes(k_ref.shape[0]) < valid
    k_keep[...] = jnp.where(keep, k_ref[...], zero)
    v_keep[...] = jnp.where(keep, v_ref[...], zero)
    dk_out[...] = jnp.zeros_like(dk_out)
    dv_out[...] = jnp.zeros_like(dv_out)
    rows_j = q_ref.shape[0] // len(spans)
    lane = lanes(rows_j)
    left = (lane < HEAD_DIM) & (lane < valid)
    right = (lane >= HEAD_DIM) & (lane < valid)
    for j, (low, high) in enumerate(spans):
        rows = pl.ds(j * rows_j, rows_j)
        visible = seen(first, place, rows, low, high)
        query, grad = q_ref[rows, :], g_ref[rows, :]
        stats = lse[rows, :]
        halves = []
        for side in range(2):
            mask = left if side == 0 else right
            mine = jnp.where(mask, query, zero)
            grad_mine = jnp.where(mask, grad, zero)
            nt = (((1,), (1,)), ((), ()))
            tn = (((0,), (0,)), ((), ()))
            scores = lax.dot_general(mine, k_keep[low:high, :], nt, preferred_element_type=F32)
            column = side * HEAD_DIM
            log_total = stats[:, column : column + 1]
            probs = jnp.where(visible, jnp.exp(scores * 0.125 - log_total), 0.0)
            grad_probs = lax.dot_general(
                grad_mine, v_keep[low:high, :], nt, preferred_element_type=F32
            )
            mixed = probs * grad_probs
            delta = jnp.sum(mixed, -1, keepdims=True)
            grad_scores = (mixed - probs * delta).astype(BF16)
            halves.append(
                jnp.dot(grad_scores, k_keep[low:high, :], preferred_element_type=F32) * 0.125
            )
            dk_out[low:high, :] += (
                lax.dot_general(grad_scores, mine, tn, preferred_element_type=F32) * 0.125
            )
            dv_out[low:high, :] += lax.dot_general(
                probs.astype(BF16), grad_mine, tn, preferred_element_type=F32
            )
        grad_query = jnp.where(lane < HEAD_DIM, halves[0], halves[1])
        dq_out[rows, :] = rotated(grad_query, cos_q[rows, :], -sin_q[rows, :]).astype(BF16)
    dk_out[...] = rotated(dk_out[...], cos_k[...], -sin_k[...])


def attend_backward(query, key, value, grad, lse, tables, limits, pieces):
    q_rows, width = query.shape
    k_rows = key.shape[0]
    spans = key_spans(pieces, k_rows // pieces)
    steps = -(-width // LANES)
    shape = jax.ShapeDtypeStruct
    return pl.pallas_call(
        partial(backward_kernel, spans, width),
        grid=(steps,),
        out_shape=(
            shape((q_rows, width), BF16),
            shape((k_rows, width), F32),
            shape((k_rows, width), F32),
        ),
        in_specs=[
            lane_block(q_rows),
            lane_block(k_rows),
            lane_block(k_rows),
            lane_block(q_rows),
            lane_block(q_rows),
            whole(q_rows, LANES),
            whole(q_rows, LANES),
            whole(k_rows, LANES),
            whole(k_rows, LANES),
            whole(q_rows, 1),
            whole(q_rows, 1),
        ],
        out_specs=(lane_block(q_rows), lane_block(k_rows), lane_block(k_rows)),
        scratch_shapes=[pltpu.VMEM((k_rows, LANES), BF16)] * 2,
        compiler_params=pltpu.CompilerParams(vmem_limit_bytes=VMEM_LIMIT),
        name="attend_backward",
    )(query, key, value, grad, lse, *tables, *limits)


def norm_back(grad_normed, unit_rows, rms_rows, gain_rows):
    scaled = grad_normed * gain_rows
    return rms_rows * (scaled - unit_rows * jnp.mean(scaled * unit_rows, -1, keepdims=True))


def on_device(
    tokens,
    doc_lengths,
    cotangent,
    attn_gain,
    w_query,
    w_key,
    w_value,
    w_out,
    mlp_gain,
    w_gate,
    w_up,
    w_down,
):
    outer = lax.axis_size("g")
    pieces_z = lax.axis_size("z")
    x, y, c = (lax.axis_index(a) for a in PLANE)
    own = 2 * y + c

    turn_pairs = [
        (i * pieces_z + z, z * pieces_z + i) for i in range(pieces_z) for z in range(pieces_z)
    ]

    def turned(block):
        return lax.ppermute(block, ("y", "c", "z"), turn_pairs)

    def joined(shard):
        if outer == 1:
            return shard
        return lax.all_gather(shard, "g", axis=0, tiled=True)

    w_query, w_key, w_value, w_out = map(joined, (w_query, w_key, w_value, w_out))
    w_gate, w_up, w_down = map(joined, (w_gate, w_up, w_down))
    rows_d = w_query.shape[0]
    model = w_query.shape[1]
    tok_rows = tokens.shape[1]
    pieces = 2 * pieces_z
    seq_len = pieces * tok_rows
    cols_h = model // 4
    cols_f = w_gate.shape[1] // 8

    def head_cols(weight, group):
        return lax.dynamic_slice_in_dim(weight, group * cols_h, cols_h, 1)

    def qkv_cols(group):
        return jnp.concatenate([head_cols(w, group) for w in (w_query, w_key, w_value)], 1)

    def spread(gain):
        padded = jnp.zeros((model,), F32)
        return lax.dynamic_update_slice_in_dim(padded, joined(gain).astype(F32), own * rows_d, 0)

    gains = jnp.pad(jnp.stack([spread(attn_gain), spread(mlp_gain)]), ((0, 6), (0, 0)))
    docs_in = jnp.pad(doc_lengths, ((0, 7), (0, LANES - doc_lengths.shape[1])))
    normed_one, tok_low, cot_low, docs_turned, gains, w_qkv, out_side = front(
        tokens[0],
        cotangent[0],
        docs_in,
        gains,
        qkv_cols(2 * y + x),
        qkv_cols(2 * (1 - y) + x),
        w_out,
        1,
    )
    inputs, upstream = tok_low.astype(F32), cot_low.astype(F32)
    lengths = docs_turned[0, : doc_lengths.shape[1]]
    gain_one, gain_two = gains[0:1], gains[1:2]
    w_qkv = w_qkv.reshape(4 * rows_d, 3 * cols_h)
    w_out_use = jnp.where(c == x, w_out, out_side)

    gate_late, up_late, normed_one = lax.optimization_barrier((w_gate, w_up, normed_one))

    def ff_cols(dest):
        first = (2 * dest + x) * cols_f
        return jnp.concatenate(
            [lax.dynamic_slice_in_dim(w, first, cols_f, 1) for w in (gate_late, up_late)], 1
        )

    ff_own = ff_cols(own)
    ff_c = swap(ff_cols(2 * y + 1 - c), "c")
    ff_y = swap(ff_cols(2 * (1 - y) + c), "y")
    ff_yc = lax.ppermute(
        ff_cols(2 * (1 - y) + 1 - c), ("y", "c"), [(i, 3 - i) for i in range(4)]
    )

    def ordered(a, b, flag):
        return jnp.where(flag == 0, jnp.stack([a, b]), jnp.stack([b, a]))

    ff_near = ordered(ff_own, ff_c, c)
    ff_far = ordered(ff_y, ff_yc, c)
    w_ff = ordered(ff_near, ff_far, y).reshape(4 * rows_d, 2 * cols_f)
    down_use = lax.dynamic_slice_in_dim(w_down, x * cols_f, cols_f, 0)

    place = jnp.arange(seq_len, dtype=jnp.int32)
    docs, offset = layout(lengths, place)
    cosine, sine_table = rope_tables(offset)

    def own_rows(array):
        cols = array.shape[1:]
        split = array.reshape((pieces // 2, 2, tok_rows) + cols)
        return lax.dynamic_index_in_dim(split, c, 1, keepdims=False).reshape(
            (seq_len // 2,) + cols
        )

    def other_rows(array):
        cols = array.shape[1:]
        split = array.reshape((pieces // 2, 2, tok_rows) + cols)
        return lax.dynamic_index_in_dim(split, 1 - c, 1, keepdims=False).reshape(
            (seq_len // 2,) + cols
        )

    tables = (own_rows(cosine), own_rows(sine_table), cosine, sine_table)
    first_key = jnp.maximum(place - offset, place - (WINDOW - 1))
    limits = (own_rows(first_key)[:, None], own_rows(place)[:, None])

    grad_mlp = lax.all_gather((BETA * upstream).astype(BF16), PLANE, axis=0, tiled=True)

    rms_one = lax.rsqrt(jnp.mean(inputs * inputs, -1, keepdims=True) + EPSILON)
    unit_one = inputs * rms_one

    query_raw = dot(own_rows(normed_one), w_qkv[:, :cols_h])
    key_raw = dot(normed_one, w_qkv[:, cols_h : 2 * cols_h])
    value = dot(normed_one, w_qkv[:, 2 * cols_h :]).astype(BF16)
    query, key, context, lse = attend_forward(query_raw, key_raw, value, tables, limits, pieces)

    attn_out = scatter_rows(dot(context, w_out_use), 1, 2)
    hidden_res = inputs + BETA * attn_out
    rms_two = lax.rsqrt(jnp.mean(hidden_res * hidden_res, -1, keepdims=True) + EPSILON)
    unit_two = hidden_res * rms_two
    normed_two = gather_rows((unit_two * gain_two).astype(BF16), 2, 3)

    gate_up = dot(normed_two, w_ff)
    gate, up = gate_up[:, :cols_f], gate_up[:, cols_f:]
    sigmoid_gate = jax.nn.sigmoid(gate)
    silu_gate = gate * sigmoid_gate
    activation = (silu_gate * up).astype(BF16)
    mlp_out = lax.psum_scatter(
        dot(activation, down_use).astype(BF16), PLANE, scatter_dimension=0, tiled=True
    ).astype(F32)
    output = turned((hidden_res + BETA * mlp_out).astype(BF16))[None]

    grad_activation = dot_nt(grad_mlp, down_use)
    grad_up = (grad_activation * silu_gate).astype(BF16)
    grad_gate = (
        grad_activation * up * (sigmoid_gate * (1.0 + gate * (1.0 - sigmoid_gate)))
    ).astype(BF16)
    grad_ff = jnp.concatenate([grad_gate, grad_up], 1)
    grad_normed_two = scatter_rows(dot_nt(grad_ff, w_ff), 2, 4)

    padded = jnp.pad(activation, ((0, 0), (0, 768 - cols_f)))
    grad_down = dot_tn(padded, grad_mlp).astype(BF16)
    grad_ff_side = swap(grad_ff, "c")

    def row_block(normed, y_of):
        return lax.dynamic_slice_in_dim(normed, (2 * y_of + c) * rows_d, rows_d, 1)

    gain_grad_two = jnp.sum(grad_normed_two * unit_two, 0)
    grad_hidden = upstream + norm_back(grad_normed_two, unit_two, rms_two, gain_two)
    grad_attn = gather_rows((BETA * grad_hidden).astype(BF16), 1, 5)
    grad_context = dot_nt(grad_attn, w_out_use).astype(BF16)

    grad_out_part = dot_tn(context, grad_attn).astype(BF16)
    half = model // 2
    keep = lax.dynamic_slice_in_dim(grad_out_part, c * half, half, 1)
    give = lax.dynamic_slice_in_dim(grad_out_part, (1 - c) * half, half, 1)
    grad_out_half = (keep.astype(F32) + swap(give, "c").astype(F32)).astype(BF16)

    grad_query, grad_key, grad_value = attend_backward(
        query, key, value, grad_context, lse, tables, limits, pieces
    )
    grad_kv = jnp.concatenate([grad_key, grad_value], 1)
    grad_kv = own_rows(grad_kv) + swap(other_rows(grad_kv).astype(BF16), "c").astype(F32)
    grad_key = grad_kv[:, :cols_h].astype(BF16)
    grad_value = grad_kv[:, cols_h:].astype(BF16)
    grad_qkv = jnp.concatenate([grad_query, grad_key, grad_value], 1)

    grad_normed_one = scatter_rows(dot_nt(grad_qkv, w_qkv), 1, 6)
    grad_qkv_side = swap(grad_qkv, "c")
    grad_qkv_all = (
        jnp.where(
            c == 0,
            jnp.stack([grad_qkv, grad_qkv_side]),
            jnp.stack([grad_qkv_side, grad_qkv]),
        )
        .reshape(2, pieces // 2, tok_rows, 3 * cols_h)
        .transpose(1, 0, 2, 3)
        .reshape(seq_len, 3 * cols_h)
    )
    def row_grads(y_of):
        block_two, block_one = row_block(normed_two, y_of), row_block(normed_one, y_of)
        return jnp.concatenate(
            [
                dot_tn(block_two, grad_ff).astype(BF16),
                dot_tn(block_two, grad_ff_side).astype(BF16),
                dot_tn(block_one, grad_qkv_all).astype(BF16),
            ],
            1,
        )

    wide = 2 * model
    third = rows_d // 12
    grads = jnp.concatenate(
        [
            row_grads(1 - y).reshape(4, 3 * PARTS, UNIT, wide),
            jnp.pad(
                jnp.concatenate(jnp.split(grad_out_half, 4, 0), 1), ((0, third), (0, 0))
            ).reshape(4, PARTS, UNIT, wide),
            row_grads(y).reshape(4, 3 * PARTS, UNIT, wide),
            jnp.concatenate(jnp.split(grad_down, 2, 0), 1).reshape(4, 2 * PARTS, UNIT, wide),
        ],
        1,
    )
    gain_grad_one = jnp.sum(grad_normed_one * unit_one, 0)
    gain_part = jnp.pad(jnp.stack([gain_grad_one, gain_grad_two]), ((0, 6), (0, 0)))
    summed, gain_grads = reduce_grads(grads, gain_part, 7)
    if outer > 1:
        gain_grads = lax.psum(gain_grads, "g")

    grad_inputs = grad_hidden + norm_back(grad_normed_one, unit_one, rms_one, gain_one)
    grad_tokens = turned(grad_inputs.astype(BF16))[None]

    shard = attn_gain.shape[0]
    first = own * rows_d + lax.axis_index("g") * shard
    gain_grads = lax.dynamic_slice_in_dim(gain_grads, first, shard, 1)

    def finish(grad):
        if outer > 1:
            grad = lax.psum_scatter(grad.astype(BF16), "g", scatter_dimension=0, tiled=True)
        return grad.astype(F32)

    *qkv_all, gate_all, up_all = place_rows(summed, c, rows_d, cols_f, cols_h)
    ff_all = (gate_all, up_all)
    down_sum = summed[DOWN_PLACE:MINE_PLACE].reshape(2, 384, wide)
    out_mine = summed[MINE_PLACE:OUT_PLACE].reshape(4, third, wide)
    out_got = summed[OUT_PLACE:].reshape(2, 4, third, wide)
    down_all = jnp.concatenate(
        [
            part
            for i in range(2)
            for part in (down_sum[i, :, :model], down_sum[i, : cols_f - 384, model:])
        ],
        0,
    )
    out_halves = [
        jnp.where((c == x) & (c == h), out_mine, out_got[h])[:3]
        .reshape(3 * third, 4, half)
        .transpose(1, 0, 2)
        .reshape(rows_d, half)
        for h in range(2)
    ]
    out_all = jnp.concatenate(out_halves, 1)

    return (
        output,
        grad_tokens,
        gain_grads[0],
        finish(qkv_all[0]),
        finish(qkv_all[1]),
        finish(qkv_all[2]),
        finish(out_all),
        gain_grads[1],
        finish(ff_all[0]),
        finish(ff_all[1]),
        finish(down_all),
    )


def solution(mesh):
    seq, fsdp, rep = (mesh.shape[a] for a in ("seq", "fsdp", "rep"))
    inner = Mesh(
        mesh.devices.reshape(seq, rep // 2, 2, fsdp // rep, rep), ("x", "y", "c", "g", "z")
    )
    owners = ("y", "c", "g")
    token_spec = P(owners, ("x", "z"), None)
    placed = (token_spec, P(owners, None), token_spec, P(owners)) + (P(owners, None),) * 4
    placed = placed + (P(owners),) + (P(owners, None),) * 3
    return jax.shard_map(
        on_device,
        mesh=inner,
        in_specs=placed,
        out_specs=(token_spec, token_spec, P(owners))
        + (P(owners, None),) * 4
        + (P(owners),)
        + (P(owners, None),) * 3,
        check_vma=False,
    )
```

```python
from functools import partial
import math

import jax
import jax.numpy as jnp
from jax import lax
from jax.experimental import pallas as pl
from jax.experimental.pallas import tpu as pltpu
from jax.sharding import Mesh, PartitionSpec as P

HEADS = 36
HEAD_DIM = 64
WINDOW = 1024

BETA = 1.4 / math.sqrt(40.0)
EPSILON = 1e-05
NEGATIVE = -1e30

PLANE = ("x", "y", "c")
LANES = 128
VMEM_LIMIT = 60 * 1024 * 1024
F32 = jnp.float32
BF16 = jnp.bfloat16


def dot(left, right):
    return jnp.dot(left, right, preferred_element_type=F32)


def dot_tn(left, right):
    return lax.dot_general(left, right, (((0,), (0,)), ((), ())), preferred_element_type=F32)


def dot_nt(left, right):
    return lax.dot_general(left, right, (((1,), (1,)), ((), ())), preferred_element_type=F32)


def swap(array, axis):
    return lax.ppermute(array, axis, [(0, 1), (1, 0)])


MESH_ID = pl.DeviceIdType.MESH
ANY = pl.BlockSpec(memory_space=pl.ANY)
IN_VMEM = pl.BlockSpec(memory_space=pltpu.VMEM)


def cost(micros):
    return pl.CostEstimate(flops=int(micros * 1.0e9), bytes_accessed=0, transcendentals=0)


def remote(src, dst, sems, index, device):
    return pltpu.make_async_remote_copy(
        src_ref=src,
        dst_ref=dst,
        send_sem=sems[0].at[index],
        recv_sem=sems[1].at[index],
        device_id=device,
        device_id_type=MESH_ID,
    )


def meet(devices):
    barrier = pltpu.get_barrier_semaphore()
    for device in devices:
        pl.semaphore_signal(barrier, inc=1, device_id=device, device_id_type=MESH_ID)
    pl.semaphore_wait(barrier, len(devices))


def gather_steps(cores, block, out, sems, base, here, meanwhile=None):
    x, y, c = (lax.axis_index(a) for a in PLANE)
    slot = c if cores == 2 else 0
    to_x, to_y, to_c = {"x": 1 - x}, {"y": 1 - y}, {"c": 1 - c}
    half = block.shape[0] // 2
    top, low = pl.ds(0, half), pl.ds(half, half)
    own, next_x = 2 * x + y, 2 * (1 - x) + y
    next_y, across = 2 * x + 1 - y, 2 * (1 - x) + 1 - y

    def give(index, rows, device):
        copy = remote(block.at[rows], out.at[own, slot, rows], sems, base + index, device)
        copy.start()
        return copy

    def forward(index, chip, rows, device):
        place = out.at[chip, slot, rows]
        copy = remote(place, place, sems, base + index, device)
        copy.start()
        return copy

    x_top = give(0, top, to_x)
    y_low = give(1, low, to_y)
    x_low = give(2, low, to_x)
    y_top = give(3, top, to_y)
    stay = pltpu.make_async_copy(block, out.at[own, slot], here)
    stay.start()
    sends = [x_top, y_low, x_low, y_top]
    passed = []
    if cores == 2:
        passed.append(give(4, pl.ds(0, 2 * half), to_c))
    if meanwhile is not None:
        meanwhile()
    x_top.wait_recv()
    y_across = forward(5, next_x, top, to_y)
    if cores == 2:
        passed.append(forward(6, next_x, top, to_c))
    y_low.wait_recv()
    x_across = forward(7, next_y, low, to_x)
    if cores == 2:
        passed.append(forward(8, next_y, low, to_c))
    x_low.wait_recv()
    if cores == 2:
        passed.append(forward(9, next_x, low, to_c))
    y_top.wait_recv()
    if cores == 2:
        passed.append(forward(10, next_y, top, to_c))
    y_across.wait_recv()
    if cores == 2:
        passed.append(forward(11, across, top, to_c))
    x_across.wait_recv()
    if cores == 2:
        passed.append(forward(12, across, low, to_c))
    for copy in passed:
        copy.wait_recv()
    stay.wait()
    for copy in sends + [y_across, x_across] + passed:
        copy.wait_send()


def gather_kernel(cores, block, out, send, recv, here):
    x, y, c = (lax.axis_index(a) for a in PLANE)
    meet([{"x": 1 - x}, {"y": 1 - y}] + ([{"c": 1 - c}] if cores == 2 else []))
    gather_steps(cores, block, out, (send, recv), 0, here)


def gather_rows(block, cores, ident):
    rows, cols = block.shape
    out = pl.pallas_call(
        partial(gather_kernel, cores),
        out_shape=jax.ShapeDtypeStruct((4, cores, rows, cols), block.dtype),
        in_specs=[IN_VMEM],
        out_specs=ANY,
        scratch_shapes=[
            pltpu.SemaphoreType.DMA((13,)),
            pltpu.SemaphoreType.DMA((13,)),
            pltpu.SemaphoreType.DMA,
        ],
        compiler_params=pltpu.CompilerParams(
            collective_id=ident, has_side_effects=True, vmem_limit_bytes=VMEM_LIMIT
        ),
        cost_estimate=cost(45),
        name="gather_rows",
    )(block)
    return out.reshape(4 * cores * rows, cols)


def front_kernel(
    docs, tokens, lengths, gains, near, far, w_out,
    rows_all, tok_out, gain_out, qkv_out, side_out, cos_q, sin_q, cos_k, sin_k, first_q,
    tok_in, len_in, gain_in, normed, send, recv, here,
):
    x, y, c = (lax.axis_index(a) for a in PLANE)
    z = lax.axis_index("z")
    to_x, to_y, to_c = {"x": 1 - x}, {"y": 1 - y}, {"c": 1 - c}
    to_yc = {"y": 1 - y, "c": 1 - c}
    own = 2 * y + c
    goal = {"y": z // 2, "c": z % 2, "z": own}
    sems = (send, recv)
    moves = own != z
    barrier = pltpu.get_barrier_semaphore()
    for device in (to_x, to_y, to_c, to_yc):
        pl.semaphore_signal(barrier, inc=1, device_id=device, device_id_type=MESH_ID)

    @pl.when(moves)
    def _():
        pl.semaphore_signal(barrier, inc=1, device_id=goal, device_id_type=MESH_ID)
        pl.semaphore_wait(barrier, 5)

    @pl.when(~moves)
    def _():
        pl.semaphore_wait(barrier, 4)

    gain_copies = [
        remote(gains, gain_in.at[2 * y + c], sems, k, device)
        for k, device in enumerate((to_y, to_c, to_yc))
    ]
    turn_copies = [
        remote(src, dst, sems, 3 + k, goal)
        for k, (src, dst) in enumerate(((lengths, len_in), (tokens, tok_in)))
    ]
    stay_copies = [
        pltpu.make_async_copy(src, dst, here.at[k])
        for k, (src, dst) in enumerate(((lengths, len_in), (tokens, tok_in)))
    ]
    for copy in gain_copies:
        copy.start()
    own_gain = pltpu.make_async_copy(gains, gain_in.at[2 * y + c], here.at[3])
    own_gain.start()

    @pl.when(moves)
    def _():
        for copy in turn_copies:
            copy.start()

    @pl.when(~moves)
    def _():
        for copy in stay_copies:
            copy.start()

    far_copy = remote(far, qkv_out.at[y, c], sems, 6, to_y)
    near_copy = remote(near, qkv_out.at[y, c], sems, 7, to_c)
    side_copy = remote(w_out, side_out, sems, 8, to_c)
    far_copy.start()
    near_copy.start()
    side_copy.start()
    own_near = pltpu.make_async_copy(near, qkv_out.at[y, c], here.at[4])
    own_near.start()

    @pl.when(moves)
    def _():
        for copy in turn_copies:
            copy.wait_recv()

    @pl.when(~moves)
    def _():
        for copy in stay_copies:
            copy.wait()

    own_gain.wait()
    for copy in gain_copies:
        copy.wait_recv()
    gain_out[...] = gain_in[0] + gain_in[1] + gain_in[2] + gain_in[3]
    keep_tok = pltpu.make_async_copy(tok_in, tok_out, here.at[5])
    keep_tok.start()
    step = 16

    @pl.loop(0, tok_in.shape[0] // step)
    def _(i):
        at = pl.ds(i * step, step)
        rows = tok_in[at, :].astype(F32)
        scale = lax.rsqrt(jnp.mean(rows * rows, -1, keepdims=True) + EPSILON)
        normed[at, :] = (rows * scale * gain_out[0:1, :]).astype(BF16)

    step = 64
    piece = tok_in.shape[0]

    def table_rows(place, at, cosine, sine):
        first = jnp.zeros((step, 1), jnp.int32)
        end = jnp.zeros((1, 1), jnp.int32)
        for k in range(docs):
            length = len_in[0:1, k : k + 1]
            end = end + length
            first = first + jnp.where(place >= end, length, 0)
        lane = lax.broadcasted_iota(jnp.int32, (step, LANES), 1) % HEAD_DIM
        half = HEAD_DIM // 2
        frequency = jnp.exp((lane % half).astype(F32) * (-2.0 * math.log(10000.0) / HEAD_DIM))
        angles = (place - first).astype(F32) * frequency
        cosine[at, :] = jnp.cos(angles)
        turned = jnp.sin(angles)
        sine[at, :] = jnp.where(lane < half, -turned, turned)
        return jnp.maximum(first, place - (WINDOW - 1))

    def tables():
        @pl.loop(0, cos_k.shape[0] // step)
        def _(i):
            place = i * step + lax.broadcasted_iota(jnp.int32, (step, 1), 0)
            table_rows(place, pl.ds(i * step, step), cos_k, sin_k)

        @pl.loop(0, cos_q.shape[0] // step)
        def _(i):
            row = i * step + lax.broadcasted_iota(jnp.int32, (step, 1), 0)
            whole_pieces = i // (piece // step)
            place = row + (whole_pieces + c) * piece
            at = pl.ds(i * step, step)
            first_q[at, :] = table_rows(place, at, cos_q, sin_q)

    gather_steps(2, normed, rows_all, sems, 9, here.at[6], tables)
    far_copy.wait_recv()
    from_far = qkv_out.at[1 - y, c]
    pass_copy = remote(from_far, from_far, sems, 22, to_c)
    pass_copy.start()
    keep_tok.wait()
    own_near.wait()
    near_copy.wait_recv()
    side_copy.wait_recv()
    pass_copy.wait_recv()

    @pl.when(moves)
    def _():
        for copy in turn_copies:
            copy.wait_send()

    for copy in gain_copies + [far_copy, near_copy, side_copy, pass_copy]:
        copy.wait_send()


def front(tokens, doc_lengths, gains, near, far, w_out, seq_len, ident):
    rows, cols = tokens.shape
    docs = doc_lengths.shape[1]
    lengths = jnp.pad(doc_lengths, ((0, 7), (0, LANES - docs)))
    shape = jax.ShapeDtypeStruct
    dma = pltpu.SemaphoreType.DMA
    outs = pl.pallas_call(
        partial(front_kernel, docs),
        out_shape=(
            shape((4, 2, rows, cols), BF16),
            shape((rows, cols), BF16),
            shape(gains.shape, F32),
            shape((2, 2) + near.shape, BF16),
            shape(w_out.shape, BF16),
            shape((seq_len // 2, LANES), F32),
            shape((seq_len // 2, LANES), F32),
            shape((seq_len, LANES), F32),
            shape((seq_len, LANES), F32),
            shape((seq_len // 2, 1), jnp.int32),
        ),
        in_specs=[IN_VMEM] * 5 + [ANY],
        out_specs=(ANY, ANY, IN_VMEM, ANY, ANY) + (IN_VMEM,) * 5,
        scratch_shapes=[
            pltpu.VMEM((rows, cols), BF16),
            pltpu.VMEM(lengths.shape, lengths.dtype),
            pltpu.VMEM((4,) + gains.shape, F32),
            pltpu.VMEM((rows, cols), BF16),
            dma((23,)),
            dma((23,)),
            dma((7,)),
        ],
        compiler_params=pltpu.CompilerParams(
            collective_id=ident, has_side_effects=True, vmem_limit_bytes=VMEM_LIMIT
        ),
        cost_estimate=cost(110),
        name="front",
    )(tokens, lengths, gains, near, far, w_out)
    return (outs[0].reshape(8 * rows, cols),) + tuple(outs[1:])


def add_rows(target, first, rows, terms):
    step = 16

    @pl.loop(0, rows // step)
    def _(i):
        at = pl.ds(first + i * step, step)
        total = None
        for ref, ref_first in terms:
            part = ref[pl.ds(ref_first + i * step, step), :].astype(F32)
            total = part if total is None else total + part
        target[at, :] = total.astype(target.dtype)


def scatter_kernel(cores, part, out, side, ready, got_x, got_y, pass_x, pass_y, send, recv):
    x, y, c = (lax.axis_index(a) for a in PLANE)
    slot = c if cores == 2 else 0
    to_x, to_y, to_c = {"x": 1 - x}, {"y": 1 - y}, {"c": 1 - c}
    sems = (send, recv)
    rows = part.shape[2]
    half = rows // 2
    top, low = pl.ds(0, half), pl.ds(half, half)
    own, next_x = 2 * x + y, 2 * (1 - x) + y
    next_y, across = 2 * x + 1 - y, 2 * (1 - x) + 1 - y
    order = [across, next_x, next_y, own]
    meet([to_x, to_y] + ([to_c] if cores == 2 else []))
    from_side = []
    if cores == 2:
        for k, chip in enumerate(order):
            copy = remote(part.at[chip, 1 - c], side.at[k], sems, k, to_c)
            copy.start()
            from_side.append(copy)

    def terms(k, first):
        out_terms = [(part.at[order[k], slot], first)]
        if cores == 2:
            out_terms.append((side.at[k], first))
        return out_terms

    def arrived(k):
        if cores == 2:
            from_side[k].wait_recv()

    def launch(index, src, dst, device):
        copy = remote(src, dst, sems, index, device)
        copy.start()
        return copy

    arrived(0)
    add_rows(ready.at[0], 0, half, terms(0, 0))
    a_x = launch(4, ready.at[0, top], pass_x, to_x)
    add_rows(ready.at[0], half, half, terms(0, half))
    a_y = launch(5, ready.at[0, low], pass_y, to_y)
    arrived(1)
    add_rows(ready.at[1], 0, half, terms(1, 0))
    x_top = launch(6, ready.at[1, top], got_x.at[top], to_x)
    arrived(2)
    add_rows(ready.at[2], half, half, terms(2, half))
    y_low = launch(7, ready.at[2, low], got_y.at[low], to_y)
    a_y.wait_recv()
    add_rows(ready.at[1], half, half, terms(1, half) + [(pass_y, 0)])
    x_low = launch(8, ready.at[1, low], got_x.at[low], to_x)
    a_x.wait_recv()
    add_rows(ready.at[2], 0, half, terms(2, 0) + [(pass_x, 0)])
    y_top = launch(9, ready.at[2, top], got_y.at[top], to_y)
    arrived(3)
    x_top.wait_recv()
    y_low.wait_recv()
    x_low.wait_recv()
    y_top.wait_recv()
    add_rows(out, 0, rows, terms(3, 0) + [(got_x, 0), (got_y, 0)])
    for copy in from_side + [a_x, a_y, x_top, y_low, x_low, y_top]:
        copy.wait_send()


def scatter_rows(partial_rows, cores, ident):
    rows = partial_rows.shape[0] // (4 * cores)
    cols = partial_rows.shape[1]
    part = partial_rows.astype(BF16).reshape(4, cores, rows, cols)
    return pl.pallas_call(
        partial(scatter_kernel, cores),
        out_shape=jax.ShapeDtypeStruct((rows, cols), F32),
        in_specs=[IN_VMEM],
        out_specs=IN_VMEM,
        scratch_shapes=[
            pltpu.VMEM((4, rows if cores == 2 else 16, cols), BF16),
            pltpu.VMEM((3, rows, cols), BF16),
            pltpu.VMEM((rows, cols), BF16),
            pltpu.VMEM((rows, cols), BF16),
            pltpu.VMEM((rows // 2, cols), BF16),
            pltpu.VMEM((rows // 2, cols), BF16),
            pltpu.SemaphoreType.DMA((10,)),
            pltpu.SemaphoreType.DMA((10,)),
        ],
        compiler_params=pltpu.CompilerParams(
            collective_id=ident, has_side_effects=True, vmem_limit_bytes=VMEM_LIMIT
        ),
        cost_estimate=cost(50),
        name="scatter_rows",
    )(part)


PARTS = 3
UNIT = 48 // PARTS
OUT_AT, UNITS = 3 * PARTS, 4 * PARTS


def reduce_kernel(
    grads, gain, out, rows_out, out_out, gain_out,
    inbox, final, gain_in, rs_send, rs_recv, ag_send, ag_recv, y_send, y_recv, x_send, x_recv,
    o_send, o_recv, g_send, g_recv, here,
):
    x, y, c = (lax.axis_index(a) for a in PLANE)
    z = lax.axis_index("z")
    to_x, to_y, to_c = {"x": 1 - x}, {"y": 1 - y}, {"c": 1 - c}
    to_xc = {"x": 1 - x, "c": 1 - c}
    above, below = {"z": z + 1}, {"z": z - 1}
    others = [{"z": (z + k) % 4} for k in (1, 2, 3)]
    meet([to_x, to_y, to_c, to_xc] + others)

    def add_unit(target, sources):
        for first in range(0, UNIT, 16):
            at = pl.ds(first, 16)
            total = sources[0][at, :].astype(F32)
            for ref in sources[1:]:
                total = total + ref[at, :].astype(F32)
            target[at, :] = total.astype(BF16)

    width = grads.shape[3] // 2
    near_half, far_half = pl.ds(0, width), pl.ds(width, width)

    def place(q, u):
        return q * UNITS + u

    def rows_place(owner_x, owner_y, q, u):
        return ((2 * owner_x + owner_y) * 4 + q) * OUT_AT + u

    def copy(src, dst, send, recv, device):
        return pltpu.make_async_remote_copy(
            src_ref=src, dst_ref=dst, send_sem=send, recv_sem=recv,
            device_id=device, device_id_type=MESH_ID,
        )

    def rs_copy(src, q, u, slot, device):
        return copy(src, inbox.at[slot, u], rs_send.at[q, u], rs_recv.at[slot, u], device)

    def rs_arrived(slot, u):
        rs_copy(inbox.at[slot, u], 0, u, slot, to_x).wait_recv()

    def up(u):
        for q in (3, 2, 1):
            @pl.when(z == 0)
            def _():
                rs_copy(grads.at[q, u], q, u, q, above).start()

            @pl.when((z > 0) & (z < q))
            def _():
                rs_arrived(q, u)
                add_unit(inbox.at[q, u], [inbox.at[q, u], grads.at[q, u]])
                rs_copy(inbox.at[q, u], q, u, q, above).start()

    def down(u):
        for q in (0, 1, 2):
            @pl.when(z == 3)
            def _():
                rs_copy(grads.at[q, u], q, u, 4 if q == 2 else q, below).start()

            for here_z in (1, 2):
                if here_z > q:
                    @pl.when(z == here_z)
                    def _():
                        rs_arrived(q, u)
                        add_unit(inbox.at[q, u], [inbox.at[q, u], grads.at[q, u]])
                        slot = 4 if here_z - 1 == q else q
                        rs_copy(inbox.at[q, u], q, u, slot, below).start()

    def ag_copy(src, q, u, way, device):
        return copy(src, out.at[place(q, u)], ag_send.at[way, q, u], ag_recv.at[q, u], device)

    def stay_copy(u):
        return pltpu.make_async_copy(final.at[u], out.at[place(z, u)], here.at[u])

    def x_copy(src, q, u, far):
        dst = rows_place(x, y, q, u) if far == 0 else rows_place(x, 1 - y, q, u)
        return copy(src, rows_out.at[dst], x_send.at[far, q, u], x_recv.at[far, q, u], to_x)

    def y_copy(src, q, u, owner_y):
        dst = rows_out.at[rows_place(x, owner_y, q, u)]
        return copy(src, dst, y_send.at[q, u], y_recv.at[q, u], to_y)

    def o_copy(src, q, k, half, way, device):
        dst = half * 4 * PARTS + q * PARTS + k
        return copy(src, out_out.at[dst], o_send.at[way, q, k], o_recv.at[half, q, k], device)

    def spread(src, q, u):
        @pl.when(u < OUT_AT)
        def _():
            y_copy(src.at[:, far_half], q, u, y).start()
            x_copy(src.at[:, near_half], q, u, 0).start()

        @pl.when((u >= OUT_AT) & (c == x))
        def _():
            o_copy(src, q, u - OUT_AT, c, 0, to_x).start()

        @pl.when((u >= OUT_AT) & (c != x))
        def _():
            o_copy(src, q, u - OUT_AT, c, 0, to_xc).start()
            o_copy(src, q, u - OUT_AT, c, 1, to_c).start()

    def finish(u):
        @pl.when(z == 0)
        def _():
            rs_arrived(4, u)
            add_unit(final.at[u], [grads.at[0, u], inbox.at[4, u]])

        for here_z in (1, 2):
            @pl.when(z == here_z)
            def _():
                rs_arrived(here_z, u)
                rs_arrived(4, u)
                add_unit(
                    final.at[u], [grads.at[here_z, u], inbox.at[here_z, u], inbox.at[4, u]]
                )

        @pl.when(z == 3)
        def _():
            rs_arrived(3, u)
            add_unit(final.at[u], [grads.at[3, u], inbox.at[3, u]])

        @pl.when(z < 3)
        def _():
            ag_copy(final.at[u], z, u, 0, above).start()

        @pl.when(z > 0)
        def _():
            ag_copy(final.at[u], z, u, 1, below).start()

        spread(final.at[u], z, u)
        stay_copy(u).start()

    def relay(u, far):
        for q in range(4):
            got = out.at[place(q, u)]

            @pl.when(z == q + far)
            def _():
                ag_copy(got, q, u, 0, to_x).wait_recv()

                @pl.when(z < 3)
                def _():
                    ag_copy(got, q, u, 0, above).start()

                spread(got, q, u)

            @pl.when(z == q - far)
            def _():
                ag_copy(got, q, u, 1, to_x).wait_recv()

                @pl.when(z > 0)
                def _():
                    ag_copy(got, q, u, 1, below).start()

                spread(got, q, u)

    def cross(u, far):
        for q in range(4):
            @pl.when((z == q + far) | (z == q - far))
            def _():
                got = rows_out.at[rows_place(x, 1 - y, q, u)]
                y_copy(got, q, u, 1 - y).wait_recv()
                x_copy(got, q, u, 1).start()

    def gain_copy(k, device):
        return copy(gain_in.at[0], gain_in.at[1 + k], g_send.at[k], g_recv.at[k], device)

    def gain_z(k, device):
        return copy(gain_in.at[0], gain_in.at[4 + z], g_send.at[3 + k], g_recv.at[3 + z], device)

    def gain_step(i):
        for k, device in enumerate((to_c, to_x, to_y)):
            @pl.when(i == k)
            def _():
                if k == 0:
                    gain_in[0] = gain[...]
                gain_copy(k, device).start()
                gain_copy(k, device).wait()
                gain_in[0] += gain_in[1 + k]

        @pl.when(i == 3)
        def _():
            for k, device in enumerate(others):
                gain_z(k, device).start()

        @pl.when(i == 5)
        def _():
            for k in range(4):
                @pl.when(z == k)
                def _():
                    gain_in[4 + k] = gain_in[0]

                @pl.when(z != k)
                def _():
                    copy(
                        gain_in.at[0], gain_in.at[4 + k], g_send.at[3], g_recv.at[3 + k], to_x
                    ).wait_recv()

            for k, device in enumerate(others):
                gain_z(k, device).wait_send()
            gain_out[...] = (gain_in[4] + gain_in[5]) + (gain_in[6] + gain_in[7])

    def when_unit(u, last, work):
        @pl.when((u >= 0) & (u < last))
        def _():
            work(u)

    @pl.loop(0, UNITS + 8)
    def _(i):
        when_unit(i - z, UNITS, up)
        when_unit(i - (3 - z), UNITS, down)
        gain_step(i)
        when_unit(i - 3, UNITS, finish)
        for far in (1, 2, 3):
            when_unit(i - 3 - far, UNITS, lambda u: relay(u, far))
        for far in (0, 1, 2, 3):
            when_unit(i - 4 - far, OUT_AT, lambda u: cross(u, far))

    @pl.loop(0, UNITS)
    def _(u):
        stay_copy(u).wait()
        for q in range(4):
            src = grads.at[q, u]

            @pl.when(z != q)
            def _():
                rs_copy(src, q, u, q, to_x).wait_send()

            @pl.when((z < 3) & (q <= z))
            def _():
                ag_copy(src, q, u, 0, to_x).wait_send()

            @pl.when((z > 0) & (q >= z))
            def _():
                ag_copy(src, q, u, 1, to_x).wait_send()

            @pl.when(u < OUT_AT)
            def _():
                half = rows_out.at[0]
                y_copy(half, q, u, y).wait_send()
                x_copy(half, q, u, 0).wait()
                x_copy(half, q, u, 1).wait()

            @pl.when(u >= OUT_AT)
            def _():
                k = u - OUT_AT
                o_copy(src, q, k, c, 0, to_x).wait_send()
                o_copy(src, q, k, 1 - c, 0, to_x).wait_recv()

                @pl.when(c != x)
                def _():
                    o_copy(src, q, k, c, 1, to_x).wait_send()
                    o_copy(src, q, k, c, 0, to_x).wait_recv()


def reduce_grads(grads, gain, ident):
    cols = grads.shape[3]
    shape = jax.ShapeDtypeStruct
    dma = pltpu.SemaphoreType.DMA
    return pl.pallas_call(
        reduce_kernel,
        out_shape=(
            shape((4 * UNITS, UNIT, cols), BF16),
            shape((16 * OUT_AT, UNIT, cols // 2), BF16),
            shape((8 * PARTS, UNIT, cols), BF16),
            shape(gain.shape, F32),
        ),
        in_specs=[IN_VMEM] * 2,
        out_specs=(ANY, ANY, ANY, IN_VMEM),
        scratch_shapes=[
            pltpu.VMEM((5, UNITS, UNIT, cols), BF16),
            pltpu.VMEM((UNITS, UNIT, cols), BF16),
            pltpu.VMEM((8,) + gain.shape, F32),
            dma((4, UNITS)),
            dma((5, UNITS)),
            dma((2, 4, UNITS)),
            dma((4, UNITS)),
            dma((4, OUT_AT)),
            dma((4, OUT_AT)),
            dma((2, 4, OUT_AT)),
            dma((2, 4, OUT_AT)),
            dma((2, 4, PARTS)),
            dma((2, 4, PARTS)),
            dma((6,)),
            dma((7,)),
            dma((UNITS,)),
        ],
        compiler_params=pltpu.CompilerParams(
            collective_id=ident, has_side_effects=True, vmem_limit_bytes=VMEM_LIMIT
        ),
        cost_estimate=cost(180),
        name="reduce_grads",
    )(grads, gain)


def rows_kernel(cols_f, cols_h, flags, mine, near, far, near_x, far_x, *refs):
    sources, outs = refs[:4], refs[4:]
    here_x, here_y, core = flags[0], flags[1], flags[2]
    rows, cols = outs[0].shape[0], mine.shape[-1]
    own = mine[...].reshape(rows, cols)
    full = [
        [
            jnp.where(
                (here_x == i) & (here_y == j), own, sources[2 * i + j][...].reshape(rows, cols)
            )
            for j in range(2)
        ]
        for i in range(2)
    ]
    for kind in range(3):
        first = kind * cols_h
        outs[kind][...] = jnp.concatenate(
            [full[i][j][:, first : first + cols_h] for j in range(2) for i in range(2)], 1
        ).astype(F32)
    by_x = [(near[...], far[...]), (near_x[...], far_x[...])]
    full = [
        [
            jnp.where(
                here_x == i,
                jnp.where(here_y == j, *by_x[0]),
                jnp.where(here_y == j, *by_x[1]),
            )
            for j in range(2)
        ]
        for i in range(2)
    ]
    for kind in range(2):
        pieces = []
        for j in range(2):
            for k in range(2):
                for i in range(2):
                    own = full[i][j][:, kind * cols_f : (kind + 1) * cols_f]
                    first = (2 + kind) * cols_f
                    side = full[i][j][:, first : first + cols_f]
                    pieces.append(jnp.where(core == k, own, side))
        outs[3 + kind][...] = jnp.concatenate(pieces, 1).astype(F32)


def place_rows(flags, mine, summed, near, far, near_x, far_x, rows_d, cols_f, cols_h):
    cols = summed.shape[-1]
    shape = jax.ShapeDtypeStruct

    def source(i, j):
        return pl.BlockSpec((PARTS, UNIT, cols), lambda s: ((2 * i + j) * 12 + s, 0, 0))

    def target(width):
        return pl.BlockSpec((48, width), lambda s: (s, 0))

    own = pl.BlockSpec((PARTS, UNIT, cols), lambda s: (s + s // 3, 0, 0))
    ff = pl.BlockSpec((48, 4 * cols_f), lambda s: (s, 0))
    widths = (4 * cols_h,) * 3 + (8 * cols_f,) * 2
    return pl.pallas_call(
        partial(rows_kernel, cols_f, cols_h),
        grid=(rows_d // 48,),
        out_shape=tuple(shape((rows_d, width), F32) for width in widths),
        in_specs=[pl.BlockSpec(memory_space=pltpu.SMEM), own] + [ff] * 4
        + [source(i, j) for i in range(2) for j in range(2)],
        out_specs=tuple(target(width) for width in widths),
        compiler_params=pltpu.CompilerParams(vmem_limit_bytes=VMEM_LIMIT),
        cost_estimate=cost(25),
        name="place_rows",
    )(flags, mine, near, far, near_x, far_x, summed, summed, summed, summed)


def lanes(rows):
    return lax.broadcasted_iota(jnp.int32, (rows, LANES), 1)


def rotated(block, cosine, sine_signed):
    lane = lanes(block.shape[0])
    turned = jnp.where(
        lane % HEAD_DIM < HEAD_DIM // 2,
        pltpu.roll(block, LANES - HEAD_DIM // 2, 1),
        pltpu.roll(block, HEAD_DIM // 2, 1),
    )
    return block * cosine + turned * sine_signed


def key_spans(pieces, rows):
    reach = WINDOW // rows
    return [
        (max(0, 2 * j - reach) * rows, (2 * j + 2) * rows) for j in range(pieces // 2)
    ]


def seen(first_ref, place_ref, rows, low, high):
    keys = low + lax.broadcasted_iota(jnp.int32, (1, high - low), 1)
    return (keys >= first_ref[rows, :]) & (keys <= place_ref[rows, :])


def forward_kernel(
    spans, width, q_raw, k_raw, v_ref, cos_q, sin_q, cos_k, sin_k, first, place,
    q_out, k_out, ctx_out, lse_out, v_keep,
):
    valid = width - pl.program_id(0) * LANES
    k_rows = k_raw.shape[0]
    keep = lanes(k_rows) < valid
    k_out[...] = jnp.where(keep, rotated(k_raw[...], cos_k[...], sin_k[...]), 0.0).astype(BF16)
    v_keep[...] = jnp.where(keep, v_ref[...], jnp.zeros((), BF16))
    keep_q = lanes(q_raw.shape[0]) < valid
    q_out[...] = jnp.where(keep_q, rotated(q_raw[...], cos_q[...], sin_q[...]), 0.0).astype(BF16)
    rows_j = q_raw.shape[0] // len(spans)
    left = lanes(rows_j) < HEAD_DIM
    zero = jnp.zeros((), BF16)
    for j, (low, high) in enumerate(spans):
        rows = pl.ds(j * rows_j, rows_j)
        visible = seen(first, place, rows, low, high)
        query = q_out[rows, :]
        halves = []
        for side in range(2):
            mine = jnp.where(left if side == 0 else ~left, query, zero)
            scores = lax.dot_general(
                mine, k_out[low:high, :], (((1,), (1,)), ((), ())), preferred_element_type=F32
            )
            scores = jnp.where(visible, scores * 0.125, NEGATIVE)
            top = jnp.max(scores, -1, keepdims=True)
            grown = jnp.exp(scores - top)
            total = jnp.sum(grown, -1, keepdims=True)
            probs = (grown * (1.0 / total)).astype(BF16)
            ctx = jnp.dot(probs, v_keep[low:high, :], preferred_element_type=F32)
            halves.append((ctx, top + jnp.log(total)))
        ctx_out[rows, :] = jnp.where(left, halves[0][0], halves[1][0]).astype(BF16)
        lse_out[rows, :] = jnp.where(left, halves[0][1], halves[1][1])


def lane_block(rows):
    return pl.BlockSpec((rows, LANES), lambda p: (0, p))


def whole(rows, cols):
    return pl.BlockSpec((rows, cols), lambda p: (0, 0))


def attend_forward(q_raw, k_raw, value, tables, limits, pieces):
    q_rows, width = q_raw.shape
    k_rows = k_raw.shape[0]
    spans = key_spans(pieces, k_rows // pieces)
    steps = -(-width // LANES)
    shape = jax.ShapeDtypeStruct
    return pl.pallas_call(
        partial(forward_kernel, spans, width),
        grid=(steps,),
        out_shape=(
            shape((q_rows, width), BF16),
            shape((k_rows, width), BF16),
            shape((q_rows, width), BF16),
            shape((q_rows, width), F32),
        ),
        in_specs=[
            lane_block(q_rows),
            lane_block(k_rows),
            lane_block(k_rows),
            whole(q_rows, LANES),
            whole(q_rows, LANES),
            whole(k_rows, LANES),
            whole(k_rows, LANES),
            whole(q_rows, 1),
            whole(q_rows, 1),
        ],
        out_specs=(
            lane_block(q_rows),
            lane_block(k_rows),
            lane_block(q_rows),
            lane_block(q_rows),
        ),
        scratch_shapes=[pltpu.VMEM((k_rows, LANES), BF16)],
        compiler_params=pltpu.CompilerParams(vmem_limit_bytes=VMEM_LIMIT),
        cost_estimate=cost(43),
        name="attend_forward",
    )(q_raw, k_raw, value, *tables, *limits)


def backward_kernel(
    spans, width, q_ref, k_ref, v_ref, g_ref, lse, cos_q, sin_q, cos_k, sin_k, first, place,
    dq_out, dk_done, dv_done, k_keep, v_keep, dk_out, dv_out, give, got, send, recv,
):
    step = pl.program_id(0)
    c = lax.axis_index("c")
    rows_j = q_ref.shape[0] // len(spans)
    pair = [("dk", dk_out, dk_done), ("dv", dv_out, dv_done)]

    def to_side(at):
        return pltpu.make_async_remote_copy(
            src_ref=give.at[at],
            dst_ref=got.at[at],
            send_sem=send.at[at],
            recv_sem=recv.at[at],
            device_id={"c": 1 - c},
            device_id_type=MESH_ID,
        )

    @pl.when(step == 0)
    def _():
        meet([{"c": 1 - c}])

    @pl.when(step > 0)
    def _():
        to_side(step - 1).wait_recv()
        for k, (_, whole_sum, done) in enumerate(pair):
            for j in range(len(spans)):
                rows = pl.ds(j * rows_j, rows_j)
                own = whole_sum[pl.ds(pl.multiple_of((2 * j + c) * rows_j, rows_j), rows_j), :]
                done[rows, :] = (own + got[step - 1, k, rows, :].astype(F32)).astype(BF16)

    @pl.when(step < pl.num_programs(0) - 1)
    def _():
        backward_step(
            spans, width, q_ref, k_ref, v_ref, g_ref, lse, cos_q, sin_q, cos_k, sin_k,
            first, place, dq_out, dk_out, dv_out, k_keep, v_keep,
        )
        for k, (_, whole_sum, _) in enumerate(pair):
            for j in range(len(spans)):
                other = pl.ds(pl.multiple_of((2 * j + 1 - c) * rows_j, rows_j), rows_j)
                give[step, k, pl.ds(j * rows_j, rows_j), :] = whole_sum[other, :].astype(BF16)
        to_side(step).start()

    @pl.when(step == pl.num_programs(0) - 1)
    def _():
        for k in range(give.shape[0]):
            to_side(k).wait_send()


def backward_step(
    spans, width, q_ref, k_ref, v_ref, g_ref, lse, cos_q, sin_q, cos_k, sin_k, first, place,
    dq_out, dk_out, dv_out, k_keep, v_keep,
):
    valid = width - pl.program_id(0) * LANES
    zero = jnp.zeros((), BF16)
    keep = lanes(k_ref.shape[0]) < valid
    k_keep[...] = jnp.where(keep, k_ref[...], zero)
    v_keep[...] = jnp.where(keep, v_ref[...], zero)
    dk_out[...] = jnp.zeros_like(dk_out)
    dv_out[...] = jnp.zeros_like(dv_out)
    rows_j = q_ref.shape[0] // len(spans)
    lane = lanes(rows_j)
    left = (lane < HEAD_DIM) & (lane < valid)
    right = (lane >= HEAD_DIM) & (lane < valid)
    for j, (low, high) in enumerate(spans):
        rows = pl.ds(j * rows_j, rows_j)
        visible = seen(first, place, rows, low, high)
        query, grad = q_ref[rows, :], g_ref[rows, :]
        stats = lse[rows, :]
        halves = []
        for side in range(2):
            mask = left if side == 0 else right
            mine = jnp.where(mask, query, zero)
            grad_mine = jnp.where(mask, grad, zero)
            nt = (((1,), (1,)), ((), ()))
            tn = (((0,), (0,)), ((), ()))
            scores = lax.dot_general(mine, k_keep[low:high, :], nt, preferred_element_type=F32)
            column = side * HEAD_DIM
            log_total = stats[:, column : column + 1]
            probs = jnp.where(visible, jnp.exp(scores * 0.125 - log_total), 0.0)
            grad_probs = lax.dot_general(
                grad_mine, v_keep[low:high, :], nt, preferred_element_type=F32
            )
            mixed = probs * grad_probs
            delta = jnp.sum(mixed, -1, keepdims=True)
            grad_scores = (mixed - probs * delta).astype(BF16)
            halves.append(
                jnp.dot(grad_scores, k_keep[low:high, :], preferred_element_type=F32) * 0.125
            )
            dk_out[low:high, :] += (
                lax.dot_general(grad_scores, mine, tn, preferred_element_type=F32) * 0.125
            )
            dv_out[low:high, :] += lax.dot_general(
                probs.astype(BF16), grad_mine, tn, preferred_element_type=F32
            )
        grad_query = jnp.where(lane < HEAD_DIM, halves[0], halves[1])
        dq_out[rows, :] = rotated(grad_query, cos_q[rows, :], -sin_q[rows, :]).astype(BF16)
    dk_out[...] = rotated(dk_out[...], cos_k[...], -sin_k[...])


def attend_backward(query, key, value, grad, lse, tables, limits, pieces, ident):
    q_rows, width = query.shape
    k_rows = key.shape[0]
    spans = key_spans(pieces, k_rows // pieces)
    steps = -(-width // LANES)
    shape = jax.ShapeDtypeStruct

    def this(rows):
        return pl.BlockSpec((rows, LANES), lambda p: (0, jnp.minimum(p, steps - 1)))

    def last(rows):
        return pl.BlockSpec((rows, LANES), lambda p: (0, jnp.maximum(p - 1, 0)))

    return pl.pallas_call(
        partial(backward_kernel, spans, width),
        grid=(steps + 1,),
        out_shape=(shape((q_rows, width), BF16),) * 3,
        in_specs=[
            this(q_rows),
            this(k_rows),
            this(k_rows),
            this(q_rows),
            this(q_rows),
            whole(q_rows, LANES),
            whole(q_rows, LANES),
            whole(k_rows, LANES),
            whole(k_rows, LANES),
            whole(q_rows, 1),
            whole(q_rows, 1),
        ],
        out_specs=(this(q_rows), last(q_rows), last(q_rows)),
        scratch_shapes=[pltpu.VMEM((k_rows, LANES), BF16)] * 2
        + [pltpu.VMEM((k_rows, LANES), F32)] * 2
        + [pltpu.VMEM((steps, 2, q_rows, LANES), BF16)] * 2
        + [pltpu.SemaphoreType.DMA((steps,))] * 2,
        compiler_params=pltpu.CompilerParams(
            collective_id=ident, has_side_effects=True, vmem_limit_bytes=VMEM_LIMIT
        ),
        cost_estimate=cost(57),
        name="attend_backward",
    )(query, key, value, grad, lse, *tables, *limits)


def norm_back(grad_normed, unit_rows, rms_rows, gain_rows):
    scaled = grad_normed * gain_rows
    return rms_rows * (scaled - unit_rows * jnp.mean(scaled * unit_rows, -1, keepdims=True))


def on_device(
    tokens,
    doc_lengths,
    cotangent,
    attn_gain,
    w_query,
    w_key,
    w_value,
    w_out,
    mlp_gain,
    w_gate,
    w_up,
    w_down,
):
    outer = lax.axis_size("g")
    pieces_z = lax.axis_size("z")
    x, y, c = (lax.axis_index(a) for a in PLANE)
    own = 2 * y + c

    turn_pairs = [
        (i * pieces_z + z, z * pieces_z + i) for i in range(pieces_z) for z in range(pieces_z)
    ]

    def turned(block):
        return lax.ppermute(block, ("y", "c", "z"), turn_pairs)

    def joined(shard):
        if outer == 1:
            return shard
        return lax.all_gather(shard, "g", axis=0, tiled=True)

    w_query, w_key, w_value, w_out = map(joined, (w_query, w_key, w_value, w_out))
    w_gate, w_up, w_down = map(joined, (w_gate, w_up, w_down))
    rows_d = w_query.shape[0]
    model = w_query.shape[1]
    tok_rows = tokens.shape[1]
    pieces = 2 * pieces_z
    seq_len = pieces * tok_rows
    cols_h = model // 4
    cols_f = w_gate.shape[1] // 8

    def head_cols(weight, group):
        return lax.dynamic_slice_in_dim(weight, group * cols_h, cols_h, 1)

    def qkv_cols(group):
        return jnp.concatenate([head_cols(w, group) for w in (w_query, w_key, w_value)], 1)

    def spread(gain):
        padded = jnp.zeros((model,), F32)
        return lax.dynamic_update_slice_in_dim(padded, joined(gain).astype(F32), own * rows_d, 0)

    gains = jnp.pad(jnp.stack([spread(attn_gain), spread(mlp_gain)]), ((0, 6), (0, 0)))
    normed_one, tok_low, gains, w_qkv, out_side, *tables, first_query = front(
        tokens[0],
        doc_lengths,
        gains,
        qkv_cols(2 * y + x),
        qkv_cols(2 * (1 - y) + x),
        w_out,
        seq_len,
        1,
    )
    cot_late, _ = lax.optimization_barrier((cotangent[0], tok_low))
    cot_low = turned(cot_late)
    inputs, upstream = tok_low.astype(F32), cot_low.astype(F32)
    gain_one, gain_two = gains[0:1], gains[1:2]
    w_qkv = w_qkv.reshape(4 * rows_d, 3 * cols_h)
    w_out_use = jnp.where(c == x, w_out, out_side)

    gate_late, up_late, normed_one = lax.optimization_barrier((w_gate, w_up, normed_one))

    def ff_cols(dest):
        first = (2 * dest + x) * cols_f
        return jnp.concatenate(
            [lax.dynamic_slice_in_dim(w, first, cols_f, 1) for w in (gate_late, up_late)], 1
        )

    ff_own = ff_cols(own)
    ff_c = swap(ff_cols(2 * y + 1 - c), "c")
    ff_y = swap(ff_cols(2 * (1 - y) + c), "y")
    ff_yc = lax.ppermute(
        ff_cols(2 * (1 - y) + 1 - c), ("y", "c"), [(i, 3 - i) for i in range(4)]
    )

    def ordered(a, b, flag):
        return jnp.where(flag == 0, jnp.stack([a, b]), jnp.stack([b, a]))

    ff_near = ordered(ff_own, ff_c, c)
    ff_far = ordered(ff_y, ff_yc, c)
    w_ff = ordered(ff_near, ff_far, y).reshape(4 * rows_d, 2 * cols_f)
    down_use = lax.dynamic_slice_in_dim(w_down, x * cols_f, cols_f, 0)

    def own_rows(array):
        cols = array.shape[1:]
        split = array.reshape((pieces // 2, 2, tok_rows) + cols)
        return lax.dynamic_index_in_dim(split, c, 1, keepdims=False).reshape(
            (seq_len // 2,) + cols
        )

    place = own_rows(jnp.arange(seq_len, dtype=jnp.int32))
    limits = (first_query, place[:, None])

    grad_mlp = lax.all_gather((BETA * upstream).astype(BF16), PLANE, axis=0, tiled=True)

    rms_one = lax.rsqrt(jnp.mean(inputs * inputs, -1, keepdims=True) + EPSILON)
    unit_one = inputs * rms_one

    query_raw = dot(own_rows(normed_one), w_qkv[:, :cols_h])
    key_raw = dot(normed_one, w_qkv[:, cols_h : 2 * cols_h])
    value = dot(normed_one, w_qkv[:, 2 * cols_h :]).astype(BF16)
    query, key, context, lse = attend_forward(query_raw, key_raw, value, tables, limits, pieces)

    attn_out = scatter_rows(dot(context, w_out_use), 1, 2)
    hidden_res = inputs + BETA * attn_out
    rms_two = lax.rsqrt(jnp.mean(hidden_res * hidden_res, -1, keepdims=True) + EPSILON)
    unit_two = hidden_res * rms_two
    normed_two = gather_rows((unit_two * gain_two).astype(BF16), 2, 3)

    gate_up = dot(normed_two, w_ff)
    gate, up = gate_up[:, :cols_f], gate_up[:, cols_f:]
    sigmoid_gate = jax.nn.sigmoid(gate)
    silu_gate = gate * sigmoid_gate
    activation = (silu_gate * up).astype(BF16)
    mlp_out = lax.psum_scatter(
        dot(activation, down_use).astype(BF16), PLANE, scatter_dimension=0, tiled=True
    ).astype(F32)
    output = turned((hidden_res + BETA * mlp_out).astype(BF16))[None]

    grad_activation = dot_nt(grad_mlp, down_use)
    grad_up = (grad_activation * silu_gate).astype(BF16)
    grad_gate = (
        grad_activation * up * (sigmoid_gate * (1.0 + gate * (1.0 - sigmoid_gate)))
    ).astype(BF16)
    grad_ff = jnp.concatenate([grad_gate, grad_up], 1)
    padded = jnp.pad(activation, ((0, 0), (0, 768 - cols_f)))
    grad_ff_side = swap(grad_ff, "c")

    def row_block(normed, y_of):
        return lax.dynamic_slice_in_dim(normed, (2 * y_of + c) * rows_d, rows_d, 1)

    def ff_rows(y_of):
        block = row_block(normed_two, y_of)
        return jnp.concatenate(
            [dot_tn(block, grad_ff).astype(BF16), dot_tn(block, grad_ff_side).astype(BF16)], 1
        )

    grad_down = dot_tn(padded, grad_mlp).astype(BF16)
    ff_near, ff_far = ff_rows(y), ff_rows(1 - y)
    back_part = dot_nt(grad_ff, w_ff).astype(BF16)
    back_part, grad_down, ff_near, ff_far = lax.optimization_barrier(
        (back_part, grad_down, ff_near, ff_far)
    )

    def sum_z(grad):
        return lax.psum_scatter(grad, "z", scatter_dimension=0, tiled=True)

    def gather_z(part, after):
        part = lax.optimization_barrier((part, after))[0]
        return lax.all_gather(part, "z", axis=0, tiled=True)

    ff_far, ff_near, grad_down = sum_z(ff_far), sum_z(ff_near), sum_z(grad_down)
    grad_normed_two = scatter_rows(back_part, 2, 4)

    gain_grad_two = jnp.sum(grad_normed_two * unit_two, 0)
    grad_hidden = upstream + norm_back(grad_normed_two, unit_two, rms_two, gain_two)
    grad_attn = gather_rows((BETA * grad_hidden).astype(BF16), 1, 5)
    grad_context = dot_nt(grad_attn, w_out_use).astype(BF16)

    grad_out_part = dot_tn(context, grad_attn).astype(BF16)
    half = model // 2
    keep = lax.dynamic_slice_in_dim(grad_out_part, c * half, half, 1)
    give = lax.dynamic_slice_in_dim(grad_out_part, (1 - c) * half, half, 1)
    grad_out_half = (keep.astype(F32) + swap(give, "c").astype(F32)).astype(BF16)

    grad_query, grad_key, grad_value = attend_backward(
        query, key, value, grad_context, lse, tables, limits, pieces, 8
    )
    ff_far = swap(gather_z(ff_far, grad_query), "y")
    ff_near = gather_z(ff_near, grad_query)
    grad_qkv = jnp.concatenate([grad_query, grad_key, grad_value], 1)

    grad_normed_one = scatter_rows(dot_nt(grad_qkv, w_qkv), 1, 6)
    grad_qkv_side = swap(grad_qkv, "c")
    grad_qkv_all = (
        jnp.where(
            c == 0,
            jnp.stack([grad_qkv, grad_qkv_side]),
            jnp.stack([grad_qkv_side, grad_qkv]),
        )
        .reshape(2, pieces // 2, tok_rows, 3 * cols_h)
        .transpose(1, 0, 2, 3)
        .reshape(seq_len, 3 * cols_h)
    )
    grad_down = gather_z(grad_down, grad_normed_one)
    third = rows_d // 12
    width = -(-3 * cols_h // LANES) * LANES

    def qkv_rows(y_of):
        part = dot_tn(row_block(normed_one, y_of), grad_qkv_all).astype(BF16)
        return jnp.pad(part, ((0, 0), (0, width - 3 * cols_h)))

    grads = jnp.concatenate(
        [
            jnp.concatenate([qkv_rows(y), qkv_rows(1 - y)], 1).reshape(
                4, OUT_AT, UNIT, 2 * width
            ),
            jnp.pad(
                jnp.concatenate(jnp.split(grad_out_half, 3, 0), 1),
                ((0, 0), (0, 2 * width - 3 * half)),
            ).reshape(4, PARTS, UNIT, 2 * width),
        ],
        1,
    )
    gain_grad_one = jnp.sum(grad_normed_one * unit_one, 0)
    gain_part = jnp.pad(jnp.stack([gain_grad_one, gain_grad_two]), ((0, 6), (0, 0)))
    mine, summed, out_got, gain_grads = reduce_grads(grads, gain_part, 7)
    if outer > 1:
        gain_grads = lax.psum(gain_grads, "g")

    grad_inputs = grad_hidden + norm_back(grad_normed_one, unit_one, rms_one, gain_one)
    grad_tokens = turned(grad_inputs.astype(BF16))[None]

    shard = attn_gain.shape[0]
    first = own * rows_d + lax.axis_index("g") * shard
    gain_grads = lax.dynamic_slice_in_dim(gain_grads, first, shard, 1)

    def finish(grad):
        if outer > 1:
            grad = lax.psum_scatter(grad.astype(BF16), "g", scatter_dimension=0, tiled=True)
        return grad.astype(F32)

    flags = jnp.stack([x, y, c]).astype(jnp.int32)
    *qkv_all, gate_all, up_all = place_rows(
        flags, mine, summed, ff_near, ff_far, swap(ff_near, "x"), swap(ff_far, "x"),
        rows_d, cols_f, cols_h,
    )
    ff_all = (gate_all, up_all)
    down_own, down_side = grad_down[:cols_f], swap(grad_down, "x")[:cols_f]
    down_all = jnp.concatenate(
        [jnp.where(x == 0, down_own, down_side), jnp.where(x == 0, down_side, down_own)], 0
    )
    out_mine = mine.reshape(4, UNITS, UNIT, 2 * width)[:, OUT_AT:, :, : 3 * half]
    out_mine = out_mine.reshape(4 * third, 3 * half)
    out_got = out_got[:, :, : 3 * half].reshape(2, 4 * third, 3 * half)
    out_halves = [
        jnp.concatenate(
            jnp.split(jnp.where((c == x) & (c == h), out_mine, out_got[h]), 3, 1), 0
        )
        for h in range(2)
    ]
    out_all = jnp.concatenate(out_halves, 1)

    return (
        output,
        grad_tokens,
        gain_grads[0],
        finish(qkv_all[0]),
        finish(qkv_all[1]),
        finish(qkv_all[2]),
        finish(out_all),
        gain_grads[1],
        finish(ff_all[0]),
        finish(ff_all[1]),
        finish(down_all),
    )


def solution(mesh):
    seq, fsdp, rep = (mesh.shape[a] for a in ("seq", "fsdp", "rep"))
    inner = Mesh(
        mesh.devices.reshape(seq, rep // 2, 2, fsdp // rep, rep), ("x", "y", "c", "g", "z")
    )
    owners = ("y", "c", "g")
    token_spec = P(owners, ("x", "z"), None)
    placed = (token_spec, P(owners, None), token_spec, P(owners)) + (P(owners, None),) * 4
    placed = placed + (P(owners),) + (P(owners, None),) * 3
    return jax.shard_map(
        on_device,
        mesh=inner,
        in_specs=placed,
        out_specs=(token_spec, token_spec, P(owners))
        + (P(owners, None),) * 4
        + (P(owners),)
        + (P(owners, None),) * 3,
        check_vma=False,
    )
```

```python
from functools import partial
import math

import jax
import jax.numpy as jnp
from jax import lax
from jax.experimental import pallas as pl
from jax.experimental.pallas import tpu as pltpu
from jax.sharding import Mesh, PartitionSpec as P

HEADS = 36
HEAD_DIM = 64
WINDOW = 1024

BETA = 1.4 / math.sqrt(40.0)
EPSILON = 1e-05
NEGATIVE = -1e30

PLANE = ("x", "y", "c")
LANES = 128
VMEM_LIMIT = 60 * 1024 * 1024
F32 = jnp.float32
BF16 = jnp.bfloat16


def dot(left, right):
    return jnp.dot(left, right, preferred_element_type=F32)


def dot_tn(left, right):
    return lax.dot_general(left, right, (((0,), (0,)), ((), ())), preferred_element_type=F32)


def dot_nt(left, right):
    return lax.dot_general(left, right, (((1,), (1,)), ((), ())), preferred_element_type=F32)


def swap(array, axis):
    return lax.ppermute(array, axis, [(0, 1), (1, 0)])


MESH_ID = pl.DeviceIdType.MESH
ANY = pl.BlockSpec(memory_space=pl.ANY)
IN_VMEM = pl.BlockSpec(memory_space=pltpu.VMEM)


def cost(micros):
    return pl.CostEstimate(flops=int(micros * 1.0e9), bytes_accessed=0, transcendentals=0)


def remote(src, dst, sems, index, device):
    return pltpu.make_async_remote_copy(
        src_ref=src,
        dst_ref=dst,
        send_sem=sems[0].at[index],
        recv_sem=sems[1].at[index],
        device_id=device,
        device_id_type=MESH_ID,
    )


def meet(devices):
    barrier = pltpu.get_barrier_semaphore()
    for device in devices:
        pl.semaphore_signal(barrier, inc=1, device_id=device, device_id_type=MESH_ID)
    pl.semaphore_wait(barrier, len(devices))


def gather_steps(cores, block, out, sems, base, here, meanwhile=None):
    x, y, c = (lax.axis_index(a) for a in PLANE)
    slot = c if cores == 2 else 0
    to_x, to_y, to_c = {"x": 1 - x}, {"y": 1 - y}, {"c": 1 - c}
    half = block.shape[0] // 2
    top, low = pl.ds(0, half), pl.ds(half, half)
    own, next_x = 2 * x + y, 2 * (1 - x) + y
    next_y, across = 2 * x + 1 - y, 2 * (1 - x) + 1 - y

    def give(index, rows, device):
        copy = remote(block.at[rows], out.at[own, slot, rows], sems, base + index, device)
        copy.start()
        return copy

    def forward(index, chip, rows, device):
        place = out.at[chip, slot, rows]
        copy = remote(place, place, sems, base + index, device)
        copy.start()
        return copy

    x_top = give(0, top, to_x)
    y_low = give(1, low, to_y)
    x_low = give(2, low, to_x)
    y_top = give(3, top, to_y)
    stay = pltpu.make_async_copy(block, out.at[own, slot], here)
    stay.start()
    sends = [x_top, y_low, x_low, y_top]
    passed = []
    if cores == 2:
        passed.append(give(4, pl.ds(0, 2 * half), to_c))
    if meanwhile is not None:
        meanwhile()
    x_top.wait_recv()
    y_across = forward(5, next_x, top, to_y)
    if cores == 2:
        passed.append(forward(6, next_x, top, to_c))
    y_low.wait_recv()
    x_across = forward(7, next_y, low, to_x)
    if cores == 2:
        passed.append(forward(8, next_y, low, to_c))
    x_low.wait_recv()
    if cores == 2:
        passed.append(forward(9, next_x, low, to_c))
    y_top.wait_recv()
    if cores == 2:
        passed.append(forward(10, next_y, top, to_c))
    y_across.wait_recv()
    if cores == 2:
        passed.append(forward(11, across, top, to_c))
    x_across.wait_recv()
    if cores == 2:
        passed.append(forward(12, across, low, to_c))
    for copy in passed:
        copy.wait_recv()
    stay.wait()
    for copy in sends + [y_across, x_across] + passed:
        copy.wait_send()


def gather_kernel(cores, block, out, send, recv, here):
    x, y, c = (lax.axis_index(a) for a in PLANE)
    meet([{"x": 1 - x}, {"y": 1 - y}] + ([{"c": 1 - c}] if cores == 2 else []))
    gather_steps(cores, block, out, (send, recv), 0, here)


def gather_rows(block, cores, ident):
    rows, cols = block.shape
    out = pl.pallas_call(
        partial(gather_kernel, cores),
        out_shape=jax.ShapeDtypeStruct((4, cores, rows, cols), block.dtype),
        in_specs=[IN_VMEM],
        out_specs=ANY,
        scratch_shapes=[
            pltpu.SemaphoreType.DMA((13,)),
            pltpu.SemaphoreType.DMA((13,)),
            pltpu.SemaphoreType.DMA,
        ],
        compiler_params=pltpu.CompilerParams(
            collective_id=ident, has_side_effects=True, vmem_limit_bytes=VMEM_LIMIT
        ),
        cost_estimate=cost(45),
        name="gather_rows",
    )(block)
    return out.reshape(4 * cores * rows, cols)


def front_kernel(
    docs, tokens, lengths, gains, near, far, w_out,
    rows_all, tok_out, gain_out, qkv_out, side_out, cos_q, sin_q, cos_k, sin_k, first_q,
    tok_in, len_in, gain_in, normed, send, recv, here,
):
    x, y, c = (lax.axis_index(a) for a in PLANE)
    z = lax.axis_index("z")
    to_x, to_y, to_c = {"x": 1 - x}, {"y": 1 - y}, {"c": 1 - c}
    to_yc = {"y": 1 - y, "c": 1 - c}
    own = 2 * y + c
    goal = {"y": z // 2, "c": z % 2, "z": own}
    sems = (send, recv)
    moves = own != z
    barrier = pltpu.get_barrier_semaphore()
    for device in (to_x, to_y, to_c, to_yc):
        pl.semaphore_signal(barrier, inc=1, device_id=device, device_id_type=MESH_ID)

    @pl.when(moves)
    def _():
        pl.semaphore_signal(barrier, inc=1, device_id=goal, device_id_type=MESH_ID)
        pl.semaphore_wait(barrier, 5)

    @pl.when(~moves)
    def _():
        pl.semaphore_wait(barrier, 4)

    gain_copies = [
        remote(gains, gain_in.at[2 * y + c], sems, k, device)
        for k, device in enumerate((to_y, to_c, to_yc))
    ]
    turn_copies = [
        remote(src, dst, sems, 3 + k, goal)
        for k, (src, dst) in enumerate(((lengths, len_in), (tokens, tok_in)))
    ]
    stay_copies = [
        pltpu.make_async_copy(src, dst, here.at[k])
        for k, (src, dst) in enumerate(((lengths, len_in), (tokens, tok_in)))
    ]
    for copy in gain_copies:
        copy.start()
    own_gain = pltpu.make_async_copy(gains, gain_in.at[2 * y + c], here.at[3])
    own_gain.start()

    @pl.when(moves)
    def _():
        for copy in turn_copies:
            copy.start()

    @pl.when(~moves)
    def _():
        for copy in stay_copies:
            copy.start()

    far_copy = remote(far, qkv_out.at[y, c], sems, 6, to_y)
    near_copy = remote(near, qkv_out.at[y, c], sems, 7, to_c)
    side_copy = remote(w_out, side_out, sems, 8, to_c)
    far_copy.start()
    near_copy.start()
    side_copy.start()
    own_near = pltpu.make_async_copy(near, qkv_out.at[y, c], here.at[4])
    own_near.start()

    @pl.when(moves)
    def _():
        for copy in turn_copies:
            copy.wait_recv()

    @pl.when(~moves)
    def _():
        for copy in stay_copies:
            copy.wait()

    own_gain.wait()
    for copy in gain_copies:
        copy.wait_recv()
    gain_out[...] = gain_in[0] + gain_in[1] + gain_in[2] + gain_in[3]
    keep_tok = pltpu.make_async_copy(tok_in, tok_out, here.at[5])
    keep_tok.start()
    step = 16

    @pl.loop(0, tok_in.shape[0] // step)
    def _(i):
        at = pl.ds(i * step, step)
        rows = tok_in[at, :].astype(F32)
        scale = lax.rsqrt(jnp.mean(rows * rows, -1, keepdims=True) + EPSILON)
        normed[at, :] = (rows * scale * gain_out[0:1, :]).astype(BF16)

    step = 64
    piece = tok_in.shape[0]

    def table_rows(place, at, cosine, sine):
        first = jnp.zeros((step, 1), jnp.int32)
        end = jnp.zeros((1, 1), jnp.int32)
        for k in range(docs):
            length = len_in[0:1, k : k + 1]
            end = end + length
            first = first + jnp.where(place >= end, length, 0)
        lane = lax.broadcasted_iota(jnp.int32, (step, LANES), 1) % HEAD_DIM
        half = HEAD_DIM // 2
        frequency = jnp.exp((lane % half).astype(F32) * (-2.0 * math.log(10000.0) / HEAD_DIM))
        angles = (place - first).astype(F32) * frequency
        cosine[at, :] = jnp.cos(angles)
        turned = jnp.sin(angles)
        sine[at, :] = jnp.where(lane < half, -turned, turned)
        return jnp.maximum(first, place - (WINDOW - 1))

    def tables():
        @pl.loop(0, cos_k.shape[0] // step)
        def _(i):
            place = i * step + lax.broadcasted_iota(jnp.int32, (step, 1), 0)
            table_rows(place, pl.ds(i * step, step), cos_k, sin_k)

        @pl.loop(0, cos_q.shape[0] // step)
        def _(i):
            row = i * step + lax.broadcasted_iota(jnp.int32, (step, 1), 0)
            whole_pieces = i // (piece // step)
            place = row + (whole_pieces + c) * piece
            at = pl.ds(i * step, step)
            first_q[at, :] = table_rows(place, at, cos_q, sin_q)

    gather_steps(2, normed, rows_all, sems, 9, here.at[6], tables)
    far_copy.wait_recv()
    from_far = qkv_out.at[1 - y, c]
    pass_copy = remote(from_far, from_far, sems, 22, to_c)
    pass_copy.start()
    keep_tok.wait()
    own_near.wait()
    near_copy.wait_recv()
    side_copy.wait_recv()
    pass_copy.wait_recv()

    @pl.when(moves)
    def _():
        for copy in turn_copies:
            copy.wait_send()

    for copy in gain_copies + [far_copy, near_copy, side_copy, pass_copy]:
        copy.wait_send()


def front(tokens, doc_lengths, gains, near, far, w_out, seq_len, ident):
    rows, cols = tokens.shape
    docs = doc_lengths.shape[1]
    lengths = jnp.pad(doc_lengths, ((0, 7), (0, LANES - docs)))
    shape = jax.ShapeDtypeStruct
    dma = pltpu.SemaphoreType.DMA
    outs = pl.pallas_call(
        partial(front_kernel, docs),
        out_shape=(
            shape((4, 2, rows, cols), BF16),
            shape((rows, cols), BF16),
            shape(gains.shape, F32),
            shape((2, 2) + near.shape, BF16),
            shape(w_out.shape, BF16),
            shape((seq_len // 2, LANES), F32),
            shape((seq_len // 2, LANES), F32),
            shape((seq_len, LANES), F32),
            shape((seq_len, LANES), F32),
            shape((seq_len // 2, 1), jnp.int32),
        ),
        in_specs=[IN_VMEM] * 5 + [ANY],
        out_specs=(ANY, ANY, IN_VMEM, ANY, ANY) + (IN_VMEM,) * 5,
        scratch_shapes=[
            pltpu.VMEM((rows, cols), BF16),
            pltpu.VMEM(lengths.shape, lengths.dtype),
            pltpu.VMEM((4,) + gains.shape, F32),
            pltpu.VMEM((rows, cols), BF16),
            dma((23,)),
            dma((23,)),
            dma((7,)),
        ],
        compiler_params=pltpu.CompilerParams(
            collective_id=ident, has_side_effects=True, vmem_limit_bytes=VMEM_LIMIT
        ),
        cost_estimate=cost(110),
        name="front",
    )(tokens, lengths, gains, near, far, w_out)
    return (outs[0].reshape(8 * rows, cols),) + tuple(outs[1:])


def add_rows(target, first, rows, terms):
    step = 16

    @pl.loop(0, rows // step)
    def _(i):
        at = pl.ds(first + i * step, step)
        total = None
        for ref, ref_first in terms:
            part = ref[pl.ds(ref_first + i * step, step), :].astype(F32)
            total = part if total is None else total + part
        target[at, :] = total.astype(target.dtype)


def scatter_stages(cores, part, out, side, ready, got_x, got_y, pass_x, pass_y, sems):
    x, y, c = (lax.axis_index(a) for a in PLANE)
    slot = c if cores == 2 else 0
    to_x, to_y, to_c = {"x": 1 - x}, {"y": 1 - y}, {"c": 1 - c}
    rows = part.shape[2]
    half = rows // 2
    top, low = pl.ds(0, half), pl.ds(half, half)
    own, next_x = 2 * x + y, 2 * (1 - x) + y
    next_y, across = 2 * x + 1 - y, 2 * (1 - x) + 1 - y
    order = [across, next_x, next_y, own]
    from_side = []
    if cores == 2:
        for k, chip in enumerate(order):
            from_side.append(remote(part.at[chip, 1 - c], side.at[k], sems, k, to_c))

    def terms(k, first):
        out_terms = [(part.at[order[k], slot], first)]
        if cores == 2:
            out_terms.append((side.at[k], first))
        return out_terms

    def arrived(k):
        if cores == 2:
            from_side[k].wait_recv()

    a_x = remote(ready.at[0, top], pass_x, sems, 4, to_x)
    a_y = remote(ready.at[0, low], pass_y, sems, 5, to_y)
    x_top = remote(ready.at[1, top], got_x.at[top], sems, 6, to_x)
    y_low = remote(ready.at[2, low], got_y.at[low], sems, 7, to_y)
    x_low = remote(ready.at[1, low], got_x.at[low], sems, 8, to_x)
    y_top = remote(ready.at[2, top], got_y.at[top], sems, 9, to_y)

    def begin():
        for copy in from_side:
            copy.start()

    def first_hop():
        arrived(0)
        add_rows(ready.at[0], 0, half, terms(0, 0))
        a_x.start()
        add_rows(ready.at[0], half, half, terms(0, half))
        a_y.start()
        arrived(1)
        add_rows(ready.at[1], 0, half, terms(1, 0))
        x_top.start()
        arrived(2)
        add_rows(ready.at[2], half, half, terms(2, half))
        y_low.start()

    def second_hop():
        a_y.wait_recv()
        add_rows(ready.at[1], half, half, terms(1, half) + [(pass_y, 0)])
        x_low.start()
        a_x.wait_recv()
        add_rows(ready.at[2], 0, half, terms(2, 0) + [(pass_x, 0)])
        y_top.start()

    def end():
        arrived(3)
        x_top.wait_recv()
        y_low.wait_recv()
        x_low.wait_recv()
        y_top.wait_recv()
        add_rows(out, 0, rows, terms(3, 0) + [(got_x, 0), (got_y, 0)])
        for copy in from_side + [a_x, a_y, x_top, y_low, x_low, y_top]:
            copy.wait_send()

    return begin, first_hop, second_hop, end


def scatter_kernel(cores, part, out, *scratch):
    x, y, c = (lax.axis_index(a) for a in PLANE)
    meet([{"x": 1 - x}, {"y": 1 - y}] + ([{"c": 1 - c}] if cores == 2 else []))
    for stage in scatter_stages(cores, part, out, *scratch[:-2], scratch[-2:]):
        stage()


def scatter_scratch(cores, rows, cols):
    return [
        pltpu.VMEM((4, rows if cores == 2 else 16, cols), BF16),
        pltpu.VMEM((3, rows, cols), BF16),
        pltpu.VMEM((rows, cols), BF16),
        pltpu.VMEM((rows, cols), BF16),
        pltpu.VMEM((rows // 2, cols), BF16),
        pltpu.VMEM((rows // 2, cols), BF16),
        pltpu.SemaphoreType.DMA((10,)),
        pltpu.SemaphoreType.DMA((10,)),
    ]


def scatter_rows(partial_rows, cores, ident):
    rows = partial_rows.shape[0] // (4 * cores)
    cols = partial_rows.shape[1]
    part = partial_rows.astype(BF16).reshape(4, cores, rows, cols)
    return pl.pallas_call(
        partial(scatter_kernel, cores),
        out_shape=jax.ShapeDtypeStruct((rows, cols), F32),
        in_specs=[IN_VMEM],
        out_specs=IN_VMEM,
        scratch_shapes=scatter_scratch(cores, rows, cols),
        compiler_params=pltpu.CompilerParams(
            collective_id=ident, has_side_effects=True, vmem_limit_bytes=VMEM_LIMIT
        ),
        cost_estimate=cost(50),
        name="scatter_rows",
    )(part)


PARTS = 3
UNIT = 48 // PARTS
OUT_AT, UNITS = 3 * PARTS, 4 * PARTS
PIECE = 48


def reduce_kernel(
    grads, gain, far_part, down_part,
    out, rows_out, out_out, gain_out,
    far_all, down_all, far_y, far_x, down_x,
    inbox, final, gain_in, rs_send, rs_recv, ag_send, ag_recv, y_send, y_recv, x_send, x_recv,
    o_send, o_recv, g_send, g_recv,
    ma_send, ma_recv, mx_send, mx_recv, my_send, my_recv, m_here, here,
):
    x, y, c = (lax.axis_index(a) for a in PLANE)
    z = lax.axis_index("z")
    to_x, to_y, to_c = {"x": 1 - x}, {"y": 1 - y}, {"c": 1 - c}
    to_xc = {"x": 1 - x, "c": 1 - c}
    above, below = {"z": z + 1}, {"z": z - 1}
    others = [{"z": (z + k) % 4} for k in (1, 2, 3)]
    meet([to_x, to_y, to_c, to_xc] + others)

    def add_unit(target, sources):
        for first in range(0, UNIT, 16):
            at = pl.ds(first, 16)
            total = sources[0][at, :].astype(F32)
            for ref in sources[1:]:
                total = total + ref[at, :].astype(F32)
            target[at, :] = total.astype(BF16)

    width = grads.shape[3] // 2
    near_half, far_half = pl.ds(0, width), pl.ds(width, width)

    def place(q, u):
        return q * UNITS + u

    def rows_place(owner_x, owner_y, q, u):
        return ((2 * owner_x + owner_y) * 4 + q) * OUT_AT + u

    def copy(src, dst, send, recv, device):
        return pltpu.make_async_remote_copy(
            src_ref=src, dst_ref=dst, send_sem=send, recv_sem=recv,
            device_id=device, device_id_type=MESH_ID,
        )

    def rs_copy(src, q, u, slot, device):
        return copy(src, inbox.at[slot, u], rs_send.at[q, u], rs_recv.at[slot, u], device)

    def rs_arrived(slot, u):
        rs_copy(inbox.at[slot, u], 0, u, slot, to_x).wait_recv()

    def up(u):
        for q in (3, 2, 1):
            @pl.when(z == 0)
            def _():
                rs_copy(grads.at[q, u], q, u, q, above).start()

            @pl.when((z > 0) & (z < q))
            def _():
                rs_arrived(q, u)
                add_unit(inbox.at[q, u], [inbox.at[q, u], grads.at[q, u]])
                rs_copy(inbox.at[q, u], q, u, q, above).start()

    def down(u):
        for q in (0, 1, 2):
            @pl.when(z == 3)
            def _():
                rs_copy(grads.at[q, u], q, u, 4 if q == 2 else q, below).start()

            for here_z in (1, 2):
                if here_z > q:
                    @pl.when(z == here_z)
                    def _():
                        rs_arrived(q, u)
                        add_unit(inbox.at[q, u], [inbox.at[q, u], grads.at[q, u]])
                        slot = 4 if here_z - 1 == q else q
                        rs_copy(inbox.at[q, u], q, u, slot, below).start()

    def ag_copy(src, q, u, way, device):
        return copy(src, out.at[place(q, u)], ag_send.at[way, q, u], ag_recv.at[q, u], device)

    def stay_copy(u):
        return pltpu.make_async_copy(final.at[u], out.at[place(z, u)], here.at[u])

    def x_copy(src, q, u, far):
        dst = rows_place(x, y, q, u) if far == 0 else rows_place(x, 1 - y, q, u)
        return copy(src, rows_out.at[dst], x_send.at[far, q, u], x_recv.at[far, q, u], to_x)

    def y_copy(src, q, u, owner_y):
        dst = rows_out.at[rows_place(x, owner_y, q, u)]
        return copy(src, dst, y_send.at[q, u], y_recv.at[q, u], to_y)

    def o_copy(src, q, k, half, way, device):
        dst = half * 4 * PARTS + q * PARTS + k
        return copy(src, out_out.at[dst], o_send.at[way, q, k], o_recv.at[half, q, k], device)

    def spread(src, q, u):
        @pl.when(u < OUT_AT)
        def _():
            y_copy(src.at[:, far_half], q, u, y).start()
            x_copy(src.at[:, near_half], q, u, 0).start()

        @pl.when((u >= OUT_AT) & (c == x))
        def _():
            o_copy(src, q, u - OUT_AT, c, 0, to_x).start()

        @pl.when((u >= OUT_AT) & (c != x))
        def _():
            o_copy(src, q, u - OUT_AT, c, 0, to_xc).start()
            o_copy(src, q, u - OUT_AT, c, 1, to_c).start()

    def finish(u):
        @pl.when(z == 0)
        def _():
            rs_arrived(4, u)
            add_unit(final.at[u], [grads.at[0, u], inbox.at[4, u]])

        for here_z in (1, 2):
            @pl.when(z == here_z)
            def _():
                rs_arrived(here_z, u)
                rs_arrived(4, u)
                add_unit(
                    final.at[u], [grads.at[here_z, u], inbox.at[here_z, u], inbox.at[4, u]]
                )

        @pl.when(z == 3)
        def _():
            rs_arrived(3, u)
            add_unit(final.at[u], [grads.at[3, u], inbox.at[3, u]])

        @pl.when(z < 3)
        def _():
            ag_copy(final.at[u], z, u, 0, above).start()

        @pl.when(z > 0)
        def _():
            ag_copy(final.at[u], z, u, 1, below).start()

        spread(final.at[u], z, u)
        stay_copy(u).start()

    def relay(u, far):
        for q in range(4):
            got = out.at[place(q, u)]

            @pl.when(z == q + far)
            def _():
                ag_copy(got, q, u, 0, to_x).wait_recv()

                @pl.when(z < 3)
                def _():
                    ag_copy(got, q, u, 0, above).start()

                spread(got, q, u)

            @pl.when(z == q - far)
            def _():
                ag_copy(got, q, u, 1, to_x).wait_recv()

                @pl.when(z > 0)
                def _():
                    ag_copy(got, q, u, 1, below).start()

                spread(got, q, u)

    def cross(u, far):
        for q in range(4):
            @pl.when((z == q + far) | (z == q - far))
            def _():
                got = rows_out.at[rows_place(x, 1 - y, q, u)]
                y_copy(got, q, u, 1 - y).wait_recv()
                x_copy(got, q, u, 1).start()

    def gain_copy(k, device):
        return copy(gain_in.at[0], gain_in.at[1 + k], g_send.at[k], g_recv.at[k], device)

    def gain_z(k, device):
        return copy(gain_in.at[0], gain_in.at[4 + z], g_send.at[3 + k], g_recv.at[3 + z], device)

    def gain_step(i):
        for k, device in enumerate((to_c, to_x, to_y)):
            @pl.when(i == k)
            def _():
                if k == 0:
                    gain_in[0] = gain[...]
                gain_copy(k, device).start()
                gain_copy(k, device).wait()
                gain_in[0] += gain_in[1 + k]

        @pl.when(i == 3)
        def _():
            for k, device in enumerate(others):
                gain_z(k, device).start()

        @pl.when(i == 5)
        def _():
            for k in range(4):
                @pl.when(z == k)
                def _():
                    gain_in[4 + k] = gain_in[0]

                @pl.when(z != k)
                def _():
                    copy(
                        gain_in.at[0], gain_in.at[4 + k], g_send.at[3], g_recv.at[3 + k], to_x
                    ).wait_recv()

            for k, device in enumerate(others):
                gain_z(k, device).wait_send()
            gain_out[...] = (gain_in[4] + gain_in[5]) + (gain_in[6] + gain_in[7])

    ready = [
        (far_part, far_all, far_x, 0),
        (down_part, down_all, down_x, 3),
    ]
    counts = [part.shape[0] // PIECE for part, _, _, _ in ready]

    def piece(ref, q, p):
        return ref.at[q, pl.ds(pl.multiple_of(p * PIECE, 16), PIECE)]

    def own_piece(kind, p):
        return ready[kind][0].at[pl.ds(pl.multiple_of(p * PIECE, 16), PIECE)]

    def ma_copy(kind, src, q, p, way, device):
        dst = piece(ready[kind][1], q, p)
        return copy(src, dst, ma_send.at[kind, way, q, p], ma_recv.at[kind, q, p], device)

    def mx_copy(kind, src, q, p):
        dst = piece(ready[kind][2], q, p)
        return copy(src, dst, mx_send.at[kind, q, p], mx_recv.at[kind, q, p], to_x)

    def my_copy(src, q, p):
        return copy(src, piece(far_y, q, p), my_send.at[q, p], my_recv.at[q, p], to_y)

    def m_stay(kind, p):
        return pltpu.make_async_copy(
            own_piece(kind, p), piece(ready[kind][1], z, p), m_here.at[kind, p]
        )

    def m_spread(kind, src, q, p):
        if kind == 0:
            my_copy(src, q, p).start()
        else:
            mx_copy(kind, src, q, p).start()

    def m_begin(kind, p):
        src = own_piece(kind, p)

        @pl.when(z < 3)
        def _():
            ma_copy(kind, src, z, p, 0, above).start()

        @pl.when(z > 0)
        def _():
            ma_copy(kind, src, z, p, 1, below).start()

        m_spread(kind, src, z, p)
        m_stay(kind, p).start()

    def m_relay(kind, p, hops):
        for q in range(4):
            got = piece(ready[kind][1], q, p)

            @pl.when(z == q + hops)
            def _():
                ma_copy(kind, got, q, p, 0, to_x).wait_recv()

                @pl.when(z < 3)
                def _():
                    ma_copy(kind, got, q, p, 0, above).start()

                m_spread(kind, got, q, p)

            @pl.when(z == q - hops)
            def _():
                ma_copy(kind, got, q, p, 1, to_x).wait_recv()

                @pl.when(z > 0)
                def _():
                    ma_copy(kind, got, q, p, 1, below).start()

                m_spread(kind, got, q, p)

    def m_cross(p, hops):
        for q in range(4):
            @pl.when((z == q + hops) | (z == q - hops))
            def _():
                got = piece(far_y, q, p)
                my_copy(got, q, p).wait_recv()
                mx_copy(0, got, q, p).start()

    def m_step(i):
        for kind, count in enumerate(counts):
            first = i - ready[kind][3]
            when_unit(first, count, partial(m_begin, kind))
            for hops in (1, 2, 3):
                when_unit(first - hops, count, lambda p: m_relay(kind, p, hops))
        for hops in (0, 1, 2, 3):
            when_unit(i - ready[0][3] - 1 - hops, counts[0], lambda p: m_cross(p, hops))

    def m_end():
        for kind, count in enumerate(counts):
            @pl.loop(0, count)
            def _(p):
                src = own_piece(kind, p)
                m_stay(kind, p).wait()
                for q in range(4):
                    @pl.when((z < 3) & (q <= z))
                    def _():
                        ma_copy(kind, src, q, p, 0, to_x).wait_send()

                    @pl.when((z > 0) & (q >= z))
                    def _():
                        ma_copy(kind, src, q, p, 1, to_x).wait_send()

                    mx_copy(kind, src, q, p).wait()
                    if kind == 0:
                        my_copy(src, q, p).wait_send()

    def when_unit(u, last, work):
        @pl.when((u >= 0) & (u < last))
        def _():
            work(u)

    @pl.loop(0, UNITS + 8)
    def _(i):
        when_unit(i - z, UNITS, up)
        when_unit(i - (3 - z), UNITS, down)
        gain_step(i)
        when_unit(i - 3, UNITS, finish)
        for far in (1, 2, 3):
            when_unit(i - 3 - far, UNITS, lambda u: relay(u, far))
        for far in (0, 1, 2, 3):
            when_unit(i - 4 - far, OUT_AT, lambda u: cross(u, far))
        m_step(i)

    m_end()

    @pl.loop(0, UNITS)
    def _(u):
        stay_copy(u).wait()
        for q in range(4):
            src = grads.at[q, u]

            @pl.when(z != q)
            def _():
                rs_copy(src, q, u, q, to_x).wait_send()

            @pl.when((z < 3) & (q <= z))
            def _():
                ag_copy(src, q, u, 0, to_x).wait_send()

            @pl.when((z > 0) & (q >= z))
            def _():
                ag_copy(src, q, u, 1, to_x).wait_send()

            @pl.when(u < OUT_AT)
            def _():
                half = rows_out.at[0]
                y_copy(half, q, u, y).wait_send()
                x_copy(half, q, u, 0).wait()
                x_copy(half, q, u, 1).wait()

            @pl.when(u >= OUT_AT)
            def _():
                k = u - OUT_AT
                o_copy(src, q, k, c, 0, to_x).wait_send()
                o_copy(src, q, k, 1 - c, 0, to_x).wait_recv()

                @pl.when(c != x)
                def _():
                    o_copy(src, q, k, c, 1, to_x).wait_send()
                    o_copy(src, q, k, c, 0, to_x).wait_recv()


def reduce_grads(grads, gain, far, down, ident):
    cols = grads.shape[3]
    shape = jax.ShapeDtypeStruct
    dma = pltpu.SemaphoreType.DMA
    return pl.pallas_call(
        reduce_kernel,
        out_shape=(
            shape((4 * UNITS, UNIT, cols), BF16),
            shape((16 * OUT_AT, UNIT, cols // 2), BF16),
            shape((8 * PARTS, UNIT, cols), BF16),
            shape(gain.shape, F32),
            shape((4,) + far.shape, BF16),
            shape((4,) + down.shape, BF16),
            shape((4,) + far.shape, BF16),
            shape((4,) + far.shape, BF16),
            shape((4,) + down.shape, BF16),
        ),
        in_specs=[IN_VMEM] * 4,
        out_specs=(ANY, ANY, ANY, IN_VMEM) + (ANY,) * 5,
        scratch_shapes=[
            pltpu.VMEM((5, UNITS, UNIT, cols), BF16),
            pltpu.VMEM((UNITS, UNIT, cols), BF16),
            pltpu.VMEM((8,) + gain.shape, F32),
            dma((4, UNITS)),
            dma((5, UNITS)),
            dma((2, 4, UNITS)),
            dma((4, UNITS)),
            dma((4, OUT_AT)),
            dma((4, OUT_AT)),
            dma((2, 4, OUT_AT)),
            dma((2, 4, OUT_AT)),
            dma((2, 4, PARTS)),
            dma((2, 4, PARTS)),
            dma((6,)),
            dma((7,)),
            dma((2, 2, 4, down.shape[0] // PIECE)),
            dma((2, 4, down.shape[0] // PIECE)),
            dma((2, 4, down.shape[0] // PIECE)),
            dma((2, 4, down.shape[0] // PIECE)),
            dma((4, far.shape[0] // PIECE)),
            dma((4, far.shape[0] // PIECE)),
            dma((2, down.shape[0] // PIECE)),
            dma((UNITS,)),
        ],
        compiler_params=pltpu.CompilerParams(
            collective_id=ident, has_side_effects=True, vmem_limit_bytes=VMEM_LIMIT
        ),
        cost_estimate=cost(300),
        name="reduce_grads",
    )(grads, gain, far, down)


def rows_kernel(cols_f, cols_h, flags, mine, near, far, near_x, far_x, *refs):
    sources, outs = refs[:4], refs[4:]
    here_x, here_y, core = flags[0], flags[1], flags[2]
    rows, cols = outs[0].shape[0], mine.shape[-1]
    own = mine[...].reshape(rows, cols)
    full = [
        [
            jnp.where(
                (here_x == i) & (here_y == j), own, sources[2 * i + j][...].reshape(rows, cols)
            )
            for j in range(2)
        ]
        for i in range(2)
    ]
    for kind in range(3):
        first = kind * cols_h
        outs[kind][...] = jnp.concatenate(
            [full[i][j][:, first : first + cols_h] for j in range(2) for i in range(2)], 1
        ).astype(F32)
    by_x = [(near[...], far[...]), (near_x[...], far_x[...])]
    full = [
        [
            jnp.where(
                here_x == i,
                jnp.where(here_y == j, *by_x[0]),
                jnp.where(here_y == j, *by_x[1]),
            )
            for j in range(2)
        ]
        for i in range(2)
    ]
    for kind in range(2):
        pieces = []
        for j in range(2):
            for k in range(2):
                for i in range(2):
                    own = full[i][j][:, kind * cols_f : (kind + 1) * cols_f]
                    first = (2 + kind) * cols_f
                    side = full[i][j][:, first : first + cols_f]
                    pieces.append(jnp.where(core == k, own, side))
        outs[3 + kind][...] = jnp.concatenate(pieces, 1).astype(F32)


def place_rows(flags, mine, summed, near, far, near_x, far_x, rows_d, cols_f, cols_h):
    cols = summed.shape[-1]
    shape = jax.ShapeDtypeStruct

    def source(i, j):
        return pl.BlockSpec((PARTS, UNIT, cols), lambda s: ((2 * i + j) * 12 + s, 0, 0))

    def target(width):
        return pl.BlockSpec((48, width), lambda s: (s, 0))

    own = pl.BlockSpec((PARTS, UNIT, cols), lambda s: (s + s // 3, 0, 0))
    ff = pl.BlockSpec((48, 4 * cols_f), lambda s: (s, 0))
    widths = (4 * cols_h,) * 3 + (8 * cols_f,) * 2
    return pl.pallas_call(
        partial(rows_kernel, cols_f, cols_h),
        grid=(rows_d // 48,),
        out_shape=tuple(shape((rows_d, width), F32) for width in widths),
        in_specs=[pl.BlockSpec(memory_space=pltpu.SMEM), own] + [ff] * 4
        + [source(i, j) for i in range(2) for j in range(2)],
        out_specs=tuple(target(width) for width in widths),
        compiler_params=pltpu.CompilerParams(vmem_limit_bytes=VMEM_LIMIT),
        cost_estimate=cost(25),
        name="place_rows",
    )(flags, mine, near, far, near_x, far_x, summed, summed, summed, summed)


def down_kernel(per_x, flags, own, side, out):
    mine = flags[0] == pl.program_id(0) // per_x
    out[...] = jnp.where(mine, own[...].astype(F32), side[...].astype(F32))


def place_down(flags, own, side, rows):
    cols = own.shape[1]
    per_x = rows // 144
    source = pl.BlockSpec((144, cols), lambda s: (s % per_x, 0))
    return pl.pallas_call(
        partial(down_kernel, per_x),
        grid=(2 * per_x,),
        out_shape=jax.ShapeDtypeStruct((2 * rows, cols), F32),
        in_specs=[pl.BlockSpec(memory_space=pltpu.SMEM), source, source],
        out_specs=pl.BlockSpec((144, cols), lambda s: (s, 0)),
        compiler_params=pltpu.CompilerParams(vmem_limit_bytes=VMEM_LIMIT),
        cost_estimate=cost(8),
        name="place_down",
    )(flags, own, side)


def lanes(rows):
    return lax.broadcasted_iota(jnp.int32, (rows, LANES), 1)


def rotated(block, cosine, sine_signed):
    lane = lanes(block.shape[0])
    turned = jnp.where(
        lane % HEAD_DIM < HEAD_DIM // 2,
        pltpu.roll(block, LANES - HEAD_DIM // 2, 1),
        pltpu.roll(block, HEAD_DIM // 2, 1),
    )
    return block * cosine + turned * sine_signed


def key_spans(pieces, rows):
    reach = WINDOW // rows
    return [
        (max(0, 2 * j - reach) * rows, (2 * j + 2) * rows) for j in range(pieces // 2)
    ]


def seen(first_ref, place_ref, rows, low, high):
    keys = low + lax.broadcasted_iota(jnp.int32, (1, high - low), 1)
    return (keys >= first_ref[rows, :]) & (keys <= place_ref[rows, :])


def forward_kernel(
    spans, width, q_raw, k_raw, v_ref, cos_q, sin_q, cos_k, sin_k, first, place,
    q_out, k_out, ctx_out, lse_out, v_keep,
):
    valid = width - pl.program_id(0) * LANES
    k_rows = k_raw.shape[0]
    keep = lanes(k_rows) < valid
    k_out[...] = jnp.where(keep, rotated(k_raw[...], cos_k[...], sin_k[...]), 0.0).astype(BF16)
    v_keep[...] = jnp.where(keep, v_ref[...], jnp.zeros((), BF16))
    keep_q = lanes(q_raw.shape[0]) < valid
    q_out[...] = jnp.where(keep_q, rotated(q_raw[...], cos_q[...], sin_q[...]), 0.0).astype(BF16)
    rows_j = q_raw.shape[0] // len(spans)
    left = lanes(rows_j) < HEAD_DIM
    zero = jnp.zeros((), BF16)
    for j, (low, high) in enumerate(spans):
        rows = pl.ds(j * rows_j, rows_j)
        visible = seen(first, place, rows, low, high)
        query = q_out[rows, :]
        halves = []
        for side in range(2):
            mine = jnp.where(left if side == 0 else ~left, query, zero)
            scores = lax.dot_general(
                mine, k_out[low:high, :], (((1,), (1,)), ((), ())), preferred_element_type=F32
            )
            scores = jnp.where(visible, scores * 0.125, NEGATIVE)
            top = jnp.max(scores, -1, keepdims=True)
            grown = jnp.exp(scores - top)
            total = jnp.sum(grown, -1, keepdims=True)
            probs = (grown * (1.0 / total)).astype(BF16)
            ctx = jnp.dot(probs, v_keep[low:high, :], preferred_element_type=F32)
            halves.append((ctx, top + jnp.log(total)))
        ctx_out[rows, :] = jnp.where(left, halves[0][0], halves[1][0]).astype(BF16)
        lse_out[rows, :] = jnp.where(left, halves[0][1], halves[1][1])


def lane_block(rows):
    return pl.BlockSpec((rows, LANES), lambda p: (0, p))


def whole(rows, cols):
    return pl.BlockSpec((rows, cols), lambda p: (0, 0))


def attend_forward(q_raw, k_raw, value, tables, limits, pieces):
    q_rows, width = q_raw.shape
    k_rows = k_raw.shape[0]
    spans = key_spans(pieces, k_rows // pieces)
    steps = -(-width // LANES)
    shape = jax.ShapeDtypeStruct
    return pl.pallas_call(
        partial(forward_kernel, spans, width),
        grid=(steps,),
        out_shape=(
            shape((q_rows, width), BF16),
            shape((k_rows, width), BF16),
            shape((q_rows, width), BF16),
            shape((q_rows, width), F32),
        ),
        in_specs=[
            lane_block(q_rows),
            lane_block(k_rows),
            lane_block(k_rows),
            whole(q_rows, LANES),
            whole(q_rows, LANES),
            whole(k_rows, LANES),
            whole(k_rows, LANES),
            whole(q_rows, 1),
            whole(q_rows, 1),
        ],
        out_specs=(
            lane_block(q_rows),
            lane_block(k_rows),
            lane_block(q_rows),
            lane_block(q_rows),
        ),
        scratch_shapes=[pltpu.VMEM((k_rows, LANES), BF16)],
        compiler_params=pltpu.CompilerParams(vmem_limit_bytes=VMEM_LIMIT),
        cost_estimate=cost(43),
        name="attend_forward",
    )(q_raw, k_raw, value, *tables, *limits)


def backward_kernel(
    spans, width, q_ref, k_ref, v_ref, g_ref, lse, cos_q, sin_q, cos_k, sin_k, first, place,
    part, dq_out, dk_done, dv_done, rows_out,
    k_keep, v_keep, dk_out, dv_out, give, got, send, recv, *scatter,
):
    step = pl.program_id(0)
    c = lax.axis_index("c")
    rows_j = q_ref.shape[0] // len(spans)
    pair = [("dk", dk_out, dk_done), ("dv", dv_out, dv_done)]

    def to_side(at):
        return pltpu.make_async_remote_copy(
            src_ref=give.at[at],
            dst_ref=got.at[at],
            send_sem=send.at[at],
            recv_sem=recv.at[at],
            device_id={"c": 1 - c},
            device_id_type=MESH_ID,
        )

    stages = scatter_stages(2, part, rows_out, *scatter[:-2], scatter[-2:])
    x, y = lax.axis_index("x"), lax.axis_index("y")

    @pl.when(step == 0)
    def _():
        meet([{"x": 1 - x}, {"y": 1 - y}, {"c": 1 - c}])

    last = pl.num_programs(0) - 1
    for at, stage in zip((0, 1, last - 2, last), stages):
        pl.when(step == at)(stage)

    @pl.when(step > 0)
    def _():
        to_side(step - 1).wait_recv()
        for k, (_, whole_sum, done) in enumerate(pair):
            for j in range(len(spans)):
                rows = pl.ds(j * rows_j, rows_j)
                own = whole_sum[pl.ds(pl.multiple_of((2 * j + c) * rows_j, rows_j), rows_j), :]
                done[rows, :] = (own + got[step - 1, k, rows, :].astype(F32)).astype(BF16)

    @pl.when(step < pl.num_programs(0) - 1)
    def _():
        backward_step(
            spans, width, q_ref, k_ref, v_ref, g_ref, lse, cos_q, sin_q, cos_k, sin_k,
            first, place, dq_out, dk_out, dv_out, k_keep, v_keep,
        )
        for k, (_, whole_sum, _) in enumerate(pair):
            for j in range(len(spans)):
                other = pl.ds(pl.multiple_of((2 * j + 1 - c) * rows_j, rows_j), rows_j)
                give[step, k, pl.ds(j * rows_j, rows_j), :] = whole_sum[other, :].astype(BF16)
        to_side(step).start()

    @pl.when(step == pl.num_programs(0) - 1)
    def _():
        for k in range(give.shape[0]):
            to_side(k).wait_send()


def backward_step(
    spans, width, q_ref, k_ref, v_ref, g_ref, lse, cos_q, sin_q, cos_k, sin_k, first, place,
    dq_out, dk_out, dv_out, k_keep, v_keep,
):
    valid = width - pl.program_id(0) * LANES
    zero = jnp.zeros((), BF16)
    keep = lanes(k_ref.shape[0]) < valid
    k_keep[...] = jnp.where(keep, k_ref[...], zero)
    v_keep[...] = jnp.where(keep, v_ref[...], zero)
    dk_out[...] = jnp.zeros_like(dk_out)
    dv_out[...] = jnp.zeros_like(dv_out)
    rows_j = q_ref.shape[0] // len(spans)
    lane = lanes(rows_j)
    left = (lane < HEAD_DIM) & (lane < valid)
    right = (lane >= HEAD_DIM) & (lane < valid)
    for j, (low, high) in enumerate(spans):
        rows = pl.ds(j * rows_j, rows_j)
        visible = seen(first, place, rows, low, high)
        query, grad = q_ref[rows, :], g_ref[rows, :]
        stats = lse[rows, :]
        halves = []
        for side in range(2):
            mask = left if side == 0 else right
            mine = jnp.where(mask, query, zero)
            grad_mine = jnp.where(mask, grad, zero)
            nt = (((1,), (1,)), ((), ()))
            tn = (((0,), (0,)), ((), ()))
            scores = lax.dot_general(mine, k_keep[low:high, :], nt, preferred_element_type=F32)
            column = side * HEAD_DIM
            log_total = stats[:, column : column + 1]
            probs = jnp.where(visible, jnp.exp(scores * 0.125 - log_total), 0.0)
            grad_probs = lax.dot_general(
                grad_mine, v_keep[low:high, :], nt, preferred_element_type=F32
            )
            mixed = probs * grad_probs
            delta = jnp.sum(mixed, -1, keepdims=True)
            grad_scores = (mixed - probs * delta).astype(BF16)
            halves.append(
                jnp.dot(grad_scores, k_keep[low:high, :], preferred_element_type=F32) * 0.125
            )
            dk_out[low:high, :] += (
                lax.dot_general(grad_scores, mine, tn, preferred_element_type=F32) * 0.125
            )
            dv_out[low:high, :] += lax.dot_general(
                probs.astype(BF16), grad_mine, tn, preferred_element_type=F32
            )
        grad_query = jnp.where(lane < HEAD_DIM, halves[0], halves[1])
        dq_out[rows, :] = rotated(grad_query, cos_q[rows, :], -sin_q[rows, :]).astype(BF16)
    dk_out[...] = rotated(dk_out[...], cos_k[...], -sin_k[...])


def attend_backward(query, key, value, grad, lse, tables, limits, partial_rows, pieces, ident):
    q_rows, width = query.shape
    k_rows = key.shape[0]
    spans = key_spans(pieces, k_rows // pieces)
    rows, cols = partial_rows.shape[0] // 8, partial_rows.shape[1]
    steps = -(-width // LANES)
    shape = jax.ShapeDtypeStruct

    def this(rows):
        return pl.BlockSpec((rows, LANES), lambda p: (0, jnp.minimum(p, steps - 1)))

    def last(rows):
        return pl.BlockSpec((rows, LANES), lambda p: (0, jnp.maximum(p - 1, 0)))

    return pl.pallas_call(
        partial(backward_kernel, spans, width),
        grid=(steps + 1,),
        out_shape=(shape((q_rows, width), BF16),) * 3 + (shape((rows, cols), F32),),
        in_specs=[
            this(q_rows),
            this(k_rows),
            this(k_rows),
            this(q_rows),
            this(q_rows),
            whole(q_rows, LANES),
            whole(q_rows, LANES),
            whole(k_rows, LANES),
            whole(k_rows, LANES),
            whole(q_rows, 1),
            whole(q_rows, 1),
            IN_VMEM,
        ],
        out_specs=(this(q_rows), last(q_rows), last(q_rows), IN_VMEM),
        scratch_shapes=[pltpu.VMEM((k_rows, LANES), BF16)] * 2
        + [pltpu.VMEM((k_rows, LANES), F32)] * 2
        + [pltpu.VMEM((steps, 2, q_rows, LANES), BF16)] * 2
        + [pltpu.SemaphoreType.DMA((steps,))] * 2
        + scatter_scratch(2, rows, cols),
        compiler_params=pltpu.CompilerParams(
            collective_id=ident, has_side_effects=True, vmem_limit_bytes=VMEM_LIMIT
        ),
        cost_estimate=cost(57),
        name="attend_backward",
    )(
        query, key, value, grad, lse, *tables, *limits,
        partial_rows.reshape(4, 2, rows, cols),
    )


def norm_back(grad_normed, unit_rows, rms_rows, gain_rows):
    scaled = grad_normed * gain_rows
    return rms_rows * (scaled - unit_rows * jnp.mean(scaled * unit_rows, -1, keepdims=True))


def on_device(
    tokens,
    doc_lengths,
    cotangent,
    attn_gain,
    w_query,
    w_key,
    w_value,
    w_out,
    mlp_gain,
    w_gate,
    w_up,
    w_down,
):
    outer = lax.axis_size("g")
    pieces_z = lax.axis_size("z")
    x, y, c = (lax.axis_index(a) for a in PLANE)
    own = 2 * y + c

    turn_pairs = [
        (i * pieces_z + z, z * pieces_z + i) for i in range(pieces_z) for z in range(pieces_z)
    ]

    def turned(block):
        return lax.ppermute(block, ("y", "c", "z"), turn_pairs)

    def joined(shard):
        if outer == 1:
            return shard
        return lax.all_gather(shard, "g", axis=0, tiled=True)

    w_query, w_key, w_value, w_out = map(joined, (w_query, w_key, w_value, w_out))
    w_gate, w_up, w_down = map(joined, (w_gate, w_up, w_down))
    rows_d = w_query.shape[0]
    model = w_query.shape[1]
    tok_rows = tokens.shape[1]
    pieces = 2 * pieces_z
    seq_len = pieces * tok_rows
    cols_h = model // 4
    cols_f = w_gate.shape[1] // 8

    def head_cols(weight, group):
        return lax.dynamic_slice_in_dim(weight, group * cols_h, cols_h, 1)

    def qkv_cols(group):
        return jnp.concatenate([head_cols(w, group) for w in (w_query, w_key, w_value)], 1)

    def spread(gain):
        padded = jnp.zeros((model,), F32)
        return lax.dynamic_update_slice_in_dim(padded, joined(gain).astype(F32), own * rows_d, 0)

    gains = jnp.pad(jnp.stack([spread(attn_gain), spread(mlp_gain)]), ((0, 6), (0, 0)))
    normed_one, tok_low, gains, w_qkv, out_side, *tables, first_query = front(
        tokens[0],
        doc_lengths,
        gains,
        qkv_cols(2 * y + x),
        qkv_cols(2 * (1 - y) + x),
        w_out,
        seq_len,
        1,
    )
    cot_late, _ = lax.optimization_barrier((cotangent[0], tok_low))
    cot_low = turned(cot_late)
    inputs, upstream = tok_low.astype(F32), cot_low.astype(F32)
    gain_one, gain_two = gains[0:1], gains[1:2]
    w_qkv = w_qkv.reshape(4 * rows_d, 3 * cols_h)
    w_out_use = jnp.where(c == x, w_out, out_side)

    gate_late, up_late, normed_one = lax.optimization_barrier((w_gate, w_up, normed_one))

    def ff_cols(dest):
        first = (2 * dest + x) * cols_f
        return jnp.concatenate(
            [lax.dynamic_slice_in_dim(w, first, cols_f, 1) for w in (gate_late, up_late)], 1
        )

    ff_own = ff_cols(own)
    ff_c = swap(ff_cols(2 * y + 1 - c), "c")
    ff_y = swap(ff_cols(2 * (1 - y) + c), "y")
    ff_yc = lax.ppermute(
        ff_cols(2 * (1 - y) + 1 - c), ("y", "c"), [(i, 3 - i) for i in range(4)]
    )

    def ordered(a, b, flag):
        return jnp.where(flag == 0, jnp.stack([a, b]), jnp.stack([b, a]))

    down_use = lax.dynamic_slice_in_dim(w_down, x * cols_f, cols_f, 0)

    def own_rows(array):
        cols = array.shape[1:]
        split = array.reshape((pieces // 2, 2, tok_rows) + cols)
        return lax.dynamic_index_in_dim(split, c, 1, keepdims=False).reshape(
            (seq_len // 2,) + cols
        )

    place = own_rows(jnp.arange(seq_len, dtype=jnp.int32))
    limits = (first_query, place[:, None])

    rms_one = lax.rsqrt(jnp.mean(inputs * inputs, -1, keepdims=True) + EPSILON)
    unit_one = inputs * rms_one

    query_raw = dot(own_rows(normed_one), w_qkv[:, :cols_h])
    key_raw = dot(normed_one, w_qkv[:, cols_h : 2 * cols_h])
    value = dot(normed_one, w_qkv[:, 2 * cols_h :]).astype(BF16)
    query, key, context, lse = attend_forward(query_raw, key_raw, value, tables, limits, pieces)

    attn_out = scatter_rows(dot(context, w_out_use), 1, 2)
    hidden_res = inputs + BETA * attn_out
    rms_two = lax.rsqrt(jnp.mean(hidden_res * hidden_res, -1, keepdims=True) + EPSILON)
    unit_two = hidden_res * rms_two
    normed_rows = (unit_two * gain_two).astype(BF16)
    normed_rows, ff_c, ff_y, ff_yc = lax.optimization_barrier((normed_rows, ff_c, ff_y, ff_yc))
    normed_two = gather_rows(normed_rows, 2, 3)
    cot_rows = lax.optimization_barrier(((BETA * upstream).astype(BF16), normed_two))[0]
    grad_mlp = lax.all_gather(cot_rows, PLANE, axis=0, tiled=True)
    ff_near = ordered(ff_own, ff_c, c)
    ff_far = ordered(ff_y, ff_yc, c)
    w_ff = ordered(ff_near, ff_far, y).reshape(4 * rows_d, 2 * cols_f)

    gate_up = dot(normed_two, w_ff)
    gate, up = gate_up[:, :cols_f], gate_up[:, cols_f:]
    sigmoid_gate = jax.nn.sigmoid(gate)
    silu_gate = gate * sigmoid_gate
    activation = (silu_gate * up).astype(BF16)
    mlp_part = dot(activation, down_use).astype(BF16)
    mlp_part, grad_mlp = lax.optimization_barrier((mlp_part, grad_mlp))

    grad_activation = dot_nt(grad_mlp, down_use)
    grad_up = (grad_activation * silu_gate).astype(BF16)
    grad_gate = (
        grad_activation * up * (sigmoid_gate * (1.0 + gate * (1.0 - sigmoid_gate)))
    ).astype(BF16)
    grad_ff = jnp.concatenate([grad_gate, grad_up], 1)
    padded = jnp.pad(activation, ((0, 0), (0, 768 - cols_f)))
    grad_ff_side = swap(grad_ff, "c")

    def row_block(normed, y_of):
        return lax.dynamic_slice_in_dim(normed, (2 * y_of + c) * rows_d, rows_d, 1)

    def ff_rows(y_of):
        block = row_block(normed_two, y_of)
        return jnp.concatenate(
            [dot_tn(block, grad_ff).astype(BF16), dot_tn(block, grad_ff_side).astype(BF16)], 1
        )

    grad_down = dot_tn(padded, grad_mlp).astype(BF16)
    ff_near, ff_far = ff_rows(y), ff_rows(1 - y)
    back_part = dot_nt(grad_ff, w_ff).astype(BF16)
    back_part, grad_down, ff_near, ff_far = lax.optimization_barrier(
        (back_part, grad_down, ff_near, ff_far)
    )

    def sum_z(grad):
        return lax.psum_scatter(grad, "z", scatter_dimension=0, tiled=True)

    ff_far, ff_near, grad_down = sum_z(ff_far), sum_z(ff_near), sum_z(grad_down)
    grad_normed_two = scatter_rows(back_part, 2, 4)

    gain_grad_two = jnp.sum(grad_normed_two * unit_two, 0)
    grad_hidden = upstream + norm_back(grad_normed_two, unit_two, rms_two, gain_two)
    grad_attn = gather_rows((BETA * grad_hidden).astype(BF16), 1, 5)
    grad_context = dot_nt(grad_attn, w_out_use).astype(BF16)

    grad_out_part = dot_tn(context, grad_attn).astype(BF16)
    half = model // 2
    keep = lax.dynamic_slice_in_dim(grad_out_part, c * half, half, 1)
    give = lax.dynamic_slice_in_dim(grad_out_part, (1 - c) * half, half, 1)
    grad_out_half = (keep.astype(F32) + swap(give, "c").astype(F32)).astype(BF16)

    grad_context, ff_far = lax.optimization_barrier((grad_context, ff_far))
    grad_query, grad_key, grad_value, mlp_out = attend_backward(
        query, key, value, grad_context, lse, tables, limits, mlp_part, pieces, 8
    )
    grad_qkv = jnp.concatenate([grad_query, grad_key, grad_value], 1)

    query_part = dot_nt(grad_qkv, w_qkv).astype(BF16)
    ff_near = lax.optimization_barrier((ff_near, grad_query))[0]
    ff_near = lax.all_gather(ff_near, "z", axis=0, tiled=True)
    grad_normed_one = scatter_rows(query_part, 1, 6)
    grad_qkv_side = swap(grad_qkv, "c")
    grad_qkv_all = (
        jnp.where(
            c == 0,
            jnp.stack([grad_qkv, grad_qkv_side]),
            jnp.stack([grad_qkv_side, grad_qkv]),
        )
        .reshape(2, pieces // 2, tok_rows, 3 * cols_h)
        .transpose(1, 0, 2, 3)
        .reshape(seq_len, 3 * cols_h)
    )
    third = rows_d // 12
    width = -(-3 * cols_h // LANES) * LANES

    def qkv_rows(y_of):
        part = dot_tn(row_block(normed_one, y_of), grad_qkv_all).astype(BF16)
        return jnp.pad(part, ((0, 0), (0, width - 3 * cols_h)))

    grads = jnp.concatenate(
        [
            jnp.concatenate([qkv_rows(y), qkv_rows(1 - y)], 1).reshape(
                4, OUT_AT, UNIT, 2 * width
            ),
            jnp.pad(
                jnp.concatenate(jnp.split(grad_out_half, 3, 0), 1),
                ((0, 0), (0, 2 * width - 3 * half)),
            ).reshape(4, PARTS, UNIT, 2 * width),
        ],
        1,
    )
    gain_grad_one = jnp.sum(grad_normed_one * unit_one, 0)
    gain_part = jnp.pad(jnp.stack([gain_grad_one, gain_grad_two]), ((0, 6), (0, 0)))
    grads, ff_near = lax.optimization_barrier((grads, ff_near))
    near_x = swap(ff_near, "x")
    mine, summed, out_got, gain_grads, _, *ff_sums = reduce_grads(
        grads, gain_part, ff_far, grad_down, 7
    )
    down_own, far_y, far_x, down_side = (
        part.reshape(-1, part.shape[-1]) for part in ff_sums
    )
    grad_inputs = grad_hidden + norm_back(grad_normed_one, unit_one, rms_one, gain_one)

    def later(array):
        return lax.optimization_barrier((array, gain_grads))[0]

    grad_tokens = turned(later(grad_inputs.astype(BF16)))[None]
    output = turned(later((hidden_res + BETA * mlp_out).astype(BF16)))[None]
    if outer > 1:
        gain_grads = lax.psum(gain_grads, "g")


    shard = attn_gain.shape[0]
    first = own * rows_d + lax.axis_index("g") * shard
    gain_grads = lax.dynamic_slice_in_dim(gain_grads, first, shard, 1)

    def finish(grad):
        if outer > 1:
            grad = lax.psum_scatter(grad.astype(BF16), "g", scatter_dimension=0, tiled=True)
        return grad.astype(F32)

    flags = jnp.stack([x, y, c]).astype(jnp.int32)
    *qkv_all, gate_all, up_all = place_rows(
        flags, mine, summed, ff_near, far_y, near_x, far_x,
        rows_d, cols_f, cols_h,
    )
    ff_all = (gate_all, up_all)
    down_all = place_down(flags, down_own, down_side, cols_f)
    out_mine = mine.reshape(4, UNITS, UNIT, 2 * width)[:, OUT_AT:, :, : 3 * half]
    out_mine = out_mine.reshape(4 * third, 3 * half)
    out_got = out_got[:, :, : 3 * half].reshape(2, 4 * third, 3 * half)
    out_halves = [
        jnp.concatenate(
            jnp.split(jnp.where((c == x) & (c == h), out_mine, out_got[h]), 3, 1), 0
        )
        for h in range(2)
    ]
    out_all = jnp.concatenate(out_halves, 1)

    return (
        output,
        grad_tokens,
        gain_grads[0],
        finish(qkv_all[0]),
        finish(qkv_all[1]),
        finish(qkv_all[2]),
        finish(out_all),
        gain_grads[1],
        finish(ff_all[0]),
        finish(ff_all[1]),
        finish(down_all),
    )


def solution(mesh):
    seq, fsdp, rep = (mesh.shape[a] for a in ("seq", "fsdp", "rep"))
    inner = Mesh(
        mesh.devices.reshape(seq, rep // 2, 2, fsdp // rep, rep), ("x", "y", "c", "g", "z")
    )
    owners = ("y", "c", "g")
    token_spec = P(owners, ("x", "z"), None)
    placed = (token_spec, P(owners, None), token_spec, P(owners)) + (P(owners, None),) * 4
    placed = placed + (P(owners),) + (P(owners, None),) * 3
    return jax.shard_map(
        on_device,
        mesh=inner,
        in_specs=placed,
        out_specs=(token_spec, token_spec, P(owners))
        + (P(owners, None),) * 4
        + (P(owners),)
        + (P(owners, None),) * 3,
        check_vma=False,
    )
```

```python
from functools import partial
import math

import jax
import jax.numpy as jnp
from jax import lax
from jax.experimental import pallas as pl
from jax.experimental.pallas import tpu as pltpu
from jax.sharding import Mesh, PartitionSpec as P

HEADS = 36
HEAD_DIM = 64
WINDOW = 1024

BETA = 1.4 / math.sqrt(40.0)
EPSILON = 1e-05
NEGATIVE = -1e30

PLANE = ("x", "y", "c")
LANES = 128
VMEM_LIMIT = 60 * 1024 * 1024
F32 = jnp.float32
BF16 = jnp.bfloat16


def dot(left, right):
    return jnp.dot(left, right, preferred_element_type=F32)


def dot_tn(left, right):
    return lax.dot_general(left, right, (((0,), (0,)), ((), ())), preferred_element_type=F32)


def dot_nt(left, right):
    return lax.dot_general(left, right, (((1,), (1,)), ((), ())), preferred_element_type=F32)


def swap(array, axis):
    return lax.ppermute(array, axis, [(0, 1), (1, 0)])


MESH_ID = pl.DeviceIdType.MESH
ANY = pl.BlockSpec(memory_space=pl.ANY)
IN_VMEM = pl.BlockSpec(memory_space=pltpu.VMEM)


def cost(micros):
    return pl.CostEstimate(flops=int(micros * 1.0e9), bytes_accessed=0, transcendentals=0)


def remote(src, dst, sems, index, device):
    return pltpu.make_async_remote_copy(
        src_ref=src,
        dst_ref=dst,
        send_sem=sems[0].at[index],
        recv_sem=sems[1].at[index],
        device_id=device,
        device_id_type=MESH_ID,
    )


def meet(devices):
    barrier = pltpu.get_barrier_semaphore()
    for device in devices:
        pl.semaphore_signal(barrier, inc=1, device_id=device, device_id_type=MESH_ID)
    pl.semaphore_wait(barrier, len(devices))


def gather_steps(cores, block, out, sems, base, here, meanwhile=None):
    x, y, c = (lax.axis_index(a) for a in PLANE)
    slot = c if cores == 2 else 0
    to_x, to_y, to_c = {"x": 1 - x}, {"y": 1 - y}, {"c": 1 - c}
    half = block.shape[0] // 2
    top, low = pl.ds(0, half), pl.ds(half, half)
    own, next_x = 2 * x + y, 2 * (1 - x) + y
    next_y, across = 2 * x + 1 - y, 2 * (1 - x) + 1 - y

    def give(index, rows, device):
        copy = remote(block.at[rows], out.at[own, slot, rows], sems, base + index, device)
        copy.start()
        return copy

    def forward(index, chip, rows, device):
        place = out.at[chip, slot, rows]
        copy = remote(place, place, sems, base + index, device)
        copy.start()
        return copy

    x_top = give(0, top, to_x)
    y_low = give(1, low, to_y)
    x_low = give(2, low, to_x)
    y_top = give(3, top, to_y)
    stay = pltpu.make_async_copy(block, out.at[own, slot], here)
    stay.start()
    sends = [x_top, y_low, x_low, y_top]
    passed = []
    if cores == 2:
        passed.append(give(4, pl.ds(0, 2 * half), to_c))
    if meanwhile is not None:
        meanwhile()
    x_top.wait_recv()
    y_across = forward(5, next_x, top, to_y)
    if cores == 2:
        passed.append(forward(6, next_x, top, to_c))
    y_low.wait_recv()
    x_across = forward(7, next_y, low, to_x)
    if cores == 2:
        passed.append(forward(8, next_y, low, to_c))
    x_low.wait_recv()
    if cores == 2:
        passed.append(forward(9, next_x, low, to_c))
    y_top.wait_recv()
    if cores == 2:
        passed.append(forward(10, next_y, top, to_c))
    y_across.wait_recv()
    if cores == 2:
        passed.append(forward(11, across, top, to_c))
    x_across.wait_recv()
    if cores == 2:
        passed.append(forward(12, across, low, to_c))
    for copy in passed:
        copy.wait_recv()
    stay.wait()
    for copy in sends + [y_across, x_across] + passed:
        copy.wait_send()


def gather_kernel(cores, block, out, send, recv, here):
    x, y, c = (lax.axis_index(a) for a in PLANE)
    meet([{"x": 1 - x}, {"y": 1 - y}] + ([{"c": 1 - c}] if cores == 2 else []))
    gather_steps(cores, block, out, (send, recv), 0, here)


def gather_rows(block, cores, ident):
    rows, cols = block.shape
    out = pl.pallas_call(
        partial(gather_kernel, cores),
        out_shape=jax.ShapeDtypeStruct((4, cores, rows, cols), block.dtype),
        in_specs=[IN_VMEM],
        out_specs=ANY,
        scratch_shapes=[
            pltpu.SemaphoreType.DMA((13,)),
            pltpu.SemaphoreType.DMA((13,)),
            pltpu.SemaphoreType.DMA,
        ],
        compiler_params=pltpu.CompilerParams(
            collective_id=ident, has_side_effects=True, vmem_limit_bytes=VMEM_LIMIT
        ),
        cost_estimate=cost(45),
        name="gather_rows",
    )(block)
    return out.reshape(4 * cores * rows, cols)


def front_kernel(
    docs, tokens, lengths, gains, near, far, w_out,
    rows_all, tok_out, gain_out, qkv_out, side_out, cos_q, sin_q, cos_k, sin_k, first_q,
    tok_in, len_in, gain_in, normed, send, recv, here,
):
    x, y, c = (lax.axis_index(a) for a in PLANE)
    z = lax.axis_index("z")
    to_x, to_y, to_c = {"x": 1 - x}, {"y": 1 - y}, {"c": 1 - c}
    to_yc = {"y": 1 - y, "c": 1 - c}
    own = 2 * y + c
    goal = {"y": z // 2, "c": z % 2, "z": own}
    sems = (send, recv)
    moves = own != z
    barrier = pltpu.get_barrier_semaphore()
    for device in (to_x, to_y, to_c, to_yc):
        pl.semaphore_signal(barrier, inc=1, device_id=device, device_id_type=MESH_ID)

    @pl.when(moves)
    def _():
        pl.semaphore_signal(barrier, inc=1, device_id=goal, device_id_type=MESH_ID)
        pl.semaphore_wait(barrier, 5)

    @pl.when(~moves)
    def _():
        pl.semaphore_wait(barrier, 4)

    gain_copies = [
        remote(gains, gain_in.at[2 * y + c], sems, k, device)
        for k, device in enumerate((to_y, to_c, to_yc))
    ]
    turn_copies = [
        remote(src, dst, sems, 3 + k, goal)
        for k, (src, dst) in enumerate(((lengths, len_in), (tokens, tok_in)))
    ]
    stay_copies = [
        pltpu.make_async_copy(src, dst, here.at[k])
        for k, (src, dst) in enumerate(((lengths, len_in), (tokens, tok_in)))
    ]
    for copy in gain_copies:
        copy.start()
    own_gain = pltpu.make_async_copy(gains, gain_in.at[2 * y + c], here.at[3])
    own_gain.start()

    @pl.when(moves)
    def _():
        for copy in turn_copies:
            copy.start()

    @pl.when(~moves)
    def _():
        for copy in stay_copies:
            copy.start()

    far_copy = remote(far, qkv_out.at[y, c], sems, 6, to_y)
    near_copy = remote(near, qkv_out.at[y, c], sems, 7, to_c)
    side_copy = remote(w_out, side_out, sems, 8, to_c)
    far_copy.start()
    near_copy.start()
    side_copy.start()
    own_near = pltpu.make_async_copy(near, qkv_out.at[y, c], here.at[4])
    own_near.start()

    @pl.when(moves)
    def _():
        for copy in turn_copies:
            copy.wait_recv()

    @pl.when(~moves)
    def _():
        for copy in stay_copies:
            copy.wait()

    own_gain.wait()
    for copy in gain_copies:
        copy.wait_recv()
    gain_out[...] = gain_in[0] + gain_in[1] + gain_in[2] + gain_in[3]
    keep_tok = pltpu.make_async_copy(tok_in, tok_out, here.at[5])
    keep_tok.start()
    step = 16

    @pl.loop(0, tok_in.shape[0] // step)
    def _(i):
        at = pl.ds(i * step, step)
        rows = tok_in[at, :].astype(F32)
        scale = lax.rsqrt(jnp.mean(rows * rows, -1, keepdims=True) + EPSILON)
        normed[at, :] = (rows * scale * gain_out[0:1, :]).astype(BF16)

    step = 64
    piece = tok_in.shape[0]

    def table_rows(place, at, cosine, sine):
        first = jnp.zeros((step, 1), jnp.int32)
        end = jnp.zeros((1, 1), jnp.int32)
        for k in range(docs):
            length = len_in[0:1, k : k + 1]
            end = end + length
            first = first + jnp.where(place >= end, length, 0)
        lane = lax.broadcasted_iota(jnp.int32, (step, LANES), 1) % HEAD_DIM
        half = HEAD_DIM // 2
        frequency = jnp.exp((lane % half).astype(F32) * (-2.0 * math.log(10000.0) / HEAD_DIM))
        angles = (place - first).astype(F32) * frequency
        cosine[at, :] = jnp.cos(angles)
        turned = jnp.sin(angles)
        sine[at, :] = jnp.where(lane < half, -turned, turned)
        return jnp.maximum(first, place - (WINDOW - 1))

    def tables():
        @pl.loop(0, cos_k.shape[0] // step)
        def _(i):
            place = i * step + lax.broadcasted_iota(jnp.int32, (step, 1), 0)
            table_rows(place, pl.ds(i * step, step), cos_k, sin_k)

        @pl.loop(0, cos_q.shape[0] // step)
        def _(i):
            row = i * step + lax.broadcasted_iota(jnp.int32, (step, 1), 0)
            whole_pieces = i // (piece // step)
            place = row + (whole_pieces + c) * piece
            at = pl.ds(i * step, step)
            first_q[at, :] = table_rows(place, at, cos_q, sin_q)

    gather_steps(2, normed, rows_all, sems, 9, here.at[6], tables)
    far_copy.wait_recv()
    from_far = qkv_out.at[1 - y, c]
    pass_copy = remote(from_far, from_far, sems, 22, to_c)
    pass_copy.start()
    keep_tok.wait()
    own_near.wait()
    near_copy.wait_recv()
    side_copy.wait_recv()
    pass_copy.wait_recv()

    @pl.when(moves)
    def _():
        for copy in turn_copies:
            copy.wait_send()

    for copy in gain_copies + [far_copy, near_copy, side_copy, pass_copy]:
        copy.wait_send()


def front(tokens, doc_lengths, gains, near, far, w_out, seq_len, ident):
    rows, cols = tokens.shape
    docs = doc_lengths.shape[1]
    lengths = jnp.pad(doc_lengths, ((0, 7), (0, LANES - docs)))
    shape = jax.ShapeDtypeStruct
    dma = pltpu.SemaphoreType.DMA
    outs = pl.pallas_call(
        partial(front_kernel, docs),
        out_shape=(
            shape((4, 2, rows, cols), BF16),
            shape((rows, cols), BF16),
            shape(gains.shape, F32),
            shape((2, 2) + near.shape, BF16),
            shape(w_out.shape, BF16),
            shape((seq_len // 2, LANES), F32),
            shape((seq_len // 2, LANES), F32),
            shape((seq_len, LANES), F32),
            shape((seq_len, LANES), F32),
            shape((seq_len // 2, 1), jnp.int32),
        ),
        in_specs=[IN_VMEM] * 5 + [ANY],
        out_specs=(ANY, ANY, IN_VMEM, ANY, ANY) + (IN_VMEM,) * 5,
        scratch_shapes=[
            pltpu.VMEM((rows, cols), BF16),
            pltpu.VMEM(lengths.shape, lengths.dtype),
            pltpu.VMEM((4,) + gains.shape, F32),
            pltpu.VMEM((rows, cols), BF16),
            dma((23,)),
            dma((23,)),
            dma((7,)),
        ],
        compiler_params=pltpu.CompilerParams(
            collective_id=ident, has_side_effects=True, vmem_limit_bytes=VMEM_LIMIT
        ),
        cost_estimate=cost(110),
        name="front",
    )(tokens, lengths, gains, near, far, w_out)
    return (outs[0].reshape(8 * rows, cols),) + tuple(outs[1:])


def add_rows(target, first, rows, terms):
    step = 16

    @pl.loop(0, rows // step)
    def _(i):
        at = pl.ds(first + i * step, step)
        total = None
        for ref, ref_first in terms:
            part = ref[pl.ds(ref_first + i * step, step), :].astype(F32)
            total = part if total is None else total + part
        target[at, :] = total.astype(target.dtype)


def scatter_stages(cores, part, out, side, ready, got_x, got_y, pass_x, pass_y, sems):
    x, y, c = (lax.axis_index(a) for a in PLANE)
    slot = c if cores == 2 else 0
    to_x, to_y, to_c = {"x": 1 - x}, {"y": 1 - y}, {"c": 1 - c}
    rows = part.shape[2]
    half = rows // 2
    top, low = pl.ds(0, half), pl.ds(half, half)
    own, next_x = 2 * x + y, 2 * (1 - x) + y
    next_y, across = 2 * x + 1 - y, 2 * (1 - x) + 1 - y
    order = [across, next_x, next_y, own]
    from_side = []
    if cores == 2:
        for k, chip in enumerate(order):
            from_side.append(remote(part.at[chip, 1 - c], side.at[k], sems, k, to_c))

    def terms(k, first):
        out_terms = [(part.at[order[k], slot], first)]
        if cores == 2:
            out_terms.append((side.at[k], first))
        return out_terms

    def arrived(k):
        if cores == 2:
            from_side[k].wait_recv()

    a_x = remote(ready.at[0, top], pass_x, sems, 4, to_x)
    a_y = remote(ready.at[0, low], pass_y, sems, 5, to_y)
    x_top = remote(ready.at[1, top], got_x.at[top], sems, 6, to_x)
    y_low = remote(ready.at[2, low], got_y.at[low], sems, 7, to_y)
    x_low = remote(ready.at[1, low], got_x.at[low], sems, 8, to_x)
    y_top = remote(ready.at[2, top], got_y.at[top], sems, 9, to_y)

    def begin():
        for copy in from_side:
            copy.start()

    def first_hop():
        arrived(0)
        add_rows(ready.at[0], 0, half, terms(0, 0))
        a_x.start()
        add_rows(ready.at[0], half, half, terms(0, half))
        a_y.start()
        arrived(1)
        add_rows(ready.at[1], 0, half, terms(1, 0))
        x_top.start()
        arrived(2)
        add_rows(ready.at[2], half, half, terms(2, half))
        y_low.start()

    def second_hop():
        a_y.wait_recv()
        add_rows(ready.at[1], half, half, terms(1, half) + [(pass_y, 0)])
        x_low.start()
        a_x.wait_recv()
        add_rows(ready.at[2], 0, half, terms(2, 0) + [(pass_x, 0)])
        y_top.start()

    def end():
        arrived(3)
        x_top.wait_recv()
        y_low.wait_recv()
        x_low.wait_recv()
        y_top.wait_recv()
        add_rows(out, 0, rows, terms(3, 0) + [(got_x, 0), (got_y, 0)])
        for copy in from_side + [a_x, a_y, x_top, y_low, x_low, y_top]:
            copy.wait_send()

    return begin, first_hop, second_hop, end


def scatter_kernel(cores, part, out, *scratch):
    x, y, c = (lax.axis_index(a) for a in PLANE)
    meet([{"x": 1 - x}, {"y": 1 - y}] + ([{"c": 1 - c}] if cores == 2 else []))
    for stage in scatter_stages(cores, part, out, *scratch[:-2], scratch[-2:]):
        stage()


def scatter_scratch(cores, rows, cols):
    return [
        pltpu.VMEM((4, rows if cores == 2 else 16, cols), BF16),
        pltpu.VMEM((3, rows, cols), BF16),
        pltpu.VMEM((rows, cols), BF16),
        pltpu.VMEM((rows, cols), BF16),
        pltpu.VMEM((rows // 2, cols), BF16),
        pltpu.VMEM((rows // 2, cols), BF16),
        pltpu.SemaphoreType.DMA((10,)),
        pltpu.SemaphoreType.DMA((10,)),
    ]


def scatter_rows(partial_rows, cores, ident):
    rows = partial_rows.shape[0] // (4 * cores)
    cols = partial_rows.shape[1]
    part = partial_rows.astype(BF16).reshape(4, cores, rows, cols)
    return pl.pallas_call(
        partial(scatter_kernel, cores),
        out_shape=jax.ShapeDtypeStruct((rows, cols), F32),
        in_specs=[IN_VMEM],
        out_specs=IN_VMEM,
        scratch_shapes=scatter_scratch(cores, rows, cols),
        compiler_params=pltpu.CompilerParams(
            collective_id=ident, has_side_effects=True, vmem_limit_bytes=VMEM_LIMIT
        ),
        cost_estimate=cost(50),
        name="scatter_rows",
    )(part)


PARTS = 3
UNIT = 48 // PARTS
OUT_AT, UNITS = 3 * PARTS, 4 * PARTS
PIECE = 48


def reduce_kernel(
    grads, gain, far_part, down_part,
    out, rows_out, out_out, gain_out,
    far_all, down_all, far_y, far_x, down_x,
    inbox, final, gain_in, rs_send, rs_recv, ag_send, ag_recv, y_send, y_recv, x_send, x_recv,
    o_send, o_recv, g_send, g_recv,
    ma_send, ma_recv, mx_send, mx_recv, my_send, my_recv, m_here, here,
):
    x, y, c = (lax.axis_index(a) for a in PLANE)
    z = lax.axis_index("z")
    to_x, to_y, to_c = {"x": 1 - x}, {"y": 1 - y}, {"c": 1 - c}
    to_xc = {"x": 1 - x, "c": 1 - c}
    above, below = {"z": z + 1}, {"z": z - 1}
    others = [{"z": (z + k) % 4} for k in (1, 2, 3)]
    meet([to_x, to_y, to_c, to_xc] + others)

    def add_unit(target, sources):
        for first in range(0, UNIT, 16):
            at = pl.ds(first, 16)
            total = sources[0][at, :].astype(F32)
            for ref in sources[1:]:
                total = total + ref[at, :].astype(F32)
            target[at, :] = total.astype(BF16)

    width = grads.shape[3] // 2
    near_half, far_half = pl.ds(0, width), pl.ds(width, width)

    def place(q, u):
        return q * UNITS + u

    def rows_place(owner_x, owner_y, q, u):
        return ((2 * owner_x + owner_y) * 4 + q) * OUT_AT + u

    def copy(src, dst, send, recv, device):
        return pltpu.make_async_remote_copy(
            src_ref=src, dst_ref=dst, send_sem=send, recv_sem=recv,
            device_id=device, device_id_type=MESH_ID,
        )

    def rs_copy(src, q, u, slot, device):
        return copy(src, inbox.at[slot, u], rs_send.at[q, u], rs_recv.at[slot, u], device)

    def rs_arrived(slot, u):
        rs_copy(inbox.at[slot, u], 0, u, slot, to_x).wait_recv()

    def up(u):
        for q in (3, 2, 1):
            @pl.when(z == 0)
            def _():
                rs_copy(grads.at[q, u], q, u, q, above).start()

            @pl.when((z > 0) & (z < q))
            def _():
                rs_arrived(q, u)
                add_unit(inbox.at[q, u], [inbox.at[q, u], grads.at[q, u]])
                rs_copy(inbox.at[q, u], q, u, q, above).start()

    def down(u):
        for q in (0, 1, 2):
            @pl.when(z == 3)
            def _():
                rs_copy(grads.at[q, u], q, u, 4 if q == 2 else q, below).start()

            for here_z in (1, 2):
                if here_z > q:
                    @pl.when(z == here_z)
                    def _():
                        rs_arrived(q, u)
                        add_unit(inbox.at[q, u], [inbox.at[q, u], grads.at[q, u]])
                        slot = 4 if here_z - 1 == q else q
                        rs_copy(inbox.at[q, u], q, u, slot, below).start()

    def ag_copy(src, q, u, way, device):
        return copy(src, out.at[place(q, u)], ag_send.at[way, q, u], ag_recv.at[q, u], device)

    def stay_copy(u):
        return pltpu.make_async_copy(final.at[u], out.at[place(z, u)], here.at[u])

    def x_copy(src, q, u, far):
        dst = rows_place(x, y, q, u) if far == 0 else rows_place(x, 1 - y, q, u)
        return copy(src, rows_out.at[dst], x_send.at[far, q, u], x_recv.at[far, q, u], to_x)

    def y_copy(src, q, u, owner_y):
        dst = rows_out.at[rows_place(x, owner_y, q, u)]
        return copy(src, dst, y_send.at[q, u], y_recv.at[q, u], to_y)

    def o_copy(src, q, k, half, way, device):
        dst = half * 4 * PARTS + q * PARTS + k
        return copy(src, out_out.at[dst], o_send.at[way, q, k], o_recv.at[half, q, k], device)

    def spread(src, q, u):
        @pl.when(u < OUT_AT)
        def _():
            y_copy(src.at[:, far_half], q, u, y).start()
            x_copy(src.at[:, near_half], q, u, 0).start()

        @pl.when((u >= OUT_AT) & (c == x))
        def _():
            o_copy(src, q, u - OUT_AT, c, 0, to_x).start()

        @pl.when((u >= OUT_AT) & (c != x))
        def _():
            o_copy(src, q, u - OUT_AT, c, 0, to_xc).start()
            o_copy(src, q, u - OUT_AT, c, 1, to_c).start()

    def finish(u):
        @pl.when(z == 0)
        def _():
            rs_arrived(4, u)
            add_unit(final.at[u], [grads.at[0, u], inbox.at[4, u]])

        for here_z in (1, 2):
            @pl.when(z == here_z)
            def _():
                rs_arrived(here_z, u)
                rs_arrived(4, u)
                add_unit(
                    final.at[u], [grads.at[here_z, u], inbox.at[here_z, u], inbox.at[4, u]]
                )

        @pl.when(z == 3)
        def _():
            rs_arrived(3, u)
            add_unit(final.at[u], [grads.at[3, u], inbox.at[3, u]])

        @pl.when(z < 3)
        def _():
            ag_copy(final.at[u], z, u, 0, above).start()

        @pl.when(z > 0)
        def _():
            ag_copy(final.at[u], z, u, 1, below).start()

        spread(final.at[u], z, u)
        stay_copy(u).start()

    def relay(u, far):
        for q in range(4):
            got = out.at[place(q, u)]

            @pl.when(z == q + far)
            def _():
                ag_copy(got, q, u, 0, to_x).wait_recv()

                @pl.when(z < 3)
                def _():
                    ag_copy(got, q, u, 0, above).start()

                spread(got, q, u)

            @pl.when(z == q - far)
            def _():
                ag_copy(got, q, u, 1, to_x).wait_recv()

                @pl.when(z > 0)
                def _():
                    ag_copy(got, q, u, 1, below).start()

                spread(got, q, u)

    def cross(u, far):
        for q in range(4):
            @pl.when((z == q + far) | (z == q - far))
            def _():
                got = rows_out.at[rows_place(x, 1 - y, q, u)]
                y_copy(got, q, u, 1 - y).wait_recv()
                x_copy(got, q, u, 1).start()

    def gain_copy(k, device):
        return copy(gain_in.at[0], gain_in.at[1 + k], g_send.at[k], g_recv.at[k], device)

    def gain_z(k, device):
        return copy(gain_in.at[0], gain_in.at[4 + z], g_send.at[3 + k], g_recv.at[3 + z], device)

    def gain_step(i):
        for k, device in enumerate((to_c, to_x, to_y)):
            @pl.when(i == k)
            def _():
                if k == 0:
                    gain_in[0] = gain[...]
                gain_copy(k, device).start()
                gain_copy(k, device).wait()
                gain_in[0] += gain_in[1 + k]

        @pl.when(i == 3)
        def _():
            for k, device in enumerate(others):
                gain_z(k, device).start()

        @pl.when(i == 5)
        def _():
            for k in range(4):
                @pl.when(z == k)
                def _():
                    gain_in[4 + k] = gain_in[0]

                @pl.when(z != k)
                def _():
                    copy(
                        gain_in.at[0], gain_in.at[4 + k], g_send.at[3], g_recv.at[3 + k], to_x
                    ).wait_recv()

            for k, device in enumerate(others):
                gain_z(k, device).wait_send()
            gain_out[...] = (gain_in[4] + gain_in[5]) + (gain_in[6] + gain_in[7])

    ready = [
        (far_part, far_all, far_x, 0),
        (down_part, down_all, down_x, 0),
    ]
    counts = [part.shape[0] // PIECE for part, _, _, _ in ready]

    def piece(ref, q, p):
        return ref.at[q, pl.ds(pl.multiple_of(p * PIECE, 16), PIECE)]

    def own_piece(kind, p):
        return ready[kind][0].at[pl.ds(pl.multiple_of(p * PIECE, 16), PIECE)]

    def ma_copy(kind, src, q, p, way, device):
        dst = piece(ready[kind][1], q, p)
        return copy(src, dst, ma_send.at[kind, way, q, p], ma_recv.at[kind, q, p], device)

    def mx_copy(kind, src, q, p):
        dst = piece(ready[kind][2], q, p)
        return copy(src, dst, mx_send.at[kind, q, p], mx_recv.at[kind, q, p], to_x)

    def my_copy(src, q, p):
        return copy(src, piece(far_y, q, p), my_send.at[q, p], my_recv.at[q, p], to_y)

    def m_stay(kind, p):
        return pltpu.make_async_copy(
            own_piece(kind, p), piece(ready[kind][1], z, p), m_here.at[kind, p]
        )

    def m_spread(kind, src, q, p):
        if kind == 0:
            my_copy(src, q, p).start()
        else:
            mx_copy(kind, src, q, p).start()

    def m_begin(kind, p):
        src = own_piece(kind, p)

        @pl.when(z < 3)
        def _():
            ma_copy(kind, src, z, p, 0, above).start()

        @pl.when(z > 0)
        def _():
            ma_copy(kind, src, z, p, 1, below).start()

        m_spread(kind, src, z, p)
        m_stay(kind, p).start()

    def m_relay(kind, p, hops):
        for q in range(4):
            got = piece(ready[kind][1], q, p)

            @pl.when(z == q + hops)
            def _():
                ma_copy(kind, got, q, p, 0, to_x).wait_recv()

                @pl.when(z < 3)
                def _():
                    ma_copy(kind, got, q, p, 0, above).start()

                m_spread(kind, got, q, p)

            @pl.when(z == q - hops)
            def _():
                ma_copy(kind, got, q, p, 1, to_x).wait_recv()

                @pl.when(z > 0)
                def _():
                    ma_copy(kind, got, q, p, 1, below).start()

                m_spread(kind, got, q, p)

    def m_cross(p, hops):
        for q in range(4):
            @pl.when((z == q + hops) | (z == q - hops))
            def _():
                got = piece(far_y, q, p)
                my_copy(got, q, p).wait_recv()
                mx_copy(0, got, q, p).start()

    def m_step(i):
        for kind, count in enumerate(counts):
            first = i - ready[kind][3]
            when_unit(first, count, partial(m_begin, kind))
            for hops in (1, 2, 3):
                when_unit(first - hops, count, lambda p: m_relay(kind, p, hops))
        for hops in (0, 1, 2, 3):
            when_unit(i - ready[0][3] - 1 - hops, counts[0], lambda p: m_cross(p, hops))

    def m_end():
        for kind, count in enumerate(counts):
            @pl.loop(0, count)
            def _(p):
                src = own_piece(kind, p)
                m_stay(kind, p).wait()
                for q in range(4):
                    @pl.when((z < 3) & (q <= z))
                    def _():
                        ma_copy(kind, src, q, p, 0, to_x).wait_send()

                    @pl.when((z > 0) & (q >= z))
                    def _():
                        ma_copy(kind, src, q, p, 1, to_x).wait_send()

                    mx_copy(kind, src, q, p).wait()
                    if kind == 0:
                        my_copy(src, q, p).wait_send()

    def when_unit(u, last, work):
        @pl.when((u >= 0) & (u < last))
        def _():
            work(u)

    @pl.loop(0, UNITS + 8)
    def _(i):
        when_unit(i - z, UNITS, up)
        when_unit(i - (3 - z), UNITS, down)
        gain_step(i)
        when_unit(i - 3, UNITS, finish)
        for far in (1, 2, 3):
            when_unit(i - 3 - far, UNITS, lambda u: relay(u, far))
        for far in (0, 1, 2, 3):
            when_unit(i - 4 - far, OUT_AT, lambda u: cross(u, far))
        m_step(i)

    m_end()

    @pl.loop(0, UNITS)
    def _(u):
        stay_copy(u).wait()
        for q in range(4):
            src = grads.at[q, u]

            @pl.when(z != q)
            def _():
                rs_copy(src, q, u, q, to_x).wait_send()

            @pl.when((z < 3) & (q <= z))
            def _():
                ag_copy(src, q, u, 0, to_x).wait_send()

            @pl.when((z > 0) & (q >= z))
            def _():
                ag_copy(src, q, u, 1, to_x).wait_send()

            @pl.when(u < OUT_AT)
            def _():
                half = rows_out.at[0]
                y_copy(half, q, u, y).wait_send()
                x_copy(half, q, u, 0).wait()
                x_copy(half, q, u, 1).wait()

            @pl.when(u >= OUT_AT)
            def _():
                k = u - OUT_AT
                o_copy(src, q, k, c, 0, to_x).wait_send()
                o_copy(src, q, k, 1 - c, 0, to_x).wait_recv()

                @pl.when(c != x)
                def _():
                    o_copy(src, q, k, c, 1, to_x).wait_send()
                    o_copy(src, q, k, c, 0, to_x).wait_recv()


def reduce_grads(grads, gain, far, down, ident):
    cols = grads.shape[3]
    shape = jax.ShapeDtypeStruct
    dma = pltpu.SemaphoreType.DMA
    return pl.pallas_call(
        reduce_kernel,
        out_shape=(
            shape((4 * UNITS, UNIT, cols), BF16),
            shape((16 * OUT_AT, UNIT, cols // 2), BF16),
            shape((8 * PARTS, UNIT, cols), BF16),
            shape(gain.shape, F32),
            shape((4,) + far.shape, BF16),
            shape((4,) + down.shape, BF16),
            shape((4,) + far.shape, BF16),
            shape((4,) + far.shape, BF16),
            shape((4,) + down.shape, BF16),
        ),
        in_specs=[IN_VMEM] * 4,
        out_specs=(ANY, ANY, ANY, IN_VMEM) + (ANY,) * 5,
        scratch_shapes=[
            pltpu.VMEM((5, UNITS, UNIT, cols), BF16),
            pltpu.VMEM((UNITS, UNIT, cols), BF16),
            pltpu.VMEM((8,) + gain.shape, F32),
            dma((4, UNITS)),
            dma((5, UNITS)),
            dma((2, 4, UNITS)),
            dma((4, UNITS)),
            dma((4, OUT_AT)),
            dma((4, OUT_AT)),
            dma((2, 4, OUT_AT)),
            dma((2, 4, OUT_AT)),
            dma((2, 4, PARTS)),
            dma((2, 4, PARTS)),
            dma((6,)),
            dma((7,)),
            dma((2, 2, 4, down.shape[0] // PIECE)),
            dma((2, 4, down.shape[0] // PIECE)),
            dma((2, 4, down.shape[0] // PIECE)),
            dma((2, 4, down.shape[0] // PIECE)),
            dma((4, far.shape[0] // PIECE)),
            dma((4, far.shape[0] // PIECE)),
            dma((2, down.shape[0] // PIECE)),
            dma((UNITS,)),
        ],
        compiler_params=pltpu.CompilerParams(
            collective_id=ident, has_side_effects=True, vmem_limit_bytes=VMEM_LIMIT
        ),
        cost_estimate=cost(300),
        name="reduce_grads",
    )(grads, gain, far, down)


def rows_kernel(cols_f, cols_h, flags, mine, near, far, near_x, far_x, *refs):
    sources, outs = refs[:4], refs[4:]
    here_x, here_y, core = flags[0], flags[1], flags[2]
    rows, cols = outs[0].shape[0], mine.shape[-1]
    own = mine[...].reshape(rows, cols)
    full = [
        [
            jnp.where(
                (here_x == i) & (here_y == j), own, sources[2 * i + j][...].reshape(rows, cols)
            )
            for j in range(2)
        ]
        for i in range(2)
    ]
    for kind in range(3):
        first = kind * cols_h
        outs[kind][...] = jnp.concatenate(
            [full[i][j][:, first : first + cols_h] for j in range(2) for i in range(2)], 1
        ).astype(F32)
    by_x = [(near[...], far[...]), (near_x[...], far_x[...])]
    full = [
        [
            jnp.where(
                here_x == i,
                jnp.where(here_y == j, *by_x[0]),
                jnp.where(here_y == j, *by_x[1]),
            )
            for j in range(2)
        ]
        for i in range(2)
    ]
    for kind in range(2):
        pieces = []
        for j in range(2):
            for k in range(2):
                for i in range(2):
                    own = full[i][j][:, kind * cols_f : (kind + 1) * cols_f]
                    first = (2 + kind) * cols_f
                    side = full[i][j][:, first : first + cols_f]
                    pieces.append(jnp.where(core == k, own, side))
        outs[3 + kind][...] = jnp.concatenate(pieces, 1).astype(F32)


def place_rows(flags, mine, summed, near, far, near_x, far_x, rows_d, cols_f, cols_h):
    cols = summed.shape[-1]
    shape = jax.ShapeDtypeStruct

    def source(i, j):
        return pl.BlockSpec((PARTS, UNIT, cols), lambda s: ((2 * i + j) * 12 + s, 0, 0))

    def target(width):
        return pl.BlockSpec((48, width), lambda s: (s, 0))

    own = pl.BlockSpec((PARTS, UNIT, cols), lambda s: (s + s // 3, 0, 0))
    ff = pl.BlockSpec((48, 4 * cols_f), lambda s: (s, 0))
    widths = (4 * cols_h,) * 3 + (8 * cols_f,) * 2
    return pl.pallas_call(
        partial(rows_kernel, cols_f, cols_h),
        grid=(rows_d // 48,),
        out_shape=tuple(shape((rows_d, width), F32) for width in widths),
        in_specs=[pl.BlockSpec(memory_space=pltpu.SMEM), own] + [ff] * 4
        + [source(i, j) for i in range(2) for j in range(2)],
        out_specs=tuple(target(width) for width in widths),
        compiler_params=pltpu.CompilerParams(vmem_limit_bytes=VMEM_LIMIT),
        cost_estimate=cost(25),
        name="place_rows",
    )(flags, mine, near, far, near_x, far_x, summed, summed, summed, summed)


def down_kernel(per_x, flags, own, side, out):
    mine = flags[0] == pl.program_id(0) // per_x
    out[...] = jnp.where(mine, own[...].astype(F32), side[...].astype(F32))


def place_down(flags, own, side, rows):
    cols = own.shape[1]
    per_x = rows // 144
    source = pl.BlockSpec((144, cols), lambda s: (s % per_x, 0))
    return pl.pallas_call(
        partial(down_kernel, per_x),
        grid=(2 * per_x,),
        out_shape=jax.ShapeDtypeStruct((2 * rows, cols), F32),
        in_specs=[pl.BlockSpec(memory_space=pltpu.SMEM), source, source],
        out_specs=pl.BlockSpec((144, cols), lambda s: (s, 0)),
        compiler_params=pltpu.CompilerParams(vmem_limit_bytes=VMEM_LIMIT),
        cost_estimate=cost(8),
        name="place_down",
    )(flags, own, side)


def lanes(rows):
    return lax.broadcasted_iota(jnp.int32, (rows, LANES), 1)


def rotated(block, cosine, sine_signed):
    lane = lanes(block.shape[0])
    turned = jnp.where(
        lane % HEAD_DIM < HEAD_DIM // 2,
        pltpu.roll(block, LANES - HEAD_DIM // 2, 1),
        pltpu.roll(block, HEAD_DIM // 2, 1),
    )
    return block * cosine + turned * sine_signed


def key_spans(pieces, rows):
    reach = WINDOW // rows
    return [
        (max(0, 2 * j - reach) * rows, (2 * j + 2) * rows) for j in range(pieces // 2)
    ]


def seen(first_ref, place_ref, rows, low, high):
    keys = low + lax.broadcasted_iota(jnp.int32, (1, high - low), 1)
    return (keys >= first_ref[rows, :]) & (keys <= place_ref[rows, :])


def forward_kernel(
    spans, width, q_raw, k_raw, v_ref, cos_q, sin_q, cos_k, sin_k, first, place,
    q_out, k_out, ctx_out, lse_out, v_keep,
):
    valid = width - pl.program_id(0) * LANES
    k_rows = k_raw.shape[0]
    keep = lanes(k_rows) < valid
    k_out[...] = jnp.where(keep, rotated(k_raw[...], cos_k[...], sin_k[...]), 0.0).astype(BF16)
    v_keep[...] = jnp.where(keep, v_ref[...], jnp.zeros((), BF16))
    keep_q = lanes(q_raw.shape[0]) < valid
    q_out[...] = jnp.where(keep_q, rotated(q_raw[...], cos_q[...], sin_q[...]), 0.0).astype(BF16)
    rows_j = q_raw.shape[0] // len(spans)
    left = lanes(rows_j) < HEAD_DIM
    zero = jnp.zeros((), BF16)
    for j, (low, high) in enumerate(spans):
        rows = pl.ds(j * rows_j, rows_j)
        visible = seen(first, place, rows, low, high)
        query = q_out[rows, :]
        halves = []
        for side in range(2):
            mine = jnp.where(left if side == 0 else ~left, query, zero)
            scores = lax.dot_general(
                mine, k_out[low:high, :], (((1,), (1,)), ((), ())), preferred_element_type=F32
            )
            scores = jnp.where(visible, scores * 0.125, NEGATIVE)
            top = jnp.max(scores, -1, keepdims=True)
            grown = jnp.exp(scores - top)
            total = jnp.sum(grown, -1, keepdims=True)
            probs = (grown * (1.0 / total)).astype(BF16)
            ctx = jnp.dot(probs, v_keep[low:high, :], preferred_element_type=F32)
            halves.append((ctx, top + jnp.log(total)))
        ctx_out[rows, :] = jnp.where(left, halves[0][0], halves[1][0]).astype(BF16)
        lse_out[rows, :] = jnp.where(left, halves[0][1], halves[1][1])


def lane_block(rows):
    return pl.BlockSpec((rows, LANES), lambda p: (0, p))


def whole(rows, cols):
    return pl.BlockSpec((rows, cols), lambda p: (0, 0))


def attend_forward(q_raw, k_raw, value, tables, limits, pieces):
    q_rows, width = q_raw.shape
    k_rows = k_raw.shape[0]
    spans = key_spans(pieces, k_rows // pieces)
    steps = -(-width // LANES)
    shape = jax.ShapeDtypeStruct
    return pl.pallas_call(
        partial(forward_kernel, spans, width),
        grid=(steps,),
        out_shape=(
            shape((q_rows, width), BF16),
            shape((k_rows, width), BF16),
            shape((q_rows, width), BF16),
            shape((q_rows, width), F32),
        ),
        in_specs=[
            lane_block(q_rows),
            lane_block(k_rows),
            lane_block(k_rows),
            whole(q_rows, LANES),
            whole(q_rows, LANES),
            whole(k_rows, LANES),
            whole(k_rows, LANES),
            whole(q_rows, 1),
            whole(q_rows, 1),
        ],
        out_specs=(
            lane_block(q_rows),
            lane_block(k_rows),
            lane_block(q_rows),
            lane_block(q_rows),
        ),
        scratch_shapes=[pltpu.VMEM((k_rows, LANES), BF16)],
        compiler_params=pltpu.CompilerParams(vmem_limit_bytes=VMEM_LIMIT),
        cost_estimate=cost(43),
        name="attend_forward",
    )(q_raw, k_raw, value, *tables, *limits)


def backward_kernel(
    spans, width, q_ref, k_ref, v_ref, g_ref, lse, cos_q, sin_q, cos_k, sin_k, first, place,
    part, dq_out, dk_done, dv_done, rows_out,
    k_keep, v_keep, dk_out, dv_out, give, got, send, recv, *scatter,
):
    step = pl.program_id(0)
    c = lax.axis_index("c")
    rows_j = q_ref.shape[0] // len(spans)
    pair = [("dk", dk_out, dk_done), ("dv", dv_out, dv_done)]

    def to_side(at):
        return pltpu.make_async_remote_copy(
            src_ref=give.at[at],
            dst_ref=got.at[at],
            send_sem=send.at[at],
            recv_sem=recv.at[at],
            device_id={"c": 1 - c},
            device_id_type=MESH_ID,
        )

    stages = scatter_stages(2, part, rows_out, *scatter[:-2], scatter[-2:])
    x, y = lax.axis_index("x"), lax.axis_index("y")

    @pl.when(step == 0)
    def _():
        meet([{"x": 1 - x}, {"y": 1 - y}, {"c": 1 - c}])

    last = pl.num_programs(0) - 1
    for at, stage in zip((0, 1, last - 2, last), stages):
        pl.when(step == at)(stage)

    @pl.when(step > 0)
    def _():
        to_side(step - 1).wait_recv()
        for k, (_, whole_sum, done) in enumerate(pair):
            for j in range(len(spans)):
                rows = pl.ds(j * rows_j, rows_j)
                own = whole_sum[pl.ds(pl.multiple_of((2 * j + c) * rows_j, rows_j), rows_j), :]
                done[rows, :] = (own + got[step - 1, k, rows, :].astype(F32)).astype(BF16)

    @pl.when(step < pl.num_programs(0) - 1)
    def _():
        backward_step(
            spans, width, q_ref, k_ref, v_ref, g_ref, lse, cos_q, sin_q, cos_k, sin_k,
            first, place, dq_out, dk_out, dv_out, k_keep, v_keep,
        )
        for k, (_, whole_sum, _) in enumerate(pair):
            for j in range(len(spans)):
                other = pl.ds(pl.multiple_of((2 * j + 1 - c) * rows_j, rows_j), rows_j)
                give[step, k, pl.ds(j * rows_j, rows_j), :] = whole_sum[other, :].astype(BF16)
        to_side(step).start()

    @pl.when(step == pl.num_programs(0) - 1)
    def _():
        for k in range(give.shape[0]):
            to_side(k).wait_send()


def backward_step(
    spans, width, q_ref, k_ref, v_ref, g_ref, lse, cos_q, sin_q, cos_k, sin_k, first, place,
    dq_out, dk_out, dv_out, k_keep, v_keep,
):
    valid = width - pl.program_id(0) * LANES
    zero = jnp.zeros((), BF16)
    keep = lanes(k_ref.shape[0]) < valid
    k_keep[...] = jnp.where(keep, k_ref[...], zero)
    v_keep[...] = jnp.where(keep, v_ref[...], zero)
    dk_out[...] = jnp.zeros_like(dk_out)
    dv_out[...] = jnp.zeros_like(dv_out)
    rows_j = q_ref.shape[0] // len(spans)
    lane = lanes(rows_j)
    left = (lane < HEAD_DIM) & (lane < valid)
    right = (lane >= HEAD_DIM) & (lane < valid)
    for j, (low, high) in enumerate(spans):
        rows = pl.ds(j * rows_j, rows_j)
        visible = seen(first, place, rows, low, high)
        query, grad = q_ref[rows, :], g_ref[rows, :]
        stats = lse[rows, :]
        halves = []
        for side in range(2):
            mask = left if side == 0 else right
            mine = jnp.where(mask, query, zero)
            grad_mine = jnp.where(mask, grad, zero)
            nt = (((1,), (1,)), ((), ()))
            tn = (((0,), (0,)), ((), ()))
            scores = lax.dot_general(mine, k_keep[low:high, :], nt, preferred_element_type=F32)
            column = side * HEAD_DIM
            log_total = stats[:, column : column + 1]
            probs = jnp.where(visible, jnp.exp(scores * 0.125 - log_total), 0.0)
            grad_probs = lax.dot_general(
                grad_mine, v_keep[low:high, :], nt, preferred_element_type=F32
            )
            mixed = probs * grad_probs
            delta = jnp.sum(mixed, -1, keepdims=True)
            grad_scores = (mixed - probs * delta).astype(BF16)
            halves.append(
                jnp.dot(grad_scores, k_keep[low:high, :], preferred_element_type=F32) * 0.125
            )
            dk_out[low:high, :] += (
                lax.dot_general(grad_scores, mine, tn, preferred_element_type=F32) * 0.125
            )
            dv_out[low:high, :] += lax.dot_general(
                probs.astype(BF16), grad_mine, tn, preferred_element_type=F32
            )
        grad_query = jnp.where(lane < HEAD_DIM, halves[0], halves[1])
        dq_out[rows, :] = rotated(grad_query, cos_q[rows, :], -sin_q[rows, :]).astype(BF16)
    dk_out[...] = rotated(dk_out[...], cos_k[...], -sin_k[...])


def attend_backward(query, key, value, grad, lse, tables, limits, partial_rows, pieces, ident):
    q_rows, width = query.shape
    k_rows = key.shape[0]
    spans = key_spans(pieces, k_rows // pieces)
    rows, cols = partial_rows.shape[0] // 8, partial_rows.shape[1]
    steps = -(-width // LANES)
    shape = jax.ShapeDtypeStruct

    def this(rows):
        return pl.BlockSpec((rows, LANES), lambda p: (0, jnp.minimum(p, steps - 1)))

    def last(rows):
        return pl.BlockSpec((rows, LANES), lambda p: (0, jnp.maximum(p - 1, 0)))

    return pl.pallas_call(
        partial(backward_kernel, spans, width),
        grid=(steps + 1,),
        out_shape=(shape((q_rows, width), BF16),) * 3 + (shape((rows, cols), F32),),
        in_specs=[
            this(q_rows),
            this(k_rows),
            this(k_rows),
            this(q_rows),
            this(q_rows),
            whole(q_rows, LANES),
            whole(q_rows, LANES),
            whole(k_rows, LANES),
            whole(k_rows, LANES),
            whole(q_rows, 1),
            whole(q_rows, 1),
            IN_VMEM,
        ],
        out_specs=(this(q_rows), last(q_rows), last(q_rows), IN_VMEM),
        scratch_shapes=[pltpu.VMEM((k_rows, LANES), BF16)] * 2
        + [pltpu.VMEM((k_rows, LANES), F32)] * 2
        + [pltpu.VMEM((steps, 2, q_rows, LANES), BF16)] * 2
        + [pltpu.SemaphoreType.DMA((steps,))] * 2
        + scatter_scratch(2, rows, cols),
        compiler_params=pltpu.CompilerParams(
            collective_id=ident, has_side_effects=True, vmem_limit_bytes=VMEM_LIMIT
        ),
        cost_estimate=cost(57),
        name="attend_backward",
    )(
        query, key, value, grad, lse, *tables, *limits,
        partial_rows.reshape(4, 2, rows, cols),
    )


def norm_back(grad_normed, unit_rows, rms_rows, gain_rows):
    scaled = grad_normed * gain_rows
    return rms_rows * (scaled - unit_rows * jnp.mean(scaled * unit_rows, -1, keepdims=True))


def on_device(
    tokens,
    doc_lengths,
    cotangent,
    attn_gain,
    w_query,
    w_key,
    w_value,
    w_out,
    mlp_gain,
    w_gate,
    w_up,
    w_down,
):
    outer = lax.axis_size("g")
    pieces_z = lax.axis_size("z")
    x, y, c = (lax.axis_index(a) for a in PLANE)
    own = 2 * y + c

    turn_pairs = [
        (i * pieces_z + z, z * pieces_z + i) for i in range(pieces_z) for z in range(pieces_z)
    ]

    def turned(block):
        return lax.ppermute(block, ("y", "c", "z"), turn_pairs)

    def joined(shard):
        if outer == 1:
            return shard
        return lax.all_gather(shard, "g", axis=0, tiled=True)

    w_query, w_key, w_value, w_out = map(joined, (w_query, w_key, w_value, w_out))
    w_gate, w_up, w_down = map(joined, (w_gate, w_up, w_down))
    rows_d = w_query.shape[0]
    model = w_query.shape[1]
    tok_rows = tokens.shape[1]
    pieces = 2 * pieces_z
    seq_len = pieces * tok_rows
    cols_h = model // 4
    cols_f = w_gate.shape[1] // 8

    def head_cols(weight, group):
        return lax.dynamic_slice_in_dim(weight, group * cols_h, cols_h, 1)

    def qkv_cols(group):
        return jnp.concatenate([head_cols(w, group) for w in (w_query, w_key, w_value)], 1)

    def spread(gain):
        padded = jnp.zeros((model,), F32)
        return lax.dynamic_update_slice_in_dim(padded, joined(gain).astype(F32), own * rows_d, 0)

    gains = jnp.pad(jnp.stack([spread(attn_gain), spread(mlp_gain)]), ((0, 6), (0, 0)))
    normed_one, tok_low, gains, w_qkv, out_side, *tables, first_query = front(
        tokens[0],
        doc_lengths,
        gains,
        qkv_cols(2 * y + x),
        qkv_cols(2 * (1 - y) + x),
        w_out,
        seq_len,
        1,
    )
    cot_late, _ = lax.optimization_barrier((cotangent[0], tok_low))
    cot_low = turned(cot_late)
    inputs, upstream = tok_low.astype(F32), cot_low.astype(F32)
    gain_one, gain_two = gains[0:1], gains[1:2]
    w_qkv = w_qkv.reshape(4 * rows_d, 3 * cols_h)
    w_out_use = jnp.where(c == x, w_out, out_side)

    gate_late, up_late, normed_one = lax.optimization_barrier((w_gate, w_up, normed_one))

    def ff_cols(dest):
        first = (2 * dest + x) * cols_f
        return jnp.concatenate(
            [lax.dynamic_slice_in_dim(w, first, cols_f, 1) for w in (gate_late, up_late)], 1
        )

    ff_own = ff_cols(own)
    ff_c = swap(ff_cols(2 * y + 1 - c), "c")
    ff_y = swap(ff_cols(2 * (1 - y) + c), "y")
    ff_yc = lax.ppermute(
        ff_cols(2 * (1 - y) + 1 - c), ("y", "c"), [(i, 3 - i) for i in range(4)]
    )

    def ordered(a, b, flag):
        return jnp.where(flag == 0, jnp.stack([a, b]), jnp.stack([b, a]))

    down_use = lax.dynamic_slice_in_dim(w_down, x * cols_f, cols_f, 0)

    def own_rows(array):
        cols = array.shape[1:]
        split = array.reshape((pieces // 2, 2, tok_rows) + cols)
        return lax.dynamic_index_in_dim(split, c, 1, keepdims=False).reshape(
            (seq_len // 2,) + cols
        )

    place = own_rows(jnp.arange(seq_len, dtype=jnp.int32))
    limits = (first_query, place[:, None])

    rms_one = lax.rsqrt(jnp.mean(inputs * inputs, -1, keepdims=True) + EPSILON)
    unit_one = inputs * rms_one

    query_raw = dot(own_rows(normed_one), w_qkv[:, :cols_h])
    key_raw = dot(normed_one, w_qkv[:, cols_h : 2 * cols_h])
    value = dot(normed_one, w_qkv[:, 2 * cols_h :]).astype(BF16)
    query, key, context, lse = attend_forward(query_raw, key_raw, value, tables, limits, pieces)

    attn_out = scatter_rows(dot(context, w_out_use), 1, 2)
    hidden_res = inputs + BETA * attn_out
    rms_two = lax.rsqrt(jnp.mean(hidden_res * hidden_res, -1, keepdims=True) + EPSILON)
    unit_two = hidden_res * rms_two
    normed_rows = (unit_two * gain_two).astype(BF16)
    normed_rows, ff_c, ff_y, ff_yc = lax.optimization_barrier((normed_rows, ff_c, ff_y, ff_yc))
    normed_two = gather_rows(normed_rows, 2, 3)
    cot_rows = lax.optimization_barrier(((BETA * upstream).astype(BF16), normed_two))[0]
    grad_mlp = lax.all_gather(cot_rows, PLANE, axis=0, tiled=True)
    ff_near = ordered(ff_own, ff_c, c)
    ff_far = ordered(ff_y, ff_yc, c)
    w_ff = ordered(ff_near, ff_far, y).reshape(4 * rows_d, 2 * cols_f)

    gate_up = dot(normed_two, w_ff)
    gate, up = gate_up[:, :cols_f], gate_up[:, cols_f:]
    sigmoid_gate = jax.nn.sigmoid(gate)
    silu_gate = gate * sigmoid_gate
    activation = (silu_gate * up).astype(BF16)
    mlp_part = dot(activation, down_use).astype(BF16)
    mlp_part, grad_mlp = lax.optimization_barrier((mlp_part, grad_mlp))

    grad_activation = dot_nt(grad_mlp, down_use)
    grad_up = (grad_activation * silu_gate).astype(BF16)
    grad_gate = (
        grad_activation * up * (sigmoid_gate * (1.0 + gate * (1.0 - sigmoid_gate)))
    ).astype(BF16)
    grad_ff = jnp.concatenate([grad_gate, grad_up], 1)
    padded = jnp.pad(activation, ((0, 0), (0, 768 - cols_f)))
    grad_ff_side = swap(grad_ff, "c")

    def row_block(normed, y_of):
        return lax.dynamic_slice_in_dim(normed, (2 * y_of + c) * rows_d, rows_d, 1)

    def ff_rows(y_of):
        block = row_block(normed_two, y_of)
        return jnp.concatenate(
            [dot_tn(block, grad_ff).astype(BF16), dot_tn(block, grad_ff_side).astype(BF16)], 1
        )

    grad_down = dot_tn(padded, grad_mlp).astype(BF16)
    ff_near, ff_far = ff_rows(y), ff_rows(1 - y)
    back_part = dot_nt(grad_ff, w_ff).astype(BF16)
    back_part, grad_down, ff_near, ff_far = lax.optimization_barrier(
        (back_part, grad_down, ff_near, ff_far)
    )

    def sum_z(grad):
        return lax.psum_scatter(grad, "z", scatter_dimension=0, tiled=True)

    ff_far, ff_near, grad_down = sum_z(ff_far), sum_z(ff_near), sum_z(grad_down)
    grad_normed_two = scatter_rows(back_part, 2, 4)

    gain_grad_two = jnp.sum(grad_normed_two * unit_two, 0)
    grad_hidden = upstream + norm_back(grad_normed_two, unit_two, rms_two, gain_two)
    grad_attn = gather_rows((BETA * grad_hidden).astype(BF16), 1, 5)
    grad_context = dot_nt(grad_attn, w_out_use).astype(BF16)

    grad_out_part = dot_tn(context, grad_attn).astype(BF16)
    half = model // 2
    keep = lax.dynamic_slice_in_dim(grad_out_part, c * half, half, 1)
    give = lax.dynamic_slice_in_dim(grad_out_part, (1 - c) * half, half, 1)
    grad_out_half = (keep.astype(F32) + swap(give, "c").astype(F32)).astype(BF16)

    grad_context, ff_near = lax.optimization_barrier((grad_context, ff_near))
    ff_near = lax.all_gather(ff_near, "z", axis=0, tiled=True)
    grad_query, grad_key, grad_value, mlp_out = attend_backward(
        query, key, value, grad_context, lse, tables, limits, mlp_part, pieces, 8
    )
    grad_qkv = jnp.concatenate([grad_query, grad_key, grad_value], 1)

    query_part = dot_nt(grad_qkv, w_qkv).astype(BF16)
    grad_normed_one = scatter_rows(query_part, 1, 6)
    grad_qkv_side = swap(grad_qkv, "c")
    grad_qkv_all = (
        jnp.where(
            c == 0,
            jnp.stack([grad_qkv, grad_qkv_side]),
            jnp.stack([grad_qkv_side, grad_qkv]),
        )
        .reshape(2, pieces // 2, tok_rows, 3 * cols_h)
        .transpose(1, 0, 2, 3)
        .reshape(seq_len, 3 * cols_h)
    )
    third = rows_d // 12
    width = -(-3 * cols_h // LANES) * LANES

    def qkv_rows(y_of):
        part = dot_tn(row_block(normed_one, y_of), grad_qkv_all).astype(BF16)
        return jnp.pad(part, ((0, 0), (0, width - 3 * cols_h)))

    grads = jnp.concatenate(
        [
            jnp.concatenate([qkv_rows(y), qkv_rows(1 - y)], 1).reshape(
                4, OUT_AT, UNIT, 2 * width
            ),
            jnp.pad(
                jnp.concatenate(jnp.split(grad_out_half, 3, 0), 1),
                ((0, 0), (0, 2 * width - 3 * half)),
            ).reshape(4, PARTS, UNIT, 2 * width),
        ],
        1,
    )
    gain_grad_one = jnp.sum(grad_normed_one * unit_one, 0)
    gain_part = jnp.pad(jnp.stack([gain_grad_one, gain_grad_two]), ((0, 6), (0, 0)))
    grads, ff_near = lax.optimization_barrier((grads, ff_near))
    near_x = swap(ff_near, "x")
    mine, summed, out_got, gain_grads, _, *ff_sums = reduce_grads(
        grads, gain_part, ff_far, grad_down, 7
    )
    down_own, far_y, far_x, down_side = (
        part.reshape(-1, part.shape[-1]) for part in ff_sums
    )
    grad_inputs = grad_hidden + norm_back(grad_normed_one, unit_one, rms_one, gain_one)

    def later(array):
        return lax.optimization_barrier((array, gain_grads))[0]

    grad_tokens = turned(later(grad_inputs.astype(BF16)))[None]
    output = turned(later((hidden_res + BETA * mlp_out).astype(BF16)))[None]
    if outer > 1:
        gain_grads = lax.psum(gain_grads, "g")


    shard = attn_gain.shape[0]
    first = own * rows_d + lax.axis_index("g") * shard
    gain_grads = lax.dynamic_slice_in_dim(gain_grads, first, shard, 1)

    def finish(grad):
        if outer > 1:
            grad = lax.psum_scatter(grad.astype(BF16), "g", scatter_dimension=0, tiled=True)
        return grad.astype(F32)

    flags = jnp.stack([x, y, c]).astype(jnp.int32)
    *qkv_all, gate_all, up_all = place_rows(
        flags, mine, summed, ff_near, far_y, near_x, far_x,
        rows_d, cols_f, cols_h,
    )
    ff_all = (gate_all, up_all)
    down_all = place_down(flags, down_own, down_side, cols_f)
    out_mine = mine.reshape(4, UNITS, UNIT, 2 * width)[:, OUT_AT:, :, : 3 * half]
    out_mine = out_mine.reshape(4 * third, 3 * half)
    out_got = out_got[:, :, : 3 * half].reshape(2, 4 * third, 3 * half)
    out_halves = [
        jnp.concatenate(
            jnp.split(jnp.where((c == x) & (c == h), out_mine, out_got[h]), 3, 1), 0
        )
        for h in range(2)
    ]
    out_all = jnp.concatenate(out_halves, 1)

    return (
        output,
        grad_tokens,
        gain_grads[0],
        finish(qkv_all[0]),
        finish(qkv_all[1]),
        finish(qkv_all[2]),
        finish(out_all),
        gain_grads[1],
        finish(ff_all[0]),
        finish(ff_all[1]),
        finish(down_all),
    )


def solution(mesh):
    seq, fsdp, rep = (mesh.shape[a] for a in ("seq", "fsdp", "rep"))
    inner = Mesh(
        mesh.devices.reshape(seq, rep // 2, 2, fsdp // rep, rep), ("x", "y", "c", "g", "z")
    )
    owners = ("y", "c", "g")
    token_spec = P(owners, ("x", "z"), None)
    placed = (token_spec, P(owners, None), token_spec, P(owners)) + (P(owners, None),) * 4
    placed = placed + (P(owners),) + (P(owners, None),) * 3
    return jax.shard_map(
        on_device,
        mesh=inner,
        in_specs=placed,
        out_specs=(token_spec, token_spec, P(owners))
        + (P(owners, None),) * 4
        + (P(owners),)
        + (P(owners, None),) * 3,
        check_vma=False,
    )
```

```python
from functools import partial
import math

import jax
import jax.numpy as jnp
from jax import lax
from jax.experimental import pallas as pl
from jax.experimental.pallas import tpu as pltpu
from jax.sharding import Mesh, PartitionSpec as P

HEADS = 36
HEAD_DIM = 64
WINDOW = 1024

BETA = 1.4 / math.sqrt(40.0)
EPSILON = 1e-05
NEGATIVE = -1e30

PLANE = ("x", "y", "c")
LANES = 128
VMEM_LIMIT = 60 * 1024 * 1024
F32 = jnp.float32
BF16 = jnp.bfloat16


def dot(left, right):
    return jnp.dot(left, right, preferred_element_type=F32)


def dot_tn(left, right):
    return lax.dot_general(left, right, (((0,), (0,)), ((), ())), preferred_element_type=F32)


def dot_nt(left, right):
    return lax.dot_general(left, right, (((1,), (1,)), ((), ())), preferred_element_type=F32)


def swap(array, axis):
    return lax.ppermute(array, axis, [(0, 1), (1, 0)])


MESH_ID = pl.DeviceIdType.MESH
ANY = pl.BlockSpec(memory_space=pl.ANY)
IN_VMEM = pl.BlockSpec(memory_space=pltpu.VMEM)


def cost(micros):
    return pl.CostEstimate(flops=int(micros * 1.0e9), bytes_accessed=0, transcendentals=0)


def remote(src, dst, sems, index, device):
    return pltpu.make_async_remote_copy(
        src_ref=src,
        dst_ref=dst,
        send_sem=sems[0].at[index],
        recv_sem=sems[1].at[index],
        device_id=device,
        device_id_type=MESH_ID,
    )


def meet(devices):
    barrier = pltpu.get_barrier_semaphore()
    for device in devices:
        pl.semaphore_signal(barrier, inc=1, device_id=device, device_id_type=MESH_ID)
    pl.semaphore_wait(barrier, len(devices))


def gather_steps(cores, block, out, sems, base, here, meanwhile=None):
    x, y, c = (lax.axis_index(a) for a in PLANE)
    slot = c if cores == 2 else 0
    to_x, to_y, to_c = {"x": 1 - x}, {"y": 1 - y}, {"c": 1 - c}
    half = block.shape[0] // 2
    top, low = pl.ds(0, half), pl.ds(half, half)
    own, next_x = 2 * x + y, 2 * (1 - x) + y
    next_y, across = 2 * x + 1 - y, 2 * (1 - x) + 1 - y

    def give(index, rows, device):
        copy = remote(block.at[rows], out.at[own, slot, rows], sems, base + index, device)
        copy.start()
        return copy

    def forward(index, chip, rows, device):
        place = out.at[chip, slot, rows]
        copy = remote(place, place, sems, base + index, device)
        copy.start()
        return copy

    x_top = give(0, top, to_x)
    y_low = give(1, low, to_y)
    x_low = give(2, low, to_x)
    y_top = give(3, top, to_y)
    stay = pltpu.make_async_copy(block, out.at[own, slot], here)
    stay.start()
    sends = [x_top, y_low, x_low, y_top]
    passed = []
    if cores == 2:
        passed.append(give(4, pl.ds(0, 2 * half), to_c))
    if meanwhile is not None:
        meanwhile()
    x_top.wait_recv()
    y_across = forward(5, next_x, top, to_y)
    if cores == 2:
        passed.append(forward(6, next_x, top, to_c))
    y_low.wait_recv()
    x_across = forward(7, next_y, low, to_x)
    if cores == 2:
        passed.append(forward(8, next_y, low, to_c))
    x_low.wait_recv()
    if cores == 2:
        passed.append(forward(9, next_x, low, to_c))
    y_top.wait_recv()
    if cores == 2:
        passed.append(forward(10, next_y, top, to_c))
    y_across.wait_recv()
    if cores == 2:
        passed.append(forward(11, across, top, to_c))
    x_across.wait_recv()
    if cores == 2:
        passed.append(forward(12, across, low, to_c))
    for copy in passed:
        copy.wait_recv()
    stay.wait()
    for copy in sends + [y_across, x_across] + passed:
        copy.wait_send()


def gather_kernel(cores, block, out, send, recv, here):
    x, y, c = (lax.axis_index(a) for a in PLANE)
    meet([{"x": 1 - x}, {"y": 1 - y}] + ([{"c": 1 - c}] if cores == 2 else []))
    gather_steps(cores, block, out, (send, recv), 0, here)


def gather_rows(block, cores, ident):
    rows, cols = block.shape
    out = pl.pallas_call(
        partial(gather_kernel, cores),
        out_shape=jax.ShapeDtypeStruct((4, cores, rows, cols), block.dtype),
        in_specs=[IN_VMEM],
        out_specs=ANY,
        scratch_shapes=[
            pltpu.SemaphoreType.DMA((13,)),
            pltpu.SemaphoreType.DMA((13,)),
            pltpu.SemaphoreType.DMA,
        ],
        compiler_params=pltpu.CompilerParams(
            collective_id=ident, has_side_effects=True, vmem_limit_bytes=VMEM_LIMIT
        ),
        cost_estimate=cost(45),
        name="gather_rows",
    )(block)
    return out.reshape(4 * cores * rows, cols)


def front_kernel(
    docs, tokens, lengths, gains, near, far, w_out,
    rows_all, tok_out, gain_out, qkv_out, side_out, cos_q, sin_q, cos_k, sin_k, first_q,
    tok_in, len_in, gain_in, normed, send, recv, here,
):
    x, y, c = (lax.axis_index(a) for a in PLANE)
    z = lax.axis_index("z")
    to_x, to_y, to_c = {"x": 1 - x}, {"y": 1 - y}, {"c": 1 - c}
    to_yc = {"y": 1 - y, "c": 1 - c}
    own = 2 * y + c
    goal = {"y": z // 2, "c": z % 2, "z": own}
    sems = (send, recv)
    moves = own != z
    barrier = pltpu.get_barrier_semaphore()
    for device in (to_x, to_y, to_c, to_yc):
        pl.semaphore_signal(barrier, inc=1, device_id=device, device_id_type=MESH_ID)

    @pl.when(moves)
    def _():
        pl.semaphore_signal(barrier, inc=1, device_id=goal, device_id_type=MESH_ID)
        pl.semaphore_wait(barrier, 5)

    @pl.when(~moves)
    def _():
        pl.semaphore_wait(barrier, 4)

    gain_copies = [
        remote(gains, gain_in.at[2 * y + c], sems, k, device)
        for k, device in enumerate((to_y, to_c, to_yc))
    ]
    turn_copies = [
        remote(src, dst, sems, 3 + k, goal)
        for k, (src, dst) in enumerate(((lengths, len_in), (tokens, tok_in)))
    ]
    stay_copies = [
        pltpu.make_async_copy(src, dst, here.at[k])
        for k, (src, dst) in enumerate(((lengths, len_in), (tokens, tok_in)))
    ]
    for copy in gain_copies:
        copy.start()
    own_gain = pltpu.make_async_copy(gains, gain_in.at[2 * y + c], here.at[3])
    own_gain.start()

    @pl.when(moves)
    def _():
        for copy in turn_copies:
            copy.start()

    @pl.when(~moves)
    def _():
        for copy in stay_copies:
            copy.start()

    far_copy = remote(far, qkv_out.at[y, c], sems, 6, to_y)
    near_copy = remote(near, qkv_out.at[y, c], sems, 7, to_c)
    side_copy = remote(w_out, side_out, sems, 8, to_c)
    far_copy.start()
    near_copy.start()
    side_copy.start()
    own_near = pltpu.make_async_copy(near, qkv_out.at[y, c], here.at[4])
    own_near.start()

    @pl.when(moves)
    def _():
        for copy in turn_copies:
            copy.wait_recv()

    @pl.when(~moves)
    def _():
        for copy in stay_copies:
            copy.wait()

    own_gain.wait()
    for copy in gain_copies:
        copy.wait_recv()
    gain_out[...] = gain_in[0] + gain_in[1] + gain_in[2] + gain_in[3]
    keep_tok = pltpu.make_async_copy(tok_in, tok_out, here.at[5])
    keep_tok.start()
    step = 16

    @pl.loop(0, tok_in.shape[0] // step)
    def _(i):
        at = pl.ds(i * step, step)
        rows = tok_in[at, :].astype(F32)
        scale = lax.rsqrt(jnp.mean(rows * rows, -1, keepdims=True) + EPSILON)
        normed[at, :] = (rows * scale * gain_out[0:1, :]).astype(BF16)

    step = 64
    piece = tok_in.shape[0]

    def table_rows(place, at, cosine, sine):
        first = jnp.zeros((step, 1), jnp.int32)
        end = jnp.zeros((1, 1), jnp.int32)
        for k in range(docs):
            length = len_in[0:1, k : k + 1]
            end = end + length
            first = first + jnp.where(place >= end, length, 0)
        lane = lax.broadcasted_iota(jnp.int32, (step, LANES), 1) % HEAD_DIM
        half = HEAD_DIM // 2
        frequency = jnp.exp((lane % half).astype(F32) * (-2.0 * math.log(10000.0) / HEAD_DIM))
        angles = (place - first).astype(F32) * frequency
        cosine[at, :] = jnp.cos(angles)
        turned = jnp.sin(angles)
        sine[at, :] = jnp.where(lane < half, -turned, turned)
        return jnp.maximum(first, place - (WINDOW - 1))

    def tables():
        @pl.loop(0, cos_k.shape[0] // step)
        def _(i):
            place = i * step + lax.broadcasted_iota(jnp.int32, (step, 1), 0)
            table_rows(place, pl.ds(i * step, step), cos_k, sin_k)

        @pl.loop(0, cos_q.shape[0] // step)
        def _(i):
            row = i * step + lax.broadcasted_iota(jnp.int32, (step, 1), 0)
            whole_pieces = i // (piece // step)
            place = row + (whole_pieces + c) * piece
            at = pl.ds(i * step, step)
            first_q[at, :] = table_rows(place, at, cos_q, sin_q)

    gather_steps(2, normed, rows_all, sems, 9, here.at[6], tables)
    far_copy.wait_recv()
    from_far = qkv_out.at[1 - y, c]
    pass_copy = remote(from_far, from_far, sems, 22, to_c)
    pass_copy.start()
    keep_tok.wait()
    own_near.wait()
    near_copy.wait_recv()
    side_copy.wait_recv()
    pass_copy.wait_recv()

    @pl.when(moves)
    def _():
        for copy in turn_copies:
            copy.wait_send()

    for copy in gain_copies + [far_copy, near_copy, side_copy, pass_copy]:
        copy.wait_send()


def front(tokens, doc_lengths, gains, near, far, w_out, seq_len, ident):
    rows, cols = tokens.shape
    docs = doc_lengths.shape[1]
    lengths = jnp.pad(doc_lengths, ((0, 7), (0, LANES - docs)))
    shape = jax.ShapeDtypeStruct
    dma = pltpu.SemaphoreType.DMA
    outs = pl.pallas_call(
        partial(front_kernel, docs),
        out_shape=(
            shape((4, 2, rows, cols), BF16),
            shape((rows, cols), BF16),
            shape(gains.shape, F32),
            shape((2, 2) + near.shape, BF16),
            shape(w_out.shape, BF16),
            shape((seq_len // 2, LANES), F32),
            shape((seq_len // 2, LANES), F32),
            shape((seq_len, LANES), F32),
            shape((seq_len, LANES), F32),
            shape((seq_len // 2, 1), jnp.int32),
        ),
        in_specs=[IN_VMEM] * 5 + [ANY],
        out_specs=(ANY, ANY, IN_VMEM, ANY, ANY) + (IN_VMEM,) * 5,
        scratch_shapes=[
            pltpu.VMEM((rows, cols), BF16),
            pltpu.VMEM(lengths.shape, lengths.dtype),
            pltpu.VMEM((4,) + gains.shape, F32),
            pltpu.VMEM((rows, cols), BF16),
            dma((23,)),
            dma((23,)),
            dma((7,)),
        ],
        compiler_params=pltpu.CompilerParams(
            collective_id=ident, has_side_effects=True, vmem_limit_bytes=VMEM_LIMIT
        ),
        cost_estimate=cost(110),
        name="front",
    )(tokens, lengths, gains, near, far, w_out)
    return (outs[0].reshape(8 * rows, cols),) + tuple(outs[1:])


def add_rows(target, first, rows, terms):
    step = 16

    @pl.loop(0, rows // step)
    def _(i):
        at = pl.ds(first + i * step, step)
        total = None
        for ref, ref_first in terms:
            part = ref[pl.ds(ref_first + i * step, step), :].astype(F32)
            total = part if total is None else total + part
        target[at, :] = total.astype(target.dtype)


def scatter_stages(cores, part, out, side, ready, got_x, got_y, pass_x, pass_y, sems):
    x, y, c = (lax.axis_index(a) for a in PLANE)
    slot = c if cores == 2 else 0
    to_x, to_y, to_c = {"x": 1 - x}, {"y": 1 - y}, {"c": 1 - c}
    rows = part.shape[2]
    half = rows // 2
    top, low = pl.ds(0, half), pl.ds(half, half)
    own, next_x = 2 * x + y, 2 * (1 - x) + y
    next_y, across = 2 * x + 1 - y, 2 * (1 - x) + 1 - y
    order = [across, next_x, next_y, own]
    from_side = []
    if cores == 2:
        for k, chip in enumerate(order):
            from_side.append(remote(part.at[chip, 1 - c], side.at[k], sems, k, to_c))

    def terms(k, first):
        out_terms = [(part.at[order[k], slot], first)]
        if cores == 2:
            out_terms.append((side.at[k], first))
        return out_terms

    def arrived(k):
        if cores == 2:
            from_side[k].wait_recv()

    a_x = remote(ready.at[0, top], pass_x, sems, 4, to_x)
    a_y = remote(ready.at[0, low], pass_y, sems, 5, to_y)
    x_top = remote(ready.at[1, top], got_x.at[top], sems, 6, to_x)
    y_low = remote(ready.at[2, low], got_y.at[low], sems, 7, to_y)
    x_low = remote(ready.at[1, low], got_x.at[low], sems, 8, to_x)
    y_top = remote(ready.at[2, top], got_y.at[top], sems, 9, to_y)

    def begin():
        for copy in from_side:
            copy.start()

    def first_hop():
        arrived(0)
        add_rows(ready.at[0], 0, half, terms(0, 0))
        a_x.start()
        add_rows(ready.at[0], half, half, terms(0, half))
        a_y.start()
        arrived(1)
        add_rows(ready.at[1], 0, half, terms(1, 0))
        x_top.start()
        arrived(2)
        add_rows(ready.at[2], half, half, terms(2, half))
        y_low.start()

    def second_hop():
        a_y.wait_recv()
        add_rows(ready.at[1], half, half, terms(1, half) + [(pass_y, 0)])
        x_low.start()
        a_x.wait_recv()
        add_rows(ready.at[2], 0, half, terms(2, 0) + [(pass_x, 0)])
        y_top.start()

    def end():
        arrived(3)
        x_top.wait_recv()
        y_low.wait_recv()
        x_low.wait_recv()
        y_top.wait_recv()
        add_rows(out, 0, rows, terms(3, 0) + [(got_x, 0), (got_y, 0)])
        for copy in from_side + [a_x, a_y, x_top, y_low, x_low, y_top]:
            copy.wait_send()

    return begin, first_hop, second_hop, end


def scatter_kernel(cores, part, out, *scratch):
    x, y, c = (lax.axis_index(a) for a in PLANE)
    meet([{"x": 1 - x}, {"y": 1 - y}] + ([{"c": 1 - c}] if cores == 2 else []))
    for stage in scatter_stages(cores, part, out, *scratch[:-2], scratch[-2:]):
        stage()


def scatter_scratch(cores, rows, cols):
    return [
        pltpu.VMEM((4, rows if cores == 2 else 16, cols), BF16),
        pltpu.VMEM((3, rows, cols), BF16),
        pltpu.VMEM((rows, cols), BF16),
        pltpu.VMEM((rows, cols), BF16),
        pltpu.VMEM((rows // 2, cols), BF16),
        pltpu.VMEM((rows // 2, cols), BF16),
        pltpu.SemaphoreType.DMA((10,)),
        pltpu.SemaphoreType.DMA((10,)),
    ]


def scatter_rows(partial_rows, cores, ident):
    rows = partial_rows.shape[0] // (4 * cores)
    cols = partial_rows.shape[1]
    part = partial_rows.astype(BF16).reshape(4, cores, rows, cols)
    return pl.pallas_call(
        partial(scatter_kernel, cores),
        out_shape=jax.ShapeDtypeStruct((rows, cols), F32),
        in_specs=[IN_VMEM],
        out_specs=IN_VMEM,
        scratch_shapes=scatter_scratch(cores, rows, cols),
        compiler_params=pltpu.CompilerParams(
            collective_id=ident, has_side_effects=True, vmem_limit_bytes=VMEM_LIMIT
        ),
        cost_estimate=cost(50),
        name="scatter_rows",
    )(part)


PARTS = 3
UNIT = 48 // PARTS
OUT_AT, UNITS = 3 * PARTS, 4 * PARTS
PIECE = 48


def reduce_kernel(
    grads, gain, far_part, down_part,
    out, rows_out, out_out, gain_out,
    far_all, down_all, far_y, far_x, down_x,
    inbox, final, gain_in, rs_send, rs_recv, ag_send, ag_recv, y_send, y_recv, x_send, x_recv,
    o_send, o_recv, g_send, g_recv,
    ma_send, ma_recv, mx_send, mx_recv, my_send, my_recv, m_here, here,
):
    x, y, c = (lax.axis_index(a) for a in PLANE)
    z = lax.axis_index("z")
    to_x, to_y, to_c = {"x": 1 - x}, {"y": 1 - y}, {"c": 1 - c}
    to_xc = {"x": 1 - x, "c": 1 - c}
    above, below = {"z": z + 1}, {"z": z - 1}
    others = [{"z": (z + k) % 4} for k in (1, 2, 3)]
    meet([to_x, to_y, to_c, to_xc] + others)

    def add_unit(target, sources):
        for first in range(0, UNIT, 16):
            at = pl.ds(first, 16)
            total = sources[0][at, :].astype(F32)
            for ref in sources[1:]:
                total = total + ref[at, :].astype(F32)
            target[at, :] = total.astype(BF16)

    width = grads.shape[3] // 2
    near_half, far_half = pl.ds(0, width), pl.ds(width, width)

    def place(q, u):
        return q * UNITS + u

    def rows_place(owner_x, owner_y, q, u):
        return ((2 * owner_x + owner_y) * 4 + q) * OUT_AT + u

    def copy(src, dst, send, recv, device):
        return pltpu.make_async_remote_copy(
            src_ref=src, dst_ref=dst, send_sem=send, recv_sem=recv,
            device_id=device, device_id_type=MESH_ID,
        )

    def rs_copy(src, q, u, slot, device):
        return copy(src, inbox.at[slot, u], rs_send.at[q, u], rs_recv.at[slot, u], device)

    def rs_arrived(slot, u):
        rs_copy(inbox.at[slot, u], 0, u, slot, to_x).wait_recv()

    def up(u):
        for q in (3, 2, 1):
            @pl.when(z == 0)
            def _():
                rs_copy(grads.at[q, u], q, u, q, above).start()

            @pl.when((z > 0) & (z < q))
            def _():
                rs_arrived(q, u)
                add_unit(inbox.at[q, u], [inbox.at[q, u], grads.at[q, u]])
                rs_copy(inbox.at[q, u], q, u, q, above).start()

    def down(u):
        for q in (0, 1, 2):
            @pl.when(z == 3)
            def _():
                rs_copy(grads.at[q, u], q, u, 4 if q == 2 else q, below).start()

            for here_z in (1, 2):
                if here_z > q:
                    @pl.when(z == here_z)
                    def _():
                        rs_arrived(q, u)
                        add_unit(inbox.at[q, u], [inbox.at[q, u], grads.at[q, u]])
                        slot = 4 if here_z - 1 == q else q
                        rs_copy(inbox.at[q, u], q, u, slot, below).start()

    def ag_copy(src, q, u, way, device):
        return copy(src, out.at[place(q, u)], ag_send.at[way, q, u], ag_recv.at[q, u], device)

    def stay_copy(u):
        return pltpu.make_async_copy(final.at[u], out.at[place(z, u)], here.at[u])

    def x_copy(src, q, u, far):
        dst = rows_place(x, y, q, u) if far == 0 else rows_place(x, 1 - y, q, u)
        return copy(src, rows_out.at[dst], x_send.at[far, q, u], x_recv.at[far, q, u], to_x)

    def y_copy(src, q, u, owner_y):
        dst = rows_out.at[rows_place(x, owner_y, q, u)]
        return copy(src, dst, y_send.at[q, u], y_recv.at[q, u], to_y)

    def o_copy(src, q, k, half, way, device):
        dst = half * 4 * PARTS + q * PARTS + k
        return copy(src, out_out.at[dst], o_send.at[way, q, k], o_recv.at[half, q, k], device)

    def spread(src, q, u):
        @pl.when(u < OUT_AT)
        def _():
            y_copy(src.at[:, far_half], q, u, y).start()
            x_copy(src.at[:, near_half], q, u, 0).start()

        @pl.when((u >= OUT_AT) & (c == x))
        def _():
            o_copy(src, q, u - OUT_AT, c, 0, to_x).start()

        @pl.when((u >= OUT_AT) & (c != x))
        def _():
            o_copy(src, q, u - OUT_AT, c, 0, to_xc).start()
            o_copy(src, q, u - OUT_AT, c, 1, to_c).start()

    def finish(u):
        @pl.when(z == 0)
        def _():
            rs_arrived(4, u)
            add_unit(final.at[u], [grads.at[0, u], inbox.at[4, u]])

        for here_z in (1, 2):
            @pl.when(z == here_z)
            def _():
                rs_arrived(here_z, u)
                rs_arrived(4, u)
                add_unit(
                    final.at[u], [grads.at[here_z, u], inbox.at[here_z, u], inbox.at[4, u]]
                )

        @pl.when(z == 3)
        def _():
            rs_arrived(3, u)
            add_unit(final.at[u], [grads.at[3, u], inbox.at[3, u]])

        @pl.when(z < 3)
        def _():
            ag_copy(final.at[u], z, u, 0, above).start()

        @pl.when(z > 0)
        def _():
            ag_copy(final.at[u], z, u, 1, below).start()

        spread(final.at[u], z, u)
        stay_copy(u).start()

    def relay(u, far):
        for q in range(4):
            got = out.at[place(q, u)]

            @pl.when(z == q + far)
            def _():
                ag_copy(got, q, u, 0, to_x).wait_recv()

                @pl.when(z < 3)
                def _():
                    ag_copy(got, q, u, 0, above).start()

                spread(got, q, u)

            @pl.when(z == q - far)
            def _():
                ag_copy(got, q, u, 1, to_x).wait_recv()

                @pl.when(z > 0)
                def _():
                    ag_copy(got, q, u, 1, below).start()

                spread(got, q, u)

    def cross(u, far):
        for q in range(4):
            @pl.when((z == q + far) | (z == q - far))
            def _():
                got = rows_out.at[rows_place(x, 1 - y, q, u)]
                y_copy(got, q, u, 1 - y).wait_recv()
                x_copy(got, q, u, 1).start()

    def gain_copy(k, device):
        return copy(gain_in.at[0], gain_in.at[1 + k], g_send.at[k], g_recv.at[k], device)

    def gain_z(k, device):
        return copy(gain_in.at[0], gain_in.at[4 + z], g_send.at[3 + k], g_recv.at[3 + z], device)

    def gain_step(i):
        for k, device in enumerate((to_c, to_x, to_y)):
            @pl.when(i == k)
            def _():
                if k == 0:
                    gain_in[0] = gain[...]
                gain_copy(k, device).start()
                gain_copy(k, device).wait()
                gain_in[0] += gain_in[1 + k]

        @pl.when(i == 3)
        def _():
            for k, device in enumerate(others):
                gain_z(k, device).start()

        @pl.when(i == 5)
        def _():
            for k in range(4):
                @pl.when(z == k)
                def _():
                    gain_in[4 + k] = gain_in[0]

                @pl.when(z != k)
                def _():
                    copy(
                        gain_in.at[0], gain_in.at[4 + k], g_send.at[3], g_recv.at[3 + k], to_x
                    ).wait_recv()

            for k, device in enumerate(others):
                gain_z(k, device).wait_send()
            gain_out[...] = (gain_in[4] + gain_in[5]) + (gain_in[6] + gain_in[7])

    ready = [
        (far_part, far_all, far_x, 0),
        (down_part, down_all, down_x, 0),
    ]
    counts = [part.shape[0] // PIECE for part, _, _, _ in ready]

    def piece(ref, q, p):
        return ref.at[q, pl.ds(pl.multiple_of(p * PIECE, 16), PIECE)]

    def own_piece(kind, p):
        return ready[kind][0].at[pl.ds(pl.multiple_of(p * PIECE, 16), PIECE)]

    def ma_copy(kind, src, q, p, way, device):
        dst = piece(ready[kind][1], q, p)
        return copy(src, dst, ma_send.at[kind, way, q, p], ma_recv.at[kind, q, p], device)

    def mx_copy(kind, src, q, p):
        dst = piece(ready[kind][2], q, p)
        return copy(src, dst, mx_send.at[kind, q, p], mx_recv.at[kind, q, p], to_x)

    def my_copy(src, q, p):
        return copy(src, piece(far_y, q, p), my_send.at[q, p], my_recv.at[q, p], to_y)

    def m_stay(kind, p):
        return pltpu.make_async_copy(
            own_piece(kind, p), piece(ready[kind][1], z, p), m_here.at[kind, p]
        )

    def m_spread(kind, src, q, p):
        if kind == 0:
            my_copy(src, q, p).start()
        else:
            mx_copy(kind, src, q, p).start()

    def m_begin(kind, p):
        src = own_piece(kind, p)

        @pl.when(z < 3)
        def _():
            ma_copy(kind, src, z, p, 0, above).start()

        @pl.when(z > 0)
        def _():
            ma_copy(kind, src, z, p, 1, below).start()

        m_spread(kind, src, z, p)
        m_stay(kind, p).start()

    def m_relay(kind, p, hops):
        for q in range(4):
            got = piece(ready[kind][1], q, p)

            @pl.when(z == q + hops)
            def _():
                ma_copy(kind, got, q, p, 0, to_x).wait_recv()

                @pl.when(z < 3)
                def _():
                    ma_copy(kind, got, q, p, 0, above).start()

                m_spread(kind, got, q, p)

            @pl.when(z == q - hops)
            def _():
                ma_copy(kind, got, q, p, 1, to_x).wait_recv()

                @pl.when(z > 0)
                def _():
                    ma_copy(kind, got, q, p, 1, below).start()

                m_spread(kind, got, q, p)

    def m_cross(p, hops):
        for q in range(4):
            @pl.when((z == q + hops) | (z == q - hops))
            def _():
                got = piece(far_y, q, p)
                my_copy(got, q, p).wait_recv()
                mx_copy(0, got, q, p).start()

    def m_step(i):
        for kind, count in enumerate(counts):
            first = i - ready[kind][3]
            when_unit(first, count, partial(m_begin, kind))
            for hops in (1, 2, 3):
                when_unit(first - hops, count, lambda p: m_relay(kind, p, hops))
        for hops in (0, 1, 2, 3):
            when_unit(i - ready[0][3] - 1 - hops, counts[0], lambda p: m_cross(p, hops))

    def m_end():
        for kind, count in enumerate(counts):
            @pl.loop(0, count)
            def _(p):
                src = own_piece(kind, p)
                m_stay(kind, p).wait()
                for q in range(4):
                    @pl.when((z < 3) & (q <= z))
                    def _():
                        ma_copy(kind, src, q, p, 0, to_x).wait_send()

                    @pl.when((z > 0) & (q >= z))
                    def _():
                        ma_copy(kind, src, q, p, 1, to_x).wait_send()

                    mx_copy(kind, src, q, p).wait()
                    if kind == 0:
                        my_copy(src, q, p).wait_send()

    def when_unit(u, last, work):
        @pl.when((u >= 0) & (u < last))
        def _():
            work(u)

    @pl.loop(0, UNITS + 8)
    def _(i):
        when_unit(i - z, UNITS, up)
        when_unit(i - (3 - z), UNITS, down)
        gain_step(i)
        when_unit(i - 3, UNITS, finish)
        for far in (1, 2, 3):
            when_unit(i - 3 - far, UNITS, lambda u: relay(u, far))
        for far in (0, 1, 2, 3):
            when_unit(i - 4 - far, OUT_AT, lambda u: cross(u, far))
        m_step(i)

    m_end()

    @pl.loop(0, UNITS)
    def _(u):
        stay_copy(u).wait()
        for q in range(4):
            src = grads.at[q, u]

            @pl.when(z != q)
            def _():
                rs_copy(src, q, u, q, to_x).wait_send()

            @pl.when((z < 3) & (q <= z))
            def _():
                ag_copy(src, q, u, 0, to_x).wait_send()

            @pl.when((z > 0) & (q >= z))
            def _():
                ag_copy(src, q, u, 1, to_x).wait_send()

            @pl.when(u < OUT_AT)
            def _():
                half = rows_out.at[0]
                y_copy(half, q, u, y).wait_send()
                x_copy(half, q, u, 0).wait()
                x_copy(half, q, u, 1).wait()

            @pl.when(u >= OUT_AT)
            def _():
                k = u - OUT_AT
                o_copy(src, q, k, c, 0, to_x).wait_send()
                o_copy(src, q, k, 1 - c, 0, to_x).wait_recv()

                @pl.when(c != x)
                def _():
                    o_copy(src, q, k, c, 1, to_x).wait_send()
                    o_copy(src, q, k, c, 0, to_x).wait_recv()


def reduce_grads(grads, gain, far, down, ident):
    cols = grads.shape[3]
    shape = jax.ShapeDtypeStruct
    dma = pltpu.SemaphoreType.DMA
    return pl.pallas_call(
        reduce_kernel,
        out_shape=(
            shape((4 * UNITS, UNIT, cols), BF16),
            shape((16 * OUT_AT, UNIT, cols // 2), BF16),
            shape((8 * PARTS, UNIT, cols), BF16),
            shape(gain.shape, F32),
            shape((4,) + far.shape, BF16),
            shape((4,) + down.shape, BF16),
            shape((4,) + far.shape, BF16),
            shape((4,) + far.shape, BF16),
            shape((4,) + down.shape, BF16),
        ),
        in_specs=[IN_VMEM] * 4,
        out_specs=(ANY, ANY, ANY, IN_VMEM) + (ANY,) * 5,
        scratch_shapes=[
            pltpu.VMEM((5, UNITS, UNIT, cols), BF16),
            pltpu.VMEM((UNITS, UNIT, cols), BF16),
            pltpu.VMEM((8,) + gain.shape, F32),
            dma((4, UNITS)),
            dma((5, UNITS)),
            dma((2, 4, UNITS)),
            dma((4, UNITS)),
            dma((4, OUT_AT)),
            dma((4, OUT_AT)),
            dma((2, 4, OUT_AT)),
            dma((2, 4, OUT_AT)),
            dma((2, 4, PARTS)),
            dma((2, 4, PARTS)),
            dma((6,)),
            dma((7,)),
            dma((2, 2, 4, down.shape[0] // PIECE)),
            dma((2, 4, down.shape[0] // PIECE)),
            dma((2, 4, down.shape[0] // PIECE)),
            dma((2, 4, down.shape[0] // PIECE)),
            dma((4, far.shape[0] // PIECE)),
            dma((4, far.shape[0] // PIECE)),
            dma((2, down.shape[0] // PIECE)),
            dma((UNITS,)),
        ],
        compiler_params=pltpu.CompilerParams(
            collective_id=ident, has_side_effects=True, vmem_limit_bytes=VMEM_LIMIT
        ),
        cost_estimate=cost(300),
        name="reduce_grads",
    )(grads, gain, far, down)


def qkv_kernel(cols_h, flags, mine, *refs):
    sources, outs = refs[:4], refs[4:]
    here_x, here_y = flags[0], flags[1]
    rows, cols = outs[0].shape[0], mine.shape[-1]
    own = mine[...].reshape(rows, cols)
    full = [
        [
            jnp.where(
                (here_x == i) & (here_y == j), own, sources[2 * i + j][...].reshape(rows, cols)
            )
            for j in range(2)
        ]
        for i in range(2)
    ]
    for kind in range(3):
        first = kind * cols_h
        outs[kind][...] = jnp.concatenate(
            [full[i][j][:, first : first + cols_h] for j in range(2) for i in range(2)], 1
        ).astype(F32)


def ff_kernel(cols_f, flags, near, far, near_x, far_x, *outs):
    here_x, here_y, core = flags[0], flags[1], flags[2]
    by_x = [(near[...], far[...]), (near_x[...], far_x[...])]
    full = [
        [
            jnp.where(
                here_x == i,
                jnp.where(here_y == j, *by_x[0]),
                jnp.where(here_y == j, *by_x[1]),
            )
            for j in range(2)
        ]
        for i in range(2)
    ]
    for kind in range(2):
        pieces = []
        for j in range(2):
            for k in range(2):
                for i in range(2):
                    own = full[i][j][:, kind * cols_f : (kind + 1) * cols_f]
                    first = (2 + kind) * cols_f
                    side = full[i][j][:, first : first + cols_f]
                    pieces.append(jnp.where(core == k, own, side))
        outs[kind][...] = jnp.concatenate(pieces, 1).astype(F32)


def row_target(width):
    return pl.BlockSpec((48, width), lambda s: (s, 0))


def place_qkv(flags, mine, summed, rows_d, cols_h):
    cols = summed.shape[-1]

    def source(i, j):
        return pl.BlockSpec((PARTS, UNIT, cols), lambda s: ((2 * i + j) * 12 + s, 0, 0))

    own = pl.BlockSpec((PARTS, UNIT, cols), lambda s: (s + s // 3, 0, 0))
    return pl.pallas_call(
        partial(qkv_kernel, cols_h),
        grid=(rows_d // 48,),
        out_shape=(jax.ShapeDtypeStruct((rows_d, 4 * cols_h), F32),) * 3,
        in_specs=[pl.BlockSpec(memory_space=pltpu.SMEM), own]
        + [source(i, j) for i in range(2) for j in range(2)],
        out_specs=(row_target(4 * cols_h),) * 3,
        compiler_params=pltpu.CompilerParams(vmem_limit_bytes=VMEM_LIMIT),
        cost_estimate=cost(9),
        name="place_qkv",
    )(flags, mine, summed, summed, summed, summed)


def place_ff(flags, near, far, near_x, far_x, rows_d, cols_f):
    ff = row_target(4 * cols_f)
    return pl.pallas_call(
        partial(ff_kernel, cols_f),
        grid=(rows_d // 48,),
        out_shape=(jax.ShapeDtypeStruct((rows_d, 8 * cols_f), F32),) * 2,
        in_specs=[pl.BlockSpec(memory_space=pltpu.SMEM)] + [ff] * 4,
        out_specs=(row_target(8 * cols_f),) * 2,
        compiler_params=pltpu.CompilerParams(vmem_limit_bytes=VMEM_LIMIT),
        cost_estimate=cost(16),
        name="place_ff",
    )(flags, near, far, near_x, far_x)


def down_kernel(per_x, flags, own, side, out):
    mine = flags[0] == pl.program_id(0) // per_x
    out[...] = jnp.where(mine, own[...].astype(F32), side[...].astype(F32))


def place_down(flags, own, side, rows):
    cols = own.shape[1]
    per_x = rows // 144
    source = pl.BlockSpec((144, cols), lambda s: (s % per_x, 0))
    return pl.pallas_call(
        partial(down_kernel, per_x),
        grid=(2 * per_x,),
        out_shape=jax.ShapeDtypeStruct((2 * rows, cols), F32),
        in_specs=[pl.BlockSpec(memory_space=pltpu.SMEM), source, source],
        out_specs=pl.BlockSpec((144, cols), lambda s: (s, 0)),
        compiler_params=pltpu.CompilerParams(vmem_limit_bytes=VMEM_LIMIT),
        cost_estimate=cost(8),
        name="place_down",
    )(flags, own, side)


def lanes(rows):
    return lax.broadcasted_iota(jnp.int32, (rows, LANES), 1)


def rotated(block, cosine, sine_signed):
    lane = lanes(block.shape[0])
    turned = jnp.where(
        lane % HEAD_DIM < HEAD_DIM // 2,
        pltpu.roll(block, LANES - HEAD_DIM // 2, 1),
        pltpu.roll(block, HEAD_DIM // 2, 1),
    )
    return block * cosine + turned * sine_signed


def key_spans(pieces, rows):
    reach = WINDOW // rows
    return [
        (max(0, 2 * j - reach) * rows, (2 * j + 2) * rows) for j in range(pieces // 2)
    ]


def seen(first_ref, place_ref, rows, low, high):
    keys = low + lax.broadcasted_iota(jnp.int32, (1, high - low), 1)
    return (keys >= first_ref[rows, :]) & (keys <= place_ref[rows, :])


def forward_kernel(
    spans, width, q_raw, k_raw, v_ref, cos_q, sin_q, cos_k, sin_k, first, place,
    q_out, k_out, ctx_out, lse_out, v_keep,
):
    valid = width - pl.program_id(0) * LANES
    k_rows = k_raw.shape[0]
    keep = lanes(k_rows) < valid
    k_out[...] = jnp.where(keep, rotated(k_raw[...], cos_k[...], sin_k[...]), 0.0).astype(BF16)
    v_keep[...] = jnp.where(keep, v_ref[...], jnp.zeros((), BF16))
    keep_q = lanes(q_raw.shape[0]) < valid
    q_out[...] = jnp.where(keep_q, rotated(q_raw[...], cos_q[...], sin_q[...]), 0.0).astype(BF16)
    rows_j = q_raw.shape[0] // len(spans)
    left = lanes(rows_j) < HEAD_DIM
    zero = jnp.zeros((), BF16)
    for j, (low, high) in enumerate(spans):
        rows = pl.ds(j * rows_j, rows_j)
        visible = seen(first, place, rows, low, high)
        query = q_out[rows, :]
        halves = []
        for side in range(2):
            mine = jnp.where(left if side == 0 else ~left, query, zero)
            scores = lax.dot_general(
                mine, k_out[low:high, :], (((1,), (1,)), ((), ())), preferred_element_type=F32
            )
            scores = jnp.where(visible, scores * 0.125, NEGATIVE)
            top = jnp.max(scores, -1, keepdims=True)
            grown = jnp.exp(scores - top)
            total = jnp.sum(grown, -1, keepdims=True)
            probs = (grown * (1.0 / total)).astype(BF16)
            ctx = jnp.dot(probs, v_keep[low:high, :], preferred_element_type=F32)
            halves.append((ctx, top + jnp.log(total)))
        ctx_out[rows, :] = jnp.where(left, halves[0][0], halves[1][0]).astype(BF16)
        lse_out[rows, :] = jnp.where(left, halves[0][1], halves[1][1])


def lane_block(rows):
    return pl.BlockSpec((rows, LANES), lambda p: (0, p))


def whole(rows, cols):
    return pl.BlockSpec((rows, cols), lambda p: (0, 0))


def attend_forward(q_raw, k_raw, value, tables, limits, pieces):
    q_rows, width = q_raw.shape
    k_rows = k_raw.shape[0]
    spans = key_spans(pieces, k_rows // pieces)
    steps = -(-width // LANES)
    shape = jax.ShapeDtypeStruct
    return pl.pallas_call(
        partial(forward_kernel, spans, width),
        grid=(steps,),
        out_shape=(
            shape((q_rows, width), BF16),
            shape((k_rows, width), BF16),
            shape((q_rows, width), BF16),
            shape((q_rows, width), F32),
        ),
        in_specs=[
            lane_block(q_rows),
            lane_block(k_rows),
            lane_block(k_rows),
            whole(q_rows, LANES),
            whole(q_rows, LANES),
            whole(k_rows, LANES),
            whole(k_rows, LANES),
            whole(q_rows, 1),
            whole(q_rows, 1),
        ],
        out_specs=(
            lane_block(q_rows),
            lane_block(k_rows),
            lane_block(q_rows),
            lane_block(q_rows),
        ),
        scratch_shapes=[pltpu.VMEM((k_rows, LANES), BF16)],
        compiler_params=pltpu.CompilerParams(vmem_limit_bytes=VMEM_LIMIT),
        cost_estimate=cost(43),
        name="attend_forward",
    )(q_raw, k_raw, value, *tables, *limits)


def backward_kernel(
    spans, width, q_ref, k_ref, v_ref, g_ref, lse, cos_q, sin_q, cos_k, sin_k, first, place,
    part, dq_out, dk_done, dv_done, rows_out,
    k_keep, v_keep, dk_out, dv_out, give, got, send, recv, *scatter,
):
    step = pl.program_id(0)
    c = lax.axis_index("c")
    rows_j = q_ref.shape[0] // len(spans)
    pair = [("dk", dk_out, dk_done), ("dv", dv_out, dv_done)]

    def to_side(at):
        return pltpu.make_async_remote_copy(
            src_ref=give.at[at],
            dst_ref=got.at[at],
            send_sem=send.at[at],
            recv_sem=recv.at[at],
            device_id={"c": 1 - c},
            device_id_type=MESH_ID,
        )

    stages = scatter_stages(2, part, rows_out, *scatter[:-2], scatter[-2:])
    x, y = lax.axis_index("x"), lax.axis_index("y")

    @pl.when(step == 0)
    def _():
        meet([{"x": 1 - x}, {"y": 1 - y}, {"c": 1 - c}])

    last = pl.num_programs(0) - 1
    for at, stage in zip((0, 1, last - 2, last), stages):
        pl.when(step == at)(stage)

    @pl.when(step > 0)
    def _():
        to_side(step - 1).wait_recv()
        for k, (_, whole_sum, done) in enumerate(pair):
            for j in range(len(spans)):
                rows = pl.ds(j * rows_j, rows_j)
                own = whole_sum[pl.ds(pl.multiple_of((2 * j + c) * rows_j, rows_j), rows_j), :]
                done[rows, :] = (own + got[step - 1, k, rows, :].astype(F32)).astype(BF16)

    @pl.when(step < pl.num_programs(0) - 1)
    def _():
        backward_step(
            spans, width, q_ref, k_ref, v_ref, g_ref, lse, cos_q, sin_q, cos_k, sin_k,
            first, place, dq_out, dk_out, dv_out, k_keep, v_keep,
        )
        for k, (_, whole_sum, _) in enumerate(pair):
            for j in range(len(spans)):
                other = pl.ds(pl.multiple_of((2 * j + 1 - c) * rows_j, rows_j), rows_j)
                give[step, k, pl.ds(j * rows_j, rows_j), :] = whole_sum[other, :].astype(BF16)
        to_side(step).start()

    @pl.when(step == pl.num_programs(0) - 1)
    def _():
        for k in range(give.shape[0]):
            to_side(k).wait_send()


def backward_step(
    spans, width, q_ref, k_ref, v_ref, g_ref, lse, cos_q, sin_q, cos_k, sin_k, first, place,
    dq_out, dk_out, dv_out, k_keep, v_keep,
):
    valid = width - pl.program_id(0) * LANES
    zero = jnp.zeros((), BF16)
    keep = lanes(k_ref.shape[0]) < valid
    k_keep[...] = jnp.where(keep, k_ref[...], zero)
    v_keep[...] = jnp.where(keep, v_ref[...], zero)
    dk_out[...] = jnp.zeros_like(dk_out)
    dv_out[...] = jnp.zeros_like(dv_out)
    rows_j = q_ref.shape[0] // len(spans)
    lane = lanes(rows_j)
    left = (lane < HEAD_DIM) & (lane < valid)
    right = (lane >= HEAD_DIM) & (lane < valid)
    for j, (low, high) in enumerate(spans):
        rows = pl.ds(j * rows_j, rows_j)
        visible = seen(first, place, rows, low, high)
        query, grad = q_ref[rows, :], g_ref[rows, :]
        stats = lse[rows, :]
        halves = []
        for side in range(2):
            mask = left if side == 0 else right
            mine = jnp.where(mask, query, zero)
            grad_mine = jnp.where(mask, grad, zero)
            nt = (((1,), (1,)), ((), ()))
            tn = (((0,), (0,)), ((), ()))
            scores = lax.dot_general(mine, k_keep[low:high, :], nt, preferred_element_type=F32)
            column = side * HEAD_DIM
            log_total = stats[:, column : column + 1]
            probs = jnp.where(visible, jnp.exp(scores * 0.125 - log_total), 0.0)
            grad_probs = lax.dot_general(
                grad_mine, v_keep[low:high, :], nt, preferred_element_type=F32
            )
            mixed = probs * grad_probs
            delta = jnp.sum(mixed, -1, keepdims=True)
            grad_scores = (mixed - probs * delta).astype(BF16)
            halves.append(
                jnp.dot(grad_scores, k_keep[low:high, :], preferred_element_type=F32) * 0.125
            )
            dk_out[low:high, :] += (
                lax.dot_general(grad_scores, mine, tn, preferred_element_type=F32) * 0.125
            )
            dv_out[low:high, :] += lax.dot_general(
                probs.astype(BF16), grad_mine, tn, preferred_element_type=F32
            )
        grad_query = jnp.where(lane < HEAD_DIM, halves[0], halves[1])
        dq_out[rows, :] = rotated(grad_query, cos_q[rows, :], -sin_q[rows, :]).astype(BF16)
    dk_out[...] = rotated(dk_out[...], cos_k[...], -sin_k[...])


def attend_backward(query, key, value, grad, lse, tables, limits, partial_rows, pieces, ident):
    q_rows, width = query.shape
    k_rows = key.shape[0]
    spans = key_spans(pieces, k_rows // pieces)
    rows, cols = partial_rows.shape[0] // 8, partial_rows.shape[1]
    steps = -(-width // LANES)
    shape = jax.ShapeDtypeStruct

    def this(rows):
        return pl.BlockSpec((rows, LANES), lambda p: (0, jnp.minimum(p, steps - 1)))

    def last(rows):
        return pl.BlockSpec((rows, LANES), lambda p: (0, jnp.maximum(p - 1, 0)))

    return pl.pallas_call(
        partial(backward_kernel, spans, width),
        grid=(steps + 1,),
        out_shape=(shape((q_rows, width), BF16),) * 3 + (shape((rows, cols), F32),),
        in_specs=[
            this(q_rows),
            this(k_rows),
            this(k_rows),
            this(q_rows),
            this(q_rows),
            whole(q_rows, LANES),
            whole(q_rows, LANES),
            whole(k_rows, LANES),
            whole(k_rows, LANES),
            whole(q_rows, 1),
            whole(q_rows, 1),
            IN_VMEM,
        ],
        out_specs=(this(q_rows), last(q_rows), last(q_rows), IN_VMEM),
        scratch_shapes=[pltpu.VMEM((k_rows, LANES), BF16)] * 2
        + [pltpu.VMEM((k_rows, LANES), F32)] * 2
        + [pltpu.VMEM((steps, 2, q_rows, LANES), BF16)] * 2
        + [pltpu.SemaphoreType.DMA((steps,))] * 2
        + scatter_scratch(2, rows, cols),
        compiler_params=pltpu.CompilerParams(
            collective_id=ident, has_side_effects=True, vmem_limit_bytes=VMEM_LIMIT
        ),
        cost_estimate=cost(57),
        name="attend_backward",
    )(
        query, key, value, grad, lse, *tables, *limits,
        partial_rows.reshape(4, 2, rows, cols),
    )


def norm_back(grad_normed, unit_rows, rms_rows, gain_rows):
    scaled = grad_normed * gain_rows
    return rms_rows * (scaled - unit_rows * jnp.mean(scaled * unit_rows, -1, keepdims=True))


def on_device(
    tokens,
    doc_lengths,
    cotangent,
    attn_gain,
    w_query,
    w_key,
    w_value,
    w_out,
    mlp_gain,
    w_gate,
    w_up,
    w_down,
):
    outer = lax.axis_size("g")
    pieces_z = lax.axis_size("z")
    x, y, c = (lax.axis_index(a) for a in PLANE)
    own = 2 * y + c

    turn_pairs = [
        (i * pieces_z + z, z * pieces_z + i) for i in range(pieces_z) for z in range(pieces_z)
    ]

    def turned(block):
        return lax.ppermute(block, ("y", "c", "z"), turn_pairs)

    def joined(shard):
        if outer == 1:
            return shard
        return lax.all_gather(shard, "g", axis=0, tiled=True)

    w_query, w_key, w_value, w_out = map(joined, (w_query, w_key, w_value, w_out))
    w_gate, w_up, w_down = map(joined, (w_gate, w_up, w_down))
    rows_d = w_query.shape[0]
    model = w_query.shape[1]
    tok_rows = tokens.shape[1]
    pieces = 2 * pieces_z
    seq_len = pieces * tok_rows
    cols_h = model // 4
    cols_f = w_gate.shape[1] // 8

    def head_cols(weight, group):
        return lax.dynamic_slice_in_dim(weight, group * cols_h, cols_h, 1)

    def qkv_cols(group):
        return jnp.concatenate([head_cols(w, group) for w in (w_query, w_key, w_value)], 1)

    def spread(gain):
        padded = jnp.zeros((model,), F32)
        return lax.dynamic_update_slice_in_dim(padded, joined(gain).astype(F32), own * rows_d, 0)

    gains = jnp.pad(jnp.stack([spread(attn_gain), spread(mlp_gain)]), ((0, 6), (0, 0)))
    normed_one, tok_low, gains, w_qkv, out_side, *tables, first_query = front(
        tokens[0],
        doc_lengths,
        gains,
        qkv_cols(2 * y + x),
        qkv_cols(2 * (1 - y) + x),
        w_out,
        seq_len,
        1,
    )
    cot_late, _ = lax.optimization_barrier((cotangent[0], tok_low))
    cot_low = turned(cot_late)
    inputs, upstream = tok_low.astype(F32), cot_low.astype(F32)
    gain_one, gain_two = gains[0:1], gains[1:2]
    w_qkv = w_qkv.reshape(4 * rows_d, 3 * cols_h)
    w_out_use = jnp.where(c == x, w_out, out_side)

    gate_late, up_late, normed_one = lax.optimization_barrier((w_gate, w_up, normed_one))

    def ff_cols(dest):
        first = (2 * dest + x) * cols_f
        return jnp.concatenate(
            [lax.dynamic_slice_in_dim(w, first, cols_f, 1) for w in (gate_late, up_late)], 1
        )

    ff_own = ff_cols(own)
    ff_c = swap(ff_cols(2 * y + 1 - c), "c")
    ff_y = swap(ff_cols(2 * (1 - y) + c), "y")
    ff_yc = lax.ppermute(
        ff_cols(2 * (1 - y) + 1 - c), ("y", "c"), [(i, 3 - i) for i in range(4)]
    )

    def ordered(a, b, flag):
        return jnp.where(flag == 0, jnp.stack([a, b]), jnp.stack([b, a]))

    down_use = lax.dynamic_slice_in_dim(w_down, x * cols_f, cols_f, 0)

    def own_rows(array):
        cols = array.shape[1:]
        split = array.reshape((pieces // 2, 2, tok_rows) + cols)
        return lax.dynamic_index_in_dim(split, c, 1, keepdims=False).reshape(
            (seq_len // 2,) + cols
        )

    place = own_rows(jnp.arange(seq_len, dtype=jnp.int32))
    limits = (first_query, place[:, None])

    rms_one = lax.rsqrt(jnp.mean(inputs * inputs, -1, keepdims=True) + EPSILON)
    unit_one = inputs * rms_one

    query_raw = dot(own_rows(normed_one), w_qkv[:, :cols_h])
    key_raw = dot(normed_one, w_qkv[:, cols_h : 2 * cols_h])
    value = dot(normed_one, w_qkv[:, 2 * cols_h :]).astype(BF16)
    query, key, context, lse = attend_forward(query_raw, key_raw, value, tables, limits, pieces)

    attn_out = scatter_rows(dot(context, w_out_use), 1, 2)
    hidden_res = inputs + BETA * attn_out
    rms_two = lax.rsqrt(jnp.mean(hidden_res * hidden_res, -1, keepdims=True) + EPSILON)
    unit_two = hidden_res * rms_two
    normed_rows = (unit_two * gain_two).astype(BF16)
    normed_rows, ff_c, ff_y, ff_yc = lax.optimization_barrier((normed_rows, ff_c, ff_y, ff_yc))
    normed_two = gather_rows(normed_rows, 2, 3)
    cot_rows = lax.optimization_barrier(((BETA * upstream).astype(BF16), normed_two))[0]
    grad_mlp = lax.all_gather(cot_rows, PLANE, axis=0, tiled=True)
    ff_near = ordered(ff_own, ff_c, c)
    ff_far = ordered(ff_y, ff_yc, c)
    w_ff = ordered(ff_near, ff_far, y).reshape(4 * rows_d, 2 * cols_f)

    gate_up = dot(normed_two, w_ff)
    gate, up = gate_up[:, :cols_f], gate_up[:, cols_f:]
    sigmoid_gate = jax.nn.sigmoid(gate)
    silu_gate = gate * sigmoid_gate
    activation = (silu_gate * up).astype(BF16)
    mlp_part = dot(activation, down_use).astype(BF16)
    mlp_part, grad_mlp = lax.optimization_barrier((mlp_part, grad_mlp))

    grad_activation = dot_nt(grad_mlp, down_use)
    grad_up = (grad_activation * silu_gate).astype(BF16)
    grad_gate = (
        grad_activation * up * (sigmoid_gate * (1.0 + gate * (1.0 - sigmoid_gate)))
    ).astype(BF16)
    grad_ff = jnp.concatenate([grad_gate, grad_up], 1)
    padded = jnp.pad(activation, ((0, 0), (0, 768 - cols_f)))
    grad_ff_side = swap(grad_ff, "c")

    def row_block(normed, y_of):
        return lax.dynamic_slice_in_dim(normed, (2 * y_of + c) * rows_d, rows_d, 1)

    def ff_rows(y_of):
        block = row_block(normed_two, y_of)
        return jnp.concatenate(
            [dot_tn(block, grad_ff).astype(BF16), dot_tn(block, grad_ff_side).astype(BF16)], 1
        )

    grad_down = dot_tn(padded, grad_mlp).astype(BF16)
    ff_near, ff_far = ff_rows(y), ff_rows(1 - y)
    back_part = dot_nt(grad_ff, w_ff).astype(BF16)
    back_part, grad_down, ff_near, ff_far = lax.optimization_barrier(
        (back_part, grad_down, ff_near, ff_far)
    )

    def sum_z(grad):
        return lax.psum_scatter(grad, "z", scatter_dimension=0, tiled=True)

    ff_far, ff_near, grad_down = sum_z(ff_far), sum_z(ff_near), sum_z(grad_down)
    grad_normed_two = scatter_rows(back_part, 2, 4)

    gain_grad_two = jnp.sum(grad_normed_two * unit_two, 0)
    grad_hidden = upstream + norm_back(grad_normed_two, unit_two, rms_two, gain_two)
    grad_attn = gather_rows((BETA * grad_hidden).astype(BF16), 1, 5)
    grad_context = dot_nt(grad_attn, w_out_use).astype(BF16)

    grad_out_part = dot_tn(context, grad_attn).astype(BF16)
    half = model // 2
    keep = lax.dynamic_slice_in_dim(grad_out_part, c * half, half, 1)
    give = lax.dynamic_slice_in_dim(grad_out_part, (1 - c) * half, half, 1)
    grad_out_half = (keep.astype(F32) + swap(give, "c").astype(F32)).astype(BF16)

    grad_context, ff_near = lax.optimization_barrier((grad_context, ff_near))
    ff_near = lax.all_gather(ff_near, "z", axis=0, tiled=True)
    grad_query, grad_key, grad_value, mlp_out = attend_backward(
        query, key, value, grad_context, lse, tables, limits, mlp_part, pieces, 8
    )
    grad_qkv = jnp.concatenate([grad_query, grad_key, grad_value], 1)

    query_part = dot_nt(grad_qkv, w_qkv).astype(BF16)
    grad_normed_one = scatter_rows(query_part, 1, 6)
    grad_qkv_side = swap(grad_qkv, "c")
    grad_qkv_all = (
        jnp.where(
            c == 0,
            jnp.stack([grad_qkv, grad_qkv_side]),
            jnp.stack([grad_qkv_side, grad_qkv]),
        )
        .reshape(2, pieces // 2, tok_rows, 3 * cols_h)
        .transpose(1, 0, 2, 3)
        .reshape(seq_len, 3 * cols_h)
    )
    third = rows_d // 12
    width = -(-3 * cols_h // LANES) * LANES

    def qkv_rows(y_of):
        part = dot_tn(row_block(normed_one, y_of), grad_qkv_all).astype(BF16)
        return jnp.pad(part, ((0, 0), (0, width - 3 * cols_h)))

    grads = jnp.concatenate(
        [
            jnp.concatenate([qkv_rows(y), qkv_rows(1 - y)], 1).reshape(
                4, OUT_AT, UNIT, 2 * width
            ),
            jnp.pad(
                jnp.concatenate(jnp.split(grad_out_half, 3, 0), 1),
                ((0, 0), (0, 2 * width - 3 * half)),
            ).reshape(4, PARTS, UNIT, 2 * width),
        ],
        1,
    )
    gain_grad_one = jnp.sum(grad_normed_one * unit_one, 0)
    gain_part = jnp.pad(jnp.stack([gain_grad_one, gain_grad_two]), ((0, 6), (0, 0)))
    grads, ff_near = lax.optimization_barrier((grads, ff_near))
    near_x = swap(ff_near, "x")
    mine, summed, out_got, gain_grads, _, *ff_sums = reduce_grads(
        grads, gain_part, ff_far, grad_down, 7
    )
    down_own, far_y, far_x, down_side = (
        part.reshape(-1, part.shape[-1]) for part in ff_sums
    )
    grad_inputs = grad_hidden + norm_back(grad_normed_one, unit_one, rms_one, gain_one)

    def later(array):
        return lax.optimization_barrier((array, gain_grads))[0]

    grad_tokens = turned(later(grad_inputs.astype(BF16)))[None]
    output = turned(later((hidden_res + BETA * mlp_out).astype(BF16)))[None]
    if outer > 1:
        gain_grads = lax.psum(gain_grads, "g")


    shard = attn_gain.shape[0]
    first = own * rows_d + lax.axis_index("g") * shard
    gain_grads = lax.dynamic_slice_in_dim(gain_grads, first, shard, 1)

    def finish(grad):
        if outer > 1:
            grad = lax.psum_scatter(grad.astype(BF16), "g", scatter_dimension=0, tiled=True)
        return grad.astype(F32)

    flags = jnp.stack([x, y, c]).astype(jnp.int32)
    qkv_all = place_qkv(flags, mine, summed, rows_d, cols_h)
    gate_all, up_all = place_ff(flags, ff_near, far_y, near_x, far_x, rows_d, cols_f)
    ff_all = (gate_all, up_all)
    down_all = place_down(flags, down_own, down_side, cols_f)
    out_mine = mine.reshape(4, UNITS, UNIT, 2 * width)[:, OUT_AT:, :, : 3 * half]
    out_mine = out_mine.reshape(4 * third, 3 * half)
    out_got = out_got[:, :, : 3 * half].reshape(2, 4 * third, 3 * half)
    out_halves = [
        jnp.concatenate(
            jnp.split(jnp.where((c == x) & (c == h), out_mine, out_got[h]), 3, 1), 0
        )
        for h in range(2)
    ]
    out_all = jnp.concatenate(out_halves, 1)

    return (
        output,
        grad_tokens,
        gain_grads[0],
        finish(qkv_all[0]),
        finish(qkv_all[1]),
        finish(qkv_all[2]),
        finish(out_all),
        gain_grads[1],
        finish(ff_all[0]),
        finish(ff_all[1]),
        finish(down_all),
    )


def solution(mesh):
    seq, fsdp, rep = (mesh.shape[a] for a in ("seq", "fsdp", "rep"))
    inner = Mesh(
        mesh.devices.reshape(seq, rep // 2, 2, fsdp // rep, rep), ("x", "y", "c", "g", "z")
    )
    owners = ("y", "c", "g")
    token_spec = P(owners, ("x", "z"), None)
    placed = (token_spec, P(owners, None), token_spec, P(owners)) + (P(owners, None),) * 4
    placed = placed + (P(owners),) + (P(owners, None),) * 3
    return jax.shard_map(
        on_device,
        mesh=inner,
        in_specs=placed,
        out_specs=(token_spec, token_spec, P(owners))
        + (P(owners, None),) * 4
        + (P(owners),)
        + (P(owners, None),) * 3,
        check_vma=False,
    )
```
